128 devices in a mesh: rep: 4 (over y), shard: 32 (over z, x, core).
Axes of the slice: x: 4, y: 4, z: 4, core: 2. Of those that a mesh axis runs over, the one named last changes fastest.
Arguments:
- layer_input: bfloat16 [8, 2048, 1024], P('rep', 'shard'), may hold values from -6 to 6
- first_layer_values: bfloat16 [8, 2048, 1024], P('rep', 'shard'), may hold values from -6 to 6
- segments: int32 [8, 2048], P('rep', 'shard'), may hold values from 0 to 10, as said below
- receptance_key_value_weight: bfloat16 [1024, 3072], P('shard'), may hold values from -0.1875 to 0.1875
- time_output_weight: bfloat16 [1024, 1024], P('shard'), may hold values from -0.375 to 0.375
- low_rank_down: bfloat16 [1024, 320], P('shard'), may hold values from -0.1875 to 0.1875
- low_rank_up: bfloat16 [320, 1024], P(None, 'shard'), may hold values from -0.75 to 0.75
- channel_key_weight: bfloat16 [1024, 4096], P('shard'), may hold values from -0.1875 to 0.1875
- channel_value_weight: bfloat16 [4096, 1024], P('shard'), may hold values from -0.09375 to 0.09375
- vectors: bfloat16 [19, 1024], P(None, 'shard'), may hold values from -12 to 1.5
- output_gradient: bfloat16 [8, 2048, 1024], P('rep', 'shard'), may hold values from -6 to 6
Outputs:
- hidden_out: bfloat16 [8, 2048, 1024], P('rep', 'shard')
- hidden_grad: float32 [8, 2048, 1024], P('rep', 'shard')
- first_values_grad: float32 [8, 2048, 1024], P('rep', 'shard')
- w_rkv_grad: float32 [1024, 3072], P('shard')
- w_out_grad: float32 [1024, 1024], P('shard')
- lora_down_grad: float32 [1024, 320], P('shard')
- lora_up_grad: float32 [320, 1024], P(None, 'shard')
- w_key_grad: float32 [1024, 4096], P('shard')
- w_val_grad: float32 [4096, 1024], P('shard')
- vectors_grad: float32 [19, 1024], P(None, 'shard')
The draws below stay inside these ranges and needn't reach their ends.
Inputs may be any that keep to these rules, and one draw needn't show every extreme that they name: `segments`: within a sequence segment numbers start at 0, never fall and rise by one at each document's first token; every document has 200 to 2000 tokens except a sequence's last, which the sequence's end may cut. In each group of 2 consecutive sequences one, which varies with the seed, is a single document. Some sequence, which varies with the seed, packs documents of exactly 200 tokens each, so that the most is reached.
All inputs are finite; a program needn't handle non-finite values.
Results may differ from the reference program's by a relative error of at most 0.023.
Values may be sent and summed in bfloat16 or wider, within the bound.
No kernel may reach another device: no remote copies, remote signals or barrier semaphores. Data moves between devices by JAX's collectives and lax.ppermute only.
A program may use at most 448 MiB of HBM per device.

```python
import jax
import jax.numpy as jnp
from jax import lax

EMBED_SIZE = 1024
H = 16
HS = 64
FF = 4096
DECAY_RANK = 64
LA = 64
LV = 32
BLK = 16
MICRO = 2
DOC_MIN = 200
DOC_MAX = 2000
LOW_RANK_TOTAL = 320
STEPS_PER_TEXT = 2048
SEQS = 8


def draw_segments(key, part):
    key = jax.random.fold_in(key, 11)
    keys = jax.random.split(key, 3)
    count = STEPS_PER_TEXT // DOC_MIN + 1
    lengths = jax.random.randint(keys[0], (SEQS, count), DOC_MIN, DOC_MAX + 1)
    whole = jax.random.randint(keys[1], (SEQS // MICRO,), 0, MICRO)
    group = jax.random.randint(keys[2], (), 0, SEQS // MICRO)
    packed_row = group * MICRO + (whole[group] + 1) % MICRO
    rows = jnp.arange(SEQS, dtype=jnp.int32)
    lengths = jnp.where((rows == packed_row)[:, None], DOC_MIN, lengths)
    ends = jnp.cumsum(lengths, axis=1)
    position = jnp.arange(STEPS_PER_TEXT, dtype=jnp.int32)
    numbered = jnp.sum((ends[:, None, :] <= position[None, :, None]).astype(jnp.int32), axis=2)
    single = rows % MICRO == jnp.repeat(whole, MICRO)
    return jnp.where(single[:, None], 0, numbered).astype(jnp.int32)


def draw_vectors(key, part):
    key = jax.random.fold_in(key, 7)
    keys = jax.random.split(key, 6)
    slowness = jax.random.uniform(keys[0], (EMBED_SIZE // HS,))
    gain_spread = 0.2
    per_channel = jnp.repeat(slowness, HS)
    jitter = jax.random.uniform(keys[1], (2, EMBED_SIZE), minval=-0.5, maxval=0.5)
    multiplier_arrays = 1.0 + gain_spread * jax.random.uniform(keys[2], (3, EMBED_SIZE), minval=-1.0, maxval=1.0)
    additive_terms = jax.random.uniform(keys[3], (3, EMBED_SIZE), minval=-0.5, maxval=0.5)
    neighbor_interpolants = jax.random.uniform(keys[4], (7, EMBED_SIZE), minval=0.05, maxval=0.95)
    auxiliary_results = jax.random.uniform(keys[5], (4, EMBED_SIZE))
    forgetting_shift_base = -3.5 - 8.0 * per_channel + jitter[0]
    speed_baseline = -2.0 - 5.0 * per_channel + jitter[1]
    skip_connection_baseline = 2.0 * auxiliary_results[0] - 1.0
    cluster_standardize_factor = 0.5 + 0.7 * auxiliary_results[1]
    speed_mixture = 0.5 + auxiliary_results[2]
    present_reward_factor = 2.0 * auxiliary_results[3] - 1.0
    position_entries = [multiplier_arrays[0], additive_terms[0], neighbor_interpolants[0], neighbor_interpolants[1], neighbor_interpolants[2], neighbor_interpolants[3], neighbor_interpolants[4], neighbor_interpolants[5], forgetting_shift_base, speed_baseline, skip_connection_baseline, cluster_standardize_factor, speed_mixture, present_reward_factor, multiplier_arrays[1], additive_terms[1], multiplier_arrays[2], additive_terms[2], neighbor_interpolants[6]]
    return jnp.stack(position_entries).astype(jnp.bfloat16)


def levels(rng, dims, shards, smallest, high):
    def one(dim, blocks):
        draws = jax.random.uniform(jax.random.fold_in(jax.random.fold_in(rng, 6), dim), (blocks,), jnp.float32, smallest / len(shards), high / len(shards))
        return jnp.repeat(jnp.exp(draws), dims[dim] // blocks).reshape((-1,) + (1,) * (len(dims) - dim - 1))

    factor_of = one(*shards[0])
    for cut in shards[1:]:
        factor_of = factor_of * one(*cut)
    return factor_of


def scatter_about(stream_key, extent, scale, limit, pieces=(), held_as=jnp.bfloat16):
    factor_of = levels(stream_key, extent, pieces, -0.22, 0.18) if pieces else 1.0
    array = jax.random.normal(stream_key, extent, jnp.float32) * scale * factor_of
    return jnp.minimum(jnp.maximum(array, -limit), limit).astype(held_as)


def setup_inputs(seed: int = 0) -> dict:
    streams_of = jax.random.split(jax.random.key(seed), 12)
    layer_input = scatter_about(streams_of[0], (SEQS, STEPS_PER_TEXT, EMBED_SIZE), 1.0, 6.0, ((0, 4), (1, 32)))
    first_layer_values = scatter_about(streams_of[1], (SEQS, STEPS_PER_TEXT, EMBED_SIZE), 1.0, 6.0, ((0, 4), (1, 32)))
    segments = draw_segments(jax.random.fold_in(streams_of[11], 71), 0)
    receptance_key_value_weight = scatter_about(streams_of[3], (EMBED_SIZE, 3 * EMBED_SIZE), EMBED_SIZE ** -0.5, 0.1875, ((0, 32),))
    time_output_weight = scatter_about(streams_of[4], (EMBED_SIZE, EMBED_SIZE), (EMBED_SIZE // 4) ** -0.5, 0.375, ((0, 32),))
    low_rank_down = scatter_about(streams_of[5], (EMBED_SIZE, LOW_RANK_TOTAL), EMBED_SIZE ** -0.5, 0.1875, ((0, 32),))
    low_rank_up = scatter_about(streams_of[6], (LOW_RANK_TOTAL, EMBED_SIZE), DECAY_RANK ** -0.5, 0.75, ((1, 32),))
    channel_key_weight = scatter_about(streams_of[7], (EMBED_SIZE, FF), EMBED_SIZE ** -0.5, 0.1875, ((0, 32),))
    channel_value_weight = scatter_about(streams_of[8], (FF, EMBED_SIZE), FF ** -0.5, 0.09375, ((0, 32),))
    vectors = draw_vectors(jax.random.fold_in(streams_of[11], 71), 0)
    output_gradient = scatter_about(streams_of[10], (SEQS, STEPS_PER_TEXT, EMBED_SIZE), 1.0, 6.0, ((0, 4), (1, 32)))
    return dict(layer_input=layer_input, first_layer_values=first_layer_values, segments=segments, receptance_key_value_weight=receptance_key_value_weight, time_output_weight=time_output_weight, low_rank_down=low_rank_down, low_rank_up=low_rank_up, channel_key_weight=channel_key_weight, channel_value_weight=channel_value_weight, vectors=vectors, output_gradient=output_gradient)


@jax.custom_vjp
def narrow_latent(v):
    return lax.optimization_barrier(v.astype(jnp.bfloat16)).astype(jnp.float32)

@jax.custom_vjp
def low_rank_gradient(v):
    return v

def low_keep(v):
    return (narrow_latent(v), None)

def low_pass(kept, grad):
    return (grad,)

def back_keep(v):
    return (v, None)

def back_low(kept, grad):
    return (narrow_latent(grad),)
narrow_latent.defvjp(low_keep, low_pass)
low_rank_gradient.defvjp(back_keep, back_low)
EXACT = lax.Precision.HIGHEST

def precise_matmul(left, right):
    return jnp.dot(left, right, precision=EXACT, preferred_element_type=jnp.float32)

def layer_norm(values, gain, bias):
    center = values - lax.optimization_barrier(jnp.mean(values, axis=-1, keepdims=True))
    spread = lax.optimization_barrier(jnp.mean(center * center, axis=-1, keepdims=True))
    return center * lax.rsqrt(spread + 1e-05) * gain + bias

def shift_rows(values, keep):
    prior = jnp.concatenate([jnp.zeros_like(values[:1]), values[:-1]], axis=0)
    return prior * keep[:, None]

def attention_partition(values):
    return values.reshape(STEPS_PER_TEXT, H, HS)

def recurrence(acceptor_entries, lagged_lookup, mixture_vals, log_decay, unit_key, rate, keep):

    def block(state, items):

        def token(state, item):
            read_t, key_t, value_t, decay_t, unit_t, rate_t, keep_t = item
            along = jnp.einsum('hvk,hk->hv', state, unit_t, precision=EXACT)
            moved = state * jnp.exp(decay_t)[:, None, :] - along[:, :, None] * (unit_t * rate_t)[:, None, :]
            state = keep_t * moved + value_t[:, :, None] * key_t[:, None, :]
            return (state, jnp.einsum('hvk,hk->hv', state, read_t, precision=EXACT))
        return lax.scan(token, state, items)
    blocked = tuple((part.reshape((STEPS_PER_TEXT // BLK, BLK) + part.shape[1:]) for part in (acceptor_entries, lagged_lookup, mixture_vals, log_decay, unit_key, rate, keep)))
    start = jnp.zeros((H, HS, HS), jnp.float32)
    final_state, outputs = lax.scan(jax.checkpoint(block), start, blocked)
    return outputs.reshape(STEPS_PER_TEXT, H, HS)

def layer_forward(layer_parameters, hidden, first, keep):
    receptance_key_value_weight, time_output_weight, low_rank_down, low_rank_up, channel_key_weight, channel_value_weight, learned_arrays = layer_parameters
    first_split = DECAY_RANK
    second_split = DECAY_RANK + LA
    third_split = DECAY_RANK + LA + LV
    normed1 = layer_norm(hidden, learned_arrays[0], learned_arrays[1])
    prior1 = shift_rows(normed1, keep)
    x_rec, decay_input, x_key, value_input, rate_input, gate_input = [narrow_latent(normed1 + (prior1 - normed1) * learned_arrays[2 + index]) for index in range(6)]
    acceptor_entries = low_rank_gradient(precise_matmul(x_rec, receptance_key_value_weight[:, :EMBED_SIZE]))
    keyed = low_rank_gradient(precise_matmul(x_key, receptance_key_value_weight[:, EMBED_SIZE:2 * EMBED_SIZE]))
    valued = low_rank_gradient(precise_matmul(value_input, receptance_key_value_weight[:, 2 * EMBED_SIZE:]))
    decay_hidden = low_rank_gradient(precise_matmul(decay_input, low_rank_down[:, :first_split]))
    rate_hidden = low_rank_gradient(precise_matmul(rate_input, low_rank_down[:, first_split:second_split]))
    residual_hidden = low_rank_gradient(precise_matmul(value_input, low_rank_down[:, second_split:third_split]))
    gate_hidden = low_rank_gradient(precise_matmul(gate_input, low_rank_down[:, third_split:]))
    decay_lifted = low_rank_gradient(precise_matmul(narrow_latent(jnp.tanh(decay_hidden)), low_rank_up[:first_split]))
    rate_lifted = low_rank_gradient(precise_matmul(narrow_latent(rate_hidden), low_rank_up[first_split:second_split]))
    residual_lifted = low_rank_gradient(precise_matmul(narrow_latent(residual_hidden), low_rank_up[second_split:third_split]))
    valve_expanded = low_rank_gradient(precise_matmul(narrow_latent(jax.nn.sigmoid(gate_hidden)), low_rank_up[third_split:]))
    log_decay = -jnp.exp(-jax.nn.softplus(-(learned_arrays[8] + decay_lifted)) - 0.5)
    rate = jax.nn.sigmoid(learned_arrays[9] + rate_lifted)
    mixture_vals = valued + (first - valued) * jax.nn.sigmoid(learned_arrays[10] + residual_lifted)
    scaled = attention_partition(keyed * learned_arrays[11])
    unit_key = scaled * lax.rsqrt(lax.optimization_barrier(jnp.sum(scaled * scaled, axis=-1, keepdims=True)) + 1e-06)
    lagged_lookup = keyed * (1.0 + (rate - 1.0) * learned_arrays[12])
    state_out = recurrence(attention_partition(acceptor_entries), attention_partition(lagged_lookup), attention_partition(mixture_vals), attention_partition(log_decay), unit_key, attention_partition(rate), keep)
    center = state_out - lax.optimization_barrier(jnp.mean(state_out, axis=-1, keepdims=True))
    spread = lax.optimization_barrier(jnp.mean(center * center, axis=-1, keepdims=True))
    standardized_source = (center * lax.rsqrt(spread + 0.00064)).reshape(STEPS_PER_TEXT, EMBED_SIZE) * learned_arrays[14] + learned_arrays[15]
    present_reward_factor = lax.optimization_barrier(jnp.sum(attention_partition(acceptor_entries * lagged_lookup * learned_arrays[13]), axis=-1, keepdims=True)) * attention_partition(mixture_vals)
    valve_product = narrow_latent((standardized_source + present_reward_factor.reshape(STEPS_PER_TEXT, EMBED_SIZE)) * valve_expanded)
    mixed_h = hidden + low_rank_gradient(precise_matmul(valve_product, time_output_weight))
    normed2 = layer_norm(mixed_h, learned_arrays[16], learned_arrays[17])
    channel = narrow_latent(normed2 + (shift_rows(normed2, keep) - normed2) * learned_arrays[18])
    key_act = low_rank_gradient(precise_matmul(channel, channel_key_weight))
    squared = narrow_latent(jnp.square(jax.nn.relu(key_act)))
    return mixed_h + precise_matmul(squared, channel_value_weight)

def reference(layer_input, first_layer_values, segments, receptance_key_value_weight, time_output_weight, low_rank_down, low_rank_up, channel_key_weight, channel_value_weight, vectors, output_gradient):
    layer_parameters = tuple((weight_matrix.astype(jnp.float32) for weight_matrix in (receptance_key_value_weight, time_output_weight, low_rank_down, low_rank_up, channel_key_weight, channel_value_weight, vectors)))

    def one_sequence(totals, item):
        hidden, first, seg_ids, seed_grad = item
        keep = jnp.concatenate([jnp.zeros((1,), jnp.float32), (seg_ids[1:] == seg_ids[:-1]).astype(jnp.float32)])
        result, pull = jax.vjp(lambda weights, values, firsts: layer_forward(weights, values, firsts, keep), layer_parameters, hidden.astype(jnp.float32), first.astype(jnp.float32))
        grad_params, grad_hidden, grad_first = pull(seed_grad.astype(jnp.float32))
        totals = jax.tree.map(jnp.add, totals, grad_params)
        return (totals, (result.astype(jnp.bfloat16), grad_hidden, grad_first))
    zeros = jax.tree.map(jnp.zeros_like, layer_parameters)
    totals, (outputs, hidden_grads, first_grads) = lax.scan(one_sequence, zeros, (layer_input, first_layer_values, segments, output_gradient))
    return (outputs, hidden_grads, first_grads, totals[0], totals[1], totals[2], totals[3], totals[4], totals[5], totals[6])
```

```python
from functools import partial

import jax
import jax.numpy as jnp
from jax import lax
from jax.experimental import pallas as pl
from jax.experimental.pallas import tpu as pltpu
from jax.sharding import PartitionSpec as P

EMBED_SIZE = 1024
H = 16
HS = 64
FF = 4096
DECAY_RANK = 64
LA = 64
LV = 32
LOW = 320
PAIR = 2 * HS
HEAD_PAIRS = H // 2
SMALL = 16

NORM_EPS = 1e-05
GROUP_EPS = 0.00064
UNIT_EPS = 1e-06
F32 = jnp.float32
BF16 = jnp.bfloat16
HEAD_VMEM = 60 * 1024 * 1024
CHAIN_VMEM = 60 * 1024 * 1024
GRAD_VMEM = 60 * 1024 * 1024
ROWS = 32
MISC = 768
TAIL = 3 * EMBED_SIZE + MISC


def dot(left, right, dims):
    return lax.dot_general(left, right, (dims, ((), ())), preferred_element_type=F32)


def halves(values):
    high = values.astype(BF16)
    return high, (values - high.astype(F32)).astype(BF16)


def dot3(left, right, dims):
    left_high, left_low = halves(left)
    right_high, right_low = halves(right)
    return (
        dot(left_high, right_high, dims)
        + dot(left_high, right_low, dims)
        + dot(left_low, right_high, dims)
    )


def dot1(left, right, dims):
    return dot(left.astype(BF16), right.astype(BF16), dims)


NN = ((1,), (0,))
NT = ((1,), (1,))
TN = ((0,), (0,))


def first_head(rows):
    return lax.broadcasted_iota(jnp.int32, (rows, PAIR), 1) < HS


def stack(folded):
    mine = first_head(folded.shape[0])
    zero = jnp.zeros_like(folded)
    return jnp.concatenate([jnp.where(mine, folded, zero), jnp.where(mine, zero, folded)], axis=0)


def unstack(full):
    return jnp.where(first_head(HS), full[:HS], full[HS:])


def head_sum(values):
    row = lax.broadcasted_iota(jnp.int32, (PAIR, PAIR), 0) // HS
    column = lax.broadcasted_iota(jnp.int32, (PAIR, PAIR), 1) // HS
    same = (row == column).astype(BF16)
    high, low = halves(values)
    return dot(high, same, NN) + dot(low, same, NN)


def running_sum(values, reverse):
    rows = values.shape[0]
    row = lax.broadcasted_iota(jnp.int32, (rows, rows), 0)
    column = lax.broadcasted_iota(jnp.int32, (rows, rows), 1)
    ones = ((column >= row) if reverse else (column <= row)).astype(BF16)
    high, low = halves(values)
    return dot(ones, high, NN) + dot(ones, low, NN)


def token_sum(values):
    return jnp.sum(values, axis=0, keepdims=True)


def token_terms(read, keyed, valued, decay_up, rate_up, residual_up, first, vec):
    place = vec[8:9] + decay_up
    log_decay = -jnp.exp(-0.5) * jax.nn.sigmoid(place)
    rate = jax.nn.sigmoid(vec[9:10] + rate_up)
    residual = jax.nn.sigmoid(vec[10:11] + residual_up)
    mixed_value = valued + (first - valued) * residual
    scaled = keyed * vec[11:12]
    inverse_norm = lax.rsqrt(head_sum(scaled * scaled) + UNIT_EPS)
    unit = scaled * inverse_norm
    key = keyed * (1.0 + (rate - 1.0) * vec[12:13])
    return place, log_decay, rate, residual, mixed_value, inverse_norm, unit, key


def decayed(read, key, unit, rate, log_decay):
    total = running_sum(log_decay, False)
    grown = jnp.exp(total)
    shrunk = jnp.exp(-total)
    before = jnp.exp(total - log_decay)
    alpha = -before * unit
    beta = unit * rate * shrunk
    key_hat = key * shrunk
    read_hat = read * grown
    return grown, shrunk, before, alpha, beta, key_hat, read_hat


def solve_lower(lower):
    row = lax.broadcasted_iota(jnp.int32, (HS, PAIR), 0)
    column = lax.broadcasted_iota(jnp.int32, (HS, PAIR), 1) % HS
    eye = (row == column).astype(F32)
    small = (row // SMALL) == (column // SMALL)
    middle = (row // (2 * SMALL)) == (column // (2 * SMALL))
    zero = jnp.zeros_like(lower)
    power = jnp.where(small, lower, zero)
    result = eye + power
    power = dot3(power, stack(power), NN)
    for last in (False, False, True):
        held = stack(power)
        if last:
            result = result + dot3(result, held, NN)
        else:
            both = dot3(jnp.concatenate([result, power], axis=0), held, NN)
            result = result + both[:HS]
            power = both[HS:]
    for part in (
        jnp.where(jnp.logical_and(middle, jnp.logical_not(small)), lower, zero),
        jnp.where(middle, zero, lower),
    ):
        inner = dot3(result, stack(part), NN)
        result = result + dot3(inner, stack(result), NN)
    return result


def first_kernel(
    read_ref, keyed_ref, valued_ref, decay_ref, rate_ref, residual_ref, first_ref, vec_ref,
    strict_ref, inclusive_ref, start_ref, end_ref,
    pay_ref, solved_ref, lower_ref, reach_b_ref, reach_k_ref, start_alpha_ref, removed_ref,
    reads_ref, out_ref, key_out_ref, value_out_ref,
):
    vec = vec_ref[...]
    row = lax.broadcasted_iota(jnp.int32, (HS, PAIR), 0)
    column = lax.broadcasted_iota(jnp.int32, (HS, PAIR), 1) % HS
    eye = row == column
    mine = first_head(HS)
    for at in range(read_ref.shape[0]):
        strict, inclusive = strict_ref[at], inclusive_ref[at]
        start, end = start_ref[at], end_ref[at]
        read = read_ref[at]
        _, log_decay, rate, _, value, _, unit, key = token_terms(
            read, keyed_ref[at], valued_ref[at], decay_ref[at], rate_ref[at], residual_ref[at],
            first_ref[at].astype(F32), vec,
        )
        grown, _, _, alpha, beta, key_hat, read_hat = decayed(read, key, unit, rate, log_decay)
        last = grown[HS - 1 : HS]
        scores = dot3(
            jnp.concatenate([alpha, read_hat], axis=0),
            jnp.concatenate([stack(beta), stack(key_hat)], axis=0),
            NT,
        )
        lower_ab = scores[:HS, :PAIR] * strict
        lower_ak = scores[:HS, PAIR:] * strict
        reach_b = scores[HS:, :PAIR] * inclusive
        reach_k = scores[HS:, PAIR:] * inclusive
        solved = solve_lower(lower_ab)
        applied = dot3(jnp.concatenate([lower_ak, reach_k], axis=0), stack(value), NN)
        pair = dot3(
            solved, jnp.concatenate([stack(alpha * start), stack(applied[:HS])], axis=1), NN
        )
        start_alpha, removed = pair[:, :PAIR], pair[:, PAIR:]
        pair = dot3(reach_b, jnp.concatenate([stack(start_alpha), stack(removed)], axis=1), NN)
        reads = read_hat * start + pair[:, :PAIR]
        out = pair[:, PAIR:] + applied[HS:]
        beta_end = beta * (last * end)
        key_end = key_hat * (last * end)
        change = unstack(dot3(start_alpha, beta_end, TN)) + jnp.where(
            eye, start[HS - 1 : HS] * last - 1.0, 0.0
        )
        inject = unstack(
            dot3(
                jnp.concatenate([removed, value], axis=0),
                jnp.concatenate([beta_end, key_end], axis=0),
                TN,
            )
        )
        turned = pltpu.roll(inject, HS, 1)
        pay_ref[at, 0] = jnp.where(mine, change, turned).astype(BF16)
        pay_ref[at, 1] = jnp.where(mine, turned, change).astype(BF16)
        solved_ref[at] = solved
        lower_ref[at] = lower_ak
        reach_b_ref[at] = reach_b
        reach_k_ref[at] = reach_k
        start_alpha_ref[at] = start_alpha
        removed_ref[at] = removed
        reads_ref[at] = reads
        out_ref[at] = out
        key_out_ref[at] = key
        value_out_ref[at] = value


def chain_kernel(odd_ref, pay_ref, out_ref):
    shift = odd_ref[0] * HS
    state = jnp.zeros((HS, HS), F32)
    for at in range(pay_ref.shape[0]):
        high, low = halves(state)
        packed = jnp.concatenate([high.astype(F32), low.astype(F32)], axis=1)
        out_ref[at] = pltpu.roll(packed, shift, 1).astype(BF16)
        item = pltpu.roll(pay_ref[at].astype(F32), shift, 1)
        change = item[:, :HS].astype(BF16)
        moved = dot(jnp.concatenate([high, low], axis=0), change, NN)
        state = state + moved[:HS] + moved[HS:] + item[:, HS:]


def chain_back_kernel(odd_ref, pay_ref, grad_ref, out_ref):
    shift = odd_ref[0] * HS
    state = jnp.zeros((HS, HS), F32)
    for at in reversed(range(pay_ref.shape[0])):
        high, low = halves(state)
        packed = jnp.concatenate([high.astype(F32), low.astype(F32)], axis=1)
        out_ref[at] = pltpu.roll(packed, shift, 1).astype(BF16)
        change = pltpu.roll(pay_ref[at].astype(F32), shift, 1)[:, :HS].astype(BF16)
        item = pltpu.roll(grad_ref[at].astype(F32), shift, 1)
        moved = dot(jnp.concatenate([high, low], axis=0), change, NT)
        state = state + moved[:HS] + moved[HS:] + item[:, :HS] + item[:, HS:]


def joined(pay):
    low_first = pay[0].astype(F32)
    low_second = pay[1].astype(F32)
    return jnp.where(
        first_head(HS),
        low_first + pltpu.roll(low_first, HS, 1),
        low_second + pltpu.roll(low_second, HS, 1),
    )


def parted(values):
    high, low = halves(values)
    high, low = high.astype(F32), pltpu.roll(low.astype(F32), HS, 1)
    mine = first_head(HS)
    return jnp.where(mine, high, low).astype(BF16), jnp.where(mine, low, high).astype(BF16)


def head_terms(state_out, read, key, vec):
    center = state_out - head_sum(state_out) * (1.0 / HS)
    inverse = lax.rsqrt(head_sum(center * center) * (1.0 / HS) + GROUP_EPS)
    bonus = head_sum(read * key * vec[13:14])
    return center * inverse, inverse, bonus


def output_kernel(
    state_ref, reads_ref, local_ref, read_ref, key_ref, value_ref, gate_ref, vec_ref,
    out_ref, gated_ref,
):
    vec = vec_ref[...]
    for at in range(reads_ref.shape[0]):
        state = joined(state_ref[at])
        state_out = local_ref[at] + dot3(reads_ref[at], stack(state), NT)
        normed, _, bonus = head_terms(state_out, read_ref[at], key_ref[at], vec)
        mixed = normed * vec[14:15] + vec[15:16] + bonus * value_ref[at]
        out_ref[at] = state_out
        gated_ref[at] = (mixed * gate_ref[at]).astype(BF16)


def head_back_kernel(
    grad_ref, out_ref, reads_ref, read_ref, key_ref, value_ref, gate_ref, vec_ref,
    out_grad_ref, gate_grad_ref, read_grad_ref, key_grad_ref, value_grad_ref, pay_ref, vec_grad_ref,
):
    vec = vec_ref[...]
    sums = jnp.zeros((8, PAIR), F32)
    place = lax.broadcasted_iota(jnp.int32, (8, PAIR), 0)
    for at in range(reads_ref.shape[0]):
        read, key, value = read_ref[at], key_ref[at], value_ref[at]
        normed, inverse, bonus = head_terms(out_ref[at], read, key, vec)
        mixed = normed * vec[14:15] + vec[15:16] + bonus * value
        grad = grad_ref[at]
        grad_mixed = grad * gate_ref[at]
        gate_grad_ref[at] = (grad * mixed).astype(BF16)
        along = head_sum(grad_mixed * value)
        value_grad_ref[at] = bonus * grad_mixed
        read_grad_ref[at] = along * key * vec[13:14]
        key_grad_ref[at] = along * read * vec[13:14]
        grad_normed = grad_mixed * vec[14:15]
        out_grad = inverse * (
            grad_normed
            - head_sum(grad_normed) * (1.0 / HS)
            - normed * (head_sum(grad_normed * normed) * (1.0 / HS))
        )
        out_grad_ref[at] = out_grad
        first, second = parted(unstack(dot3(out_grad, reads_ref[at], TN)))
        pay_ref[at, 0] = first
        pay_ref[at, 1] = second
        sums = sums + jnp.where(place == 0, token_sum(along * read * key), 0.0)
        sums = sums + jnp.where(place == 1, token_sum(grad_mixed * normed), 0.0)
        sums = sums + jnp.where(place == 2, token_sum(grad_mixed), 0.0)
    vec_grad_ref[...] = sums


def last_kernel(
    read_ref, keyed_ref, valued_ref, decay_ref, rate_ref, residual_ref, first_ref, vec_ref,
    strict_ref, inclusive_ref, start_ref, end_ref,
    solved_ref, lower_ref, reach_b_ref, reach_k_ref, start_alpha_ref, removed_ref,
    state_ref, after_ref, out_grad_ref, read_grad_ref, key_grad_ref, value_grad_ref,
    d_read_ref, d_keyed_ref, d_valued_ref, d_decay_ref, d_rate_ref, d_residual_ref, d_first_ref,
    vec_grad_ref,
):
    vec = vec_ref[...]
    sums = jnp.zeros((8, PAIR), F32)
    place = lax.broadcasted_iota(jnp.int32, (8, PAIR), 0)
    final_row = lax.broadcasted_iota(jnp.int32, (HS, PAIR), 0) == HS - 1
    for at in range(read_ref.shape[0]):
        strict, inclusive = strict_ref[at], inclusive_ref[at]
        start, end = start_ref[at], end_ref[at]
        read, keyed, valued = read_ref[at], keyed_ref[at], valued_ref[at]
        first = first_ref[at].astype(F32)
        spot, log_decay, rate, residual, value, inverse_norm, unit, key = token_terms(
            read, keyed, valued, decay_ref[at], rate_ref[at], residual_ref[at], first, vec
        )
        grown, shrunk, before, alpha, beta, key_hat, read_hat = decayed(
            read, key, unit, rate, log_decay
        )
        last = grown[HS - 1 : HS]
        beta_end = beta * (last * end)
        key_end = key_hat * (last * end)
        state = joined(state_ref[at])
        after = joined(after_ref[at])
        out_grad = out_grad_ref[at]
        solution_rows = dot3(start_alpha_ref[at], stack(state), NT) + removed_ref[at]
        reached = dot3(
            jnp.concatenate([reach_b_ref[at], reach_k_ref[at]], axis=1), out_grad, TN
        )
        carried = dot3(jnp.concatenate([beta_end, key_end], axis=0), stack(after), NT)
        d_rows = unstack(reached[:PAIR]) + carried[:HS]
        d_value = unstack(reached[PAIR:]) + carried[HS:]
        back = unstack(dot3(solved_ref[at], d_rows, TN))
        d_value = d_value + unstack(dot3(lower_ref[at], back, TN)) + value_grad_ref[at]
        outer = jnp.concatenate([out_grad, back], axis=0)
        scores = dot3(
            outer, jnp.concatenate([stack(solution_rows), stack(value)], axis=0), NT
        )
        mask = jnp.concatenate([inclusive, strict], axis=0)
        scores = scores * jnp.concatenate([mask, mask], axis=1)
        ends = dot3(jnp.concatenate([solution_rows, value], axis=0), stack(after), NN)
        d_beta_end, d_key_end = ends[:HS] * end, ends[HS:] * end
        entries = dot3(outer, stack(state), NN)
        lefts = dot3(scores, jnp.concatenate([stack(beta), stack(key_hat)], axis=0), NN)
        d_read_hat = entries[:HS] * start + lefts[:HS]
        d_alpha = entries[HS:] * start + lefts[HS:]
        rights = dot3(scores, jnp.concatenate([read_hat, alpha], axis=0), TN)
        d_beta = unstack(rights[:PAIR]) + d_beta_end * last
        d_key_hat = unstack(rights[PAIR:]) + d_key_end * last
        d_last = token_sum(beta * d_beta_end + key_hat * d_key_end) + start[
            HS - 1 : HS
        ] * token_sum(state * after)
        d_moved = d_beta * shrunk
        d_key = key_grad_ref[at] + d_key_hat * shrunk
        d_read_ref[at] = (read_grad_ref[at] + d_read_hat * grown).astype(BF16)
        along = d_alpha * alpha
        d_total = d_read_hat * read_hat - d_beta * beta - d_key_hat * key_hat + along
        d_total = d_total + jnp.where(final_row, d_last * last, 0.0)
        d_decay = running_sum(d_total, True) - along
        d_unit = rate * d_moved - before * d_alpha
        d_rate = unit * d_moved + d_key * keyed * vec[12:13]
        d_scaled = (d_unit - unit * head_sum(unit * d_unit)) * inverse_norm
        d_keyed = d_key * (1.0 + (rate - 1.0) * vec[12:13]) + d_scaled * vec[11:12]
        d_first = d_value * residual
        d_residual = d_first * (first - valued) * (1.0 - residual)
        d_rate_up = d_rate * rate * (1.0 - rate)
        d_decay_up = d_decay * log_decay * jax.nn.sigmoid(-spot)
        d_keyed_ref[at] = d_keyed.astype(BF16)
        d_valued_ref[at] = (d_value * (1.0 - residual)).astype(BF16)
        d_decay_ref[at] = d_decay_up.astype(BF16)
        d_rate_ref[at] = d_rate_up.astype(BF16)
        d_residual_ref[at] = d_residual.astype(BF16)
        d_first_ref[at] = d_first
        for row, part in enumerate(
            (d_decay_up, d_rate_up, d_residual, d_scaled * keyed, d_key * keyed * (rate - 1.0))
        ):
            sums = sums + jnp.where(place == row, token_sum(part), 0.0)
    vec_grad_ref[...] = sums


def head_call(body, inputs, outputs, flops):
    count = inputs[0][0].shape[0]

    def spec(kind):
        if kind == "tokens":
            return pl.BlockSpec((count, HS, PAIR), lambda i: (0, 0, i))
        if kind == "rows":
            return pl.BlockSpec((24, PAIR), lambda i: (0, i))
        if kind == "sums":
            return pl.BlockSpec((8, PAIR), lambda i: (0, i))
        if kind == "pay":
            return pl.BlockSpec((count, 2, HS, PAIR), lambda i: (0, i, 0, 0))
        return pl.BlockSpec((count, HS, PAIR), lambda i: (0, 0, 0))

    shapes = {
        "tokens": (count, HS, EMBED_SIZE),
        "sums": (8, EMBED_SIZE),
        "pay": (count, H, HS, PAIR),
    }
    bytes_moved = sum(4 * a.size for a, _ in inputs) + 4 * sum(
        count * HS * EMBED_SIZE for _ in outputs
    )
    return pl.pallas_call(
        body,
        grid=(HEAD_PAIRS,),
        in_specs=[spec(kind) for _, kind in inputs],
        out_specs=[spec(kind) for kind, _ in outputs],
        out_shape=[jax.ShapeDtypeStruct(shapes[kind], dtype) for kind, dtype in outputs],
        compiler_params=pltpu.CompilerParams(vmem_limit_bytes=HEAD_VMEM),
        cost_estimate=pl.CostEstimate(
            flops=flops, bytes_accessed=bytes_moved, transcendentals=count * HS * EMBED_SIZE * 6
        ),
    )(*[array for array, _ in inputs])


def chain_call(body, odd, *arrays):
    return pl.pallas_call(
        body,
        in_specs=[pl.BlockSpec(memory_space=pltpu.SMEM)]
        + [pl.BlockSpec(memory_space=pltpu.VMEM)] * len(arrays),
        out_specs=pl.BlockSpec(memory_space=pltpu.VMEM),
        out_shape=jax.ShapeDtypeStruct(arrays[0].shape, BF16),
        compiler_params=pltpu.CompilerParams(vmem_limit_bytes=CHAIN_VMEM),
        cost_estimate=pl.CostEstimate(
            flops=32 * 4 * HS**3, bytes_accessed=3 * 1024 * 1024, transcendentals=0
        ),
    )(odd, *arrays)


def turned_into(target, values):
    for at in range(values.shape[1] // 128):
        target(at, values[:, at * 128 : (at + 1) * 128].astype(F32).T.astype(BF16))


def channel_grad_kernel(
    squared_ref, seed_ref, channel_ref, act_ref, gated_ref, att_ref, out_ref, hidden, features
):
    step = pl.program_id(0)

    def into_hidden(at, part):
        hidden[at] = part.reshape(4, ROWS, 128)

    def into_features(at, part):
        features[at] = part

    @pl.when(step == 0)
    def _():
        turned_into(into_hidden, squared_ref)

    @pl.when(step == 4)
    def _():
        turned_into(into_features, channel_ref)

    @pl.when(step == 8)
    def _():
        turned_into(into_features, gated_ref)

    def write(group, left, right):
        out_ref[pl.ds(group * 4, 4)] = (
            dot(left, right, NN).astype(BF16).reshape(4, ROWS, EMBED_SIZE)
        )

    @pl.when(step < 4)
    def _():
        for group in range(8):
            left = hidden[pl.ds(group * 4, 4), step].reshape(128, 128)
            write(group, left, seed_ref[...])

    @pl.when(jnp.logical_and(step >= 4, step < 8))
    def _():
        for group in range(8):
            write(group, features[group], act_ref[...])

    @pl.when(step == 8)
    def _():
        for group in range(8):
            write(group, features[group], att_ref[...])


def channel_grads(squared, seed, channel, act, gated, att):
    tokens = squared.shape[0]
    whole = lambda width: pl.BlockSpec((tokens, width), lambda j: (0, 0))
    return pl.pallas_call(
        channel_grad_kernel,
        grid=(9,),
        in_specs=[
            whole(FF),
            whole(EMBED_SIZE),
            whole(EMBED_SIZE),
            pl.BlockSpec((tokens, EMBED_SIZE), lambda j: (0, jnp.clip(j - 4, 0, 3))),
            whole(EMBED_SIZE),
            whole(EMBED_SIZE),
        ],
        out_specs=pl.BlockSpec((32, ROWS, EMBED_SIZE), lambda j: (0, j, 0)),
        out_shape=jax.ShapeDtypeStruct((32, 9 * ROWS, EMBED_SIZE), BF16),
        scratch_shapes=[
            pltpu.VMEM((32, 4, ROWS, tokens), BF16),
            pltpu.VMEM((8, 128, tokens), BF16),
        ],
        compiler_params=pltpu.CompilerParams(vmem_limit_bytes=GRAD_VMEM),
        cost_estimate=pl.CostEstimate(
            flops=2 * tokens * 9 * EMBED_SIZE**2, bytes_accessed=20_000_000, transcendentals=0
        ),
    )(squared, seed, channel, act, gated, att)


def time_grad_kernel(core_ref, *refs):
    lefts, (d_read, d_keyed, d_valued, lows), vec_grad, outs, turned = (
        refs[:10], refs[10:14], refs[14], refs[15:19], refs[19]
    )

    def into(slot):
        def write(at, part):
            turned[slot, at * 2 : at * 2 + 2] = part.reshape(2, 2, ROWS, 128)

        return write

    for slot, left in enumerate(lefts):
        turned_into(into(slot), left)
    tokens = lefts[0].shape[0]
    rows = vec_grad.shape[0]
    padded = jnp.concatenate(
        [vec_grad[...], jnp.zeros((128 - rows, EMBED_SIZE), F32)], axis=0
    )
    turned_into(into(10), padded)
    low_all = lows[...]
    lane = lax.broadcasted_iota(jnp.int32, low_all.shape, 1)
    edges = (0, DECAY_RANK, DECAY_RANK + LA, DECAY_RANK + LA + LV, LOW)
    parts = []
    for side in range(2):
        for at in range(4):
            inside = jnp.logical_and(
                lane >= side * LOW + edges[at], lane < side * LOW + edges[at + 1]
            )
            parts.append(jnp.where(inside, low_all, jnp.zeros_like(low_all)))
    cut = 3 * EMBED_SIZE - TAIL // 2 - EMBED_SIZE
    core = core_ref[0]
    for which in range(2):
        chosen = (1 - core) if which == 0 else core
        first, second = outs[2 * which], outs[2 * which + 1]
        for group in range(4):
            rows_at = pl.ds(group * 128, 128)

            def left(slot):
                return turned[slot, pl.ds(group * 4, 4), chosen].reshape(128, 128)

            by_key = dot(left(2), d_keyed[...], NN).astype(BF16)
            first[rows_at, :EMBED_SIZE] = dot(left(0), d_read[...], NN).astype(BF16)
            first[rows_at, EMBED_SIZE:] = by_key[:, : EMBED_SIZE - cut]
            second[rows_at, :cut] = by_key[:, EMBED_SIZE - cut :]
            second[rows_at, cut : cut + EMBED_SIZE] = dot(left(3), d_valued[...], NN).astype(BF16)
            total = jnp.zeros((128, 2 * LOW), F32)
            for slot, part in zip((1, 4, 3, 5, 6, 7, 8, 9), parts):
                total = total + dot(left(slot), part, NN)
            second[rows_at, cut + EMBED_SIZE : cut + EMBED_SIZE + 2 * LOW] = total.astype(BF16)
            second[rows_at, cut + EMBED_SIZE + 2 * LOW :] = left(10)


def time_grads(core, lefts, rights, vec_grad):
    tokens = lefts[0].shape[0]
    half = (EMBED_SIZE // 2, TAIL // 2)
    return pl.pallas_call(
        time_grad_kernel,
        grid=(1,),
        in_specs=[pl.BlockSpec(memory_space=pltpu.SMEM)]
        + [pl.BlockSpec(part.shape, lambda i: (0, 0)) for part in (*lefts, *rights, vec_grad)],
        out_specs=[pl.BlockSpec(half, lambda i: (0, 0))] * 4,
        out_shape=[jax.ShapeDtypeStruct(half, BF16)] * 4,
        scratch_shapes=[pltpu.VMEM((11, 16, 2, ROWS, tokens), BF16)],
        compiler_params=pltpu.CompilerParams(vmem_limit_bytes=GRAD_VMEM),
        cost_estimate=pl.CostEstimate(
            flops=2 * tokens * EMBED_SIZE * 4 * TAIL, bytes_accessed=12_000_000, transcendentals=0
        ),
    )(core, *lefts, *rights, vec_grad)


def moved(values, z=0, x=0, core=0):
    pairs = []
    for at in range(32):
        spot = (at // 8, at // 2 % 4, at % 2)
        to = ((spot[0] + z) % 4, (spot[1] + x) % 4, (spot[2] + core) % 2)
        pairs.append((at, to[0] * 8 + to[1] * 2 + to[2]))
    return lax.ppermute(values, "shard", pairs)


def along_ring(chunk, send):
    far = chunk(2)
    half = far.shape[0] // 2
    from_behind = send(far[:half], 1)
    from_ahead = send(far[half:], -1)
    ahead, behind = chunk(1).astype(F32), chunk(3).astype(F32)
    ahead = jnp.concatenate([ahead[:half] + from_behind.astype(F32), ahead[half:]], axis=0)
    behind = jnp.concatenate([behind[:half], behind[half:] + from_ahead.astype(F32)], axis=0)
    one = send(ahead.astype(BF16), 1)
    other = send(behind.astype(BF16), -1)
    return chunk(0).astype(F32) + one.astype(F32) + other.astype(F32)


def around_ring(chunk, send):
    total = chunk(0).astype(F32)
    for step in (1, 3, 2):
        total = total + send(chunk(step), step).astype(F32)
    return total


def summed_by_owner(others, owns, beside):
    place = lax.axis_index("shard")
    z, x = place // 8, place // 2 % 4
    arrived = [moved(part, core=1) for part in others]
    whole = [
        (own.astype(F32) + part.astype(F32)).astype(BF16).reshape(4, 4, ROWS, -1)
        for own, part in zip(owns, arrived)
    ]
    pick = lambda values, at, axis: lax.dynamic_index_in_dim(values, at % 4, axis, keepdims=False)
    along_x = lambda values, by: moved(values, x=by)
    along_z = lambda values, by: moved(values, z=by)
    first = along_ring(lambda k: pick(whole[0], x + k, 1), along_x).astype(BF16)
    second = along_ring(lambda k: pick(whole[1], z + k, 0), along_z).astype(BF16)
    first, second, beside = lax.optimization_barrier((first, second, beside))
    first = around_ring(lambda k: pick(first, z + k, 0), along_z)
    second = around_ring(lambda k: pick(second, x + k, 0), along_x)
    return jnp.concatenate([first, second], axis=1), beside


def summed_over_groups(values):
    place = lax.axis_index("rep")
    send = lambda part, by: lax.ppermute(part, "rep", [(i, (i + by) % 4) for i in range(4)])
    quarters = values.astype(BF16).reshape(4, -1, values.shape[1])
    pick = lambda k: lax.dynamic_index_in_dim(quarters, (place + k) % 4, 0, keepdims=False)
    mine = around_ring(pick, send).astype(BF16)
    parts = jnp.stack([mine] + [send(mine, step) for step in (1, 2, 3)])
    ordered = [
        lax.dynamic_index_in_dim(parts, (place - k) % 4, 0, keepdims=False) for k in range(4)
    ]
    return jnp.concatenate(ordered, axis=0).astype(F32)


def passed_along(rows, by):
    size = lax.axis_size("shard")
    pairs = [(i, i + by) for i in range(size) if 0 <= i + by < size]
    return lax.ppermute(rows, "shard", pairs)


def product(left, right):
    return jnp.dot(left, right, preferred_element_type=F32)


def product_tn(left, right):
    return lax.dot_general(left, right, (((0,), (0,)), ((), ())), preferred_element_type=F32)


def product_nt(left, right):
    return lax.dot_general(left, right, (((1,), (1,)), ((), ())), preferred_element_type=F32)


def layer_norm(values, gain, bias):
    center = values - jnp.mean(values, axis=-1, keepdims=True)
    spread = jnp.mean(center * center, axis=-1, keepdims=True)
    return center * lax.rsqrt(spread + NORM_EPS) * gain + bias


def norm_piece(values, vec, row):
    return layer_norm(values, vec[row], vec[row + 1])


def mix_piece(values, before, vec, keep, first_row, count):
    prior = jnp.concatenate([before[:, None], values[:, :-1]], axis=1) * keep[:, :, None]
    delta = prior - values
    return tuple(values + delta * vec[first_row + index] for index in range(count))


def flat(values):
    return values.reshape(-1, values.shape[-1])


def gathered(shard):
    return lax.all_gather(shard, "shard", axis=0, tiled=True)


def scattered(full):
    return lax.psum_scatter(full, "shard", scatter_dimension=0, tiled=True)


def exchanged(pay):
    return lax.all_to_all(pay.reshape((-1,) + pay.shape[-2:]), "shard", 0, 0, tiled=False)


def local(
    layer_input,
    first_layer_values,
    segments,
    receptance_key_value_weight,
    time_output_weight,
    low_rank_down,
    low_rank_up,
    channel_key_weight,
    channel_value_weight,
    vectors,
    output_gradient,
):
    count, length, width = layer_input.shape
    rkv_end = 3 * EMBED_SIZE
    down_end = rkv_end + LOW
    up_end = down_end + LOW
    vec_end = up_end + vectors.shape[0]
    splits = (0, DECAY_RANK, DECAY_RANK + LA, DECAY_RANK + LA + LV, LOW)
    packed = jnp.concatenate(
        [
            receptance_key_value_weight,
            low_rank_down,
            low_rank_up.T,
            vectors.T,
            jnp.zeros((vectors.shape[1], 109), BF16),
        ],
        axis=1,
    )
    full = gathered(packed)
    full_out_key = gathered(jnp.concatenate([channel_key_weight, time_output_weight], axis=1))
    full_val = gathered(channel_value_weight)
    full_rkv = full[:, :rkv_end]
    full_down = full[:, rkv_end:down_end]
    full_up = full[:, down_end:up_end]
    vec = full[:, up_end : up_end + 24].T.astype(F32)
    full_key = full_out_key[:, :FF]
    full_out = full_out_key[:, FF:]
    downs = [full_down[:, splits[i] : splits[i + 1]] for i in range(4)]
    ups = [full_up[:, splits[i] : splits[i + 1]] for i in range(4)]

    edge = passed_along(segments[:, -1] + 1, 1) - 1
    keep = jnp.concatenate(
        [segments[:, :1] == edge[:, None], segments[:, 1:] == segments[:, :-1]], axis=1
    ).astype(F32)
    same = (segments[:, :, None] == segments[:, None, :]).astype(F32)
    later = lax.broadcasted_iota(jnp.int32, (length, length), 0)
    earlier = lax.broadcasted_iota(jnp.int32, (length, length), 1)
    strict = jnp.tile(same * (later > earlier).astype(F32), (1, 1, 2))
    inclusive = jnp.tile(same * (later >= earlier).astype(F32), (1, 1, 2))
    start = jnp.broadcast_to(
        (segments == edge[:, None]).astype(F32)[:, :, None], (count, length, PAIR)
    )
    end = jnp.broadcast_to(same[:, -1, :, None], (count, length, PAIR))
    masks = [(strict, "masks"), (inclusive, "masks"), (start, "masks"), (end, "masks")]
    odd = (lax.axis_index("shard") % 2).astype(jnp.int32).reshape(1)

    hidden = layer_input.astype(F32)
    raw_before = passed_along(layer_input[:, -1], 1).astype(F32)
    normed1, pull_norm1 = jax.vjp(partial(norm_piece, row=0), hidden, vec)
    before1 = norm_piece(raw_before, vec, 0)
    mixes, pull_mix1 = jax.vjp(
        partial(mix_piece, keep=keep, first_row=2, count=6), normed1, before1, vec
    )
    x_r, x_w, x_k, x_v, x_a, x_g = [flat(part.astype(BF16)) for part in mixes]
    shape = (count, length, width)
    read = product(x_r, full_rkv[:, :EMBED_SIZE]).reshape(shape)
    keyed = product(x_k, full_rkv[:, EMBED_SIZE : 2 * EMBED_SIZE]).reshape(shape)
    valued = product(x_v, full_rkv[:, 2 * EMBED_SIZE :]).reshape(shape)
    low_inputs = (x_w, x_a, x_v, x_g)
    lows = [product(part, weight) for part, weight in zip(low_inputs, downs)]
    decay_f = jnp.tanh(lows[0])
    gate_f = jax.nn.sigmoid(lows[3])
    mids = [decay_f.astype(BF16), lows[1].astype(BF16), lows[2].astype(BF16), gate_f.astype(BF16)]
    decay_up, rate_up, residual_up, gate = [
        product_nt(part, weight).reshape(shape) for part, weight in zip(mids, ups)
    ]
    tokens = [
        (part, "tokens")
        for part in (read, keyed, valued, decay_up, rate_up, residual_up, first_layer_values)
    ]
    (
        pay, solved, lower, reach_b, reach_k, start_alpha, removed, reads, local_out, key, value
    ) = head_call(
        first_kernel,
        tokens + [(vec, "rows")] + masks,
        [("pay", BF16)] + [("tokens", F32)] * 10,
        3_000_000_000,
    )
    chain_items = exchanged(pay)
    states = exchanged(chain_call(chain_kernel, odd, chain_items)).reshape(pay.shape)
    gate_terms = [
        (read, "tokens"), (key, "tokens"), (value, "tokens"), (gate, "tokens"), (vec, "rows")
    ]
    state_out, gated = head_call(
        output_kernel,
        [(states, "pay"), (reads, "tokens"), (local_out, "tokens")] + gate_terms,
        [("tokens", F32), ("tokens", BF16)],
        300_000_000,
    )
    gated = flat(gated)
    mixed_h = hidden + product(gated, full_out).reshape(shape)

    normed2, pull_norm2 = jax.vjp(partial(norm_piece, row=16), mixed_h, vec)
    before2 = passed_along(normed2[:, -1], 1)
    channel, pull_mix2 = jax.vjp(
        partial(mix_piece, keep=keep, first_row=18, count=1), normed2, before2, vec
    )
    channel_low = flat(channel[0].astype(BF16))
    key_act = jax.nn.relu(product(channel_low, full_key))
    squared = jnp.square(key_act).astype(BF16)
    hidden_out = (mixed_h + product(squared, full_val).reshape(shape)).astype(BF16)

    seed = flat(output_gradient)
    grad_act = (2.0 * key_act * product_nt(seed, full_val)).astype(BF16)
    grad_channel = product_nt(grad_act, full_key).reshape(shape)
    grad_norm2, grad_before2, vec_grad_a = pull_mix2((grad_channel,))
    grad_norm2 = grad_norm2.at[:, -1].add(passed_along(grad_before2, -1))
    grad_mixed, vec_grad_b = pull_norm2(grad_norm2)
    grad_mixed = grad_mixed + output_gradient.astype(F32)
    grad_att = flat(grad_mixed.astype(BF16))
    grad_gated = product_nt(grad_att, full_out).reshape(shape)
    channel_part = channel_grads(squared, seed, channel_low, grad_act, gated, grad_att)
    grad_gated, channel_part = lax.optimization_barrier((grad_gated, channel_part))
    own_channel = scattered(channel_part)[0]

    out_grad, gate_grad, read_grad, key_grad, value_grad, grad_pay, vec_sums_a = head_call(
        head_back_kernel,
        [(grad_gated, "tokens"), (state_out, "tokens"), (reads, "tokens")] + gate_terms,
        [("tokens", F32), ("tokens", BF16)]
        + [("tokens", F32)] * 3
        + [("pay", BF16), ("sums", F32)],
        300_000_000,
    )
    after = exchanged(
        chain_call(chain_back_kernel, odd, chain_items, exchanged(grad_pay))
    ).reshape(pay.shape)
    d_read, d_keyed, d_valued, d_decay, d_rate, d_residual, first_grad, vec_sums_b = head_call(
        last_kernel,
        tokens
        + [(vec, "rows")]
        + masks
        + [
            (part, "tokens")
            for part in (solved, lower, reach_b, reach_k, start_alpha, removed)
        ]
        + [(states, "pay"), (after, "pay")]
        + [(part, "tokens") for part in (out_grad, read_grad, key_grad, value_grad)],
        [("tokens", BF16)] * 6 + [("tokens", F32), ("sums", F32)],
        3_000_000_000,
    )
    d_read, d_keyed, d_valued = flat(d_read), flat(d_keyed), flat(d_valued)
    d_ups = [flat(part) for part in (d_decay, d_rate, d_residual, gate_grad)]
    d_mids = [product(part, weight) for part, weight in zip(d_ups, ups)]
    d_mids[0] = d_mids[0] * (1.0 - decay_f * decay_f)
    d_mids[3] = d_mids[3] * gate_f * (1.0 - gate_f)
    d_lows = [part.astype(BF16) for part in d_mids]
    back = [product_nt(low, weight) for low, weight in zip(d_lows, downs)]
    d_x_r = product_nt(d_read, full_rkv[:, :EMBED_SIZE])
    d_x_k = product_nt(d_keyed, full_rkv[:, EMBED_SIZE : 2 * EMBED_SIZE])
    d_x_v = product_nt(d_valued, full_rkv[:, 2 * EMBED_SIZE :]) + back[2]
    grad_norm1, grad_before1, vec_grad_c = pull_mix1(
        tuple(part.reshape(shape) for part in (d_x_r, back[0], d_x_k, d_x_v, back[1], back[3]))
    )
    grad_norm1 = grad_norm1.at[:, -1].add(passed_along(grad_before1, -1))
    grad_hidden, vec_grad_d = pull_norm1(grad_norm1)
    hidden_grad = grad_mixed + grad_hidden
    vec_grad = vec_grad_a + vec_grad_b + vec_grad_c + vec_grad_d
    vec_grad = vec_grad + jnp.concatenate(
        [
            jnp.zeros((8, width), F32),
            vec_sums_b[:5],
            vec_sums_a[:3],
            jnp.zeros((vec.shape[0] - 16, width), F32),
        ],
        axis=0,
    )
    lows_all = jnp.concatenate(d_lows + mids, axis=1)
    core = (lax.axis_index("shard") % 2).astype(jnp.int32).reshape(1)
    grads = time_grads(
        core,
        (x_r, x_w, x_k, x_v, x_a, x_g, *d_ups),
        (d_read, d_keyed, d_valued, lows_all),
        vec_grad,
    )
    own, own_channel = summed_by_owner(grads[:2], grads[2:], summed_over_groups(own_channel))
    own = summed_over_groups(own)
    own_key = jnp.concatenate([own_channel[128 + 32 * k : 160 + 32 * k] for k in range(4)], axis=1)
    return (
        hidden_out,
        hidden_grad,
        first_grad,
        own[:, :rkv_end],
        own_channel[256:],
        own[:, rkv_end:down_end],
        own[:, down_end:up_end].T,
        own_key,
        own_channel[:128],
        own[:, up_end:vec_end].T,
    )


def solution(mesh):
    tokens = P("rep", "shard", None)
    rows = P("shard", None)
    columns = P(None, "shard")
    return jax.shard_map(
        local,
        mesh=mesh,
        in_specs=(
            tokens, tokens, P("rep", "shard"), rows, rows, rows, columns, rows, rows, columns, tokens
        ),
        out_specs=(tokens, tokens, tokens, rows, rows, rows, columns, rows, rows, columns),
        check_vma=False,
    )
```

```python
from functools import partial

import jax
import jax.numpy as jnp
from jax import lax
from jax.experimental import pallas as pl
from jax.experimental.pallas import tpu as pltpu
from jax.sharding import PartitionSpec as P

EMBED_SIZE = 1024
H = 16
HS = 64
FF = 4096
DECAY_RANK = 64
LA = 64
LV = 32
LOW = 320
PAIR = 2 * HS
HEAD_PAIRS = H // 2
SMALL = 16

NORM_EPS = 1e-05
GROUP_EPS = 0.00064
UNIT_EPS = 1e-06
F32 = jnp.float32
BF16 = jnp.bfloat16
HEAD_VMEM = 60 * 1024 * 1024
CHAIN_VMEM = 60 * 1024 * 1024
GRAD_VMEM = 60 * 1024 * 1024
ROWS = 32
LOW_WIDE = 384
DOWN_AT = 3 * EMBED_SIZE
UP_AT = DOWN_AT + LOW_WIDE
OUT_AT = UP_AT + LOW_WIDE
HALF = 2 * EMBED_SIZE + LOW_WIDE
EDGES = (0, DECAY_RANK, DECAY_RANK + LA, DECAY_RANK + LA + LV, LOW)


def dot(left, right, dims):
    return lax.dot_general(left, right, (dims, ((), ())), preferred_element_type=F32)


def halves(values):
    high = values.astype(BF16)
    return high, (values - high.astype(F32)).astype(BF16)


def dot3(left, right, dims):
    left_high, left_low = halves(left)
    right_high, right_low = halves(right)
    return (
        dot(left_high, right_high, dims)
        + dot(left_high, right_low, dims)
        + dot(left_low, right_high, dims)
    )


def dot1(left, right, dims):
    return dot(left.astype(BF16), right.astype(BF16), dims)


NN = ((1,), (0,))
NT = ((1,), (1,))
TN = ((0,), (0,))


def first_head(rows):
    return lax.broadcasted_iota(jnp.int32, (rows, PAIR), 1) < HS


def stack(folded):
    mine = first_head(folded.shape[0])
    zero = jnp.zeros_like(folded)
    return jnp.concatenate([jnp.where(mine, folded, zero), jnp.where(mine, zero, folded)], axis=0)


def unstack(full):
    return jnp.where(first_head(HS), full[:HS], full[HS:])


def head_sum(values):
    row = lax.broadcasted_iota(jnp.int32, (PAIR, PAIR), 0) // HS
    column = lax.broadcasted_iota(jnp.int32, (PAIR, PAIR), 1) // HS
    same = (row == column).astype(BF16)
    high, low = halves(values)
    return dot(high, same, NN) + dot(low, same, NN)


def running_sum(values, reverse):
    rows = values.shape[0]
    row = lax.broadcasted_iota(jnp.int32, (rows, rows), 0)
    column = lax.broadcasted_iota(jnp.int32, (rows, rows), 1)
    ones = ((column >= row) if reverse else (column <= row)).astype(BF16)
    high, low = halves(values)
    return dot(ones, high, NN) + dot(ones, low, NN)


def token_sum(values):
    return jnp.sum(values, axis=0, keepdims=True)


def key_terms(keyed, decay_up, rate_up, vec):
    place = vec[8:9] + decay_up
    log_decay = -jnp.exp(-0.5) * jax.nn.sigmoid(place)
    rate = jax.nn.sigmoid(vec[9:10] + rate_up)
    scaled = keyed * vec[11:12]
    inverse_norm = lax.rsqrt(head_sum(scaled * scaled) + UNIT_EPS)
    unit = scaled * inverse_norm
    key = keyed * (1.0 + (rate - 1.0) * vec[12:13])
    return place, log_decay, rate, inverse_norm, unit, key


def value_terms(valued, residual_up, first, vec):
    residual = jax.nn.sigmoid(vec[10:11] + residual_up)
    return residual, valued + (first - valued) * residual


def decayed(key, unit, rate, log_decay):
    total = running_sum(log_decay, False)
    grown = jnp.exp(total)
    shrunk = jnp.exp(-total)
    before = jnp.exp(total - log_decay)
    alpha = -before * unit
    beta = unit * rate * shrunk
    key_hat = key * shrunk
    return grown, shrunk, before, alpha, beta, key_hat


def solve_lower(lower):
    row = lax.broadcasted_iota(jnp.int32, (HS, PAIR), 0)
    column = lax.broadcasted_iota(jnp.int32, (HS, PAIR), 1) % HS
    eye = (row == column).astype(F32)
    small = (row // SMALL) == (column // SMALL)
    middle = (row // (2 * SMALL)) == (column // (2 * SMALL))
    zero = jnp.zeros_like(lower)
    power = jnp.where(small, lower, zero)
    result = eye + power
    power = dot3(power, stack(power), NN)
    yield
    for last in (False, False, True):
        held = stack(power)
        if last:
            result = result + dot3(result, held, NN)
        else:
            both = dot3(jnp.concatenate([result, power], axis=0), held, NN)
            result = result + both[:HS]
            power = both[HS:]
        yield
    for part in (
        jnp.where(jnp.logical_and(middle, jnp.logical_not(small)), lower, zero),
        jnp.where(middle, zero, lower),
    ):
        inner = dot3(result, stack(part), NN)
        yield
        result = result + dot3(inner, stack(result), NN)
        yield
    return result


def first_unit(
    at,
    keyed_ref, valued_ref, decay_ref, rate_ref, residual_ref, first_ref, vec_ref,
    strict_ref, start_ref, end_ref,
    pay_ref, solved_ref, lower_ref, start_alpha_ref, removed_ref, key_out_ref, value_out_ref,
):
    vec = vec_ref[...]
    strict, start, end = strict_ref[at], start_ref[at], end_ref[at]
    _, log_decay, rate, _, unit, key = key_terms(keyed_ref[at], decay_ref[at], rate_ref[at], vec)
    _, value = value_terms(valued_ref[at], residual_ref[at], first_ref[at].astype(F32), vec)
    key_out_ref[at] = key
    value_out_ref[at] = value
    yield
    grown, _, _, alpha, beta, key_hat = decayed(key, unit, rate, log_decay)
    last = grown[HS - 1 : HS]
    yield
    scores = dot3(alpha, jnp.concatenate([stack(beta), stack(key_hat)], axis=0), NT)
    yield
    lower_ak = scores[:, PAIR:] * strict
    lower_ref[at] = lower_ak
    applied = dot3(lower_ak, stack(value), NN)
    solved = yield from solve_lower(scores[:, :PAIR] * strict)
    solved_ref[at] = solved
    pair = dot3(solved, jnp.concatenate([stack(alpha * start), stack(applied)], axis=1), NN)
    yield
    start_alpha, removed = pair[:, :PAIR], pair[:, PAIR:]
    start_alpha_ref[at] = start_alpha
    removed_ref[at] = removed
    beta_end = beta * (last * end)
    key_end = key_hat * (last * end)
    change = unstack(dot3(start_alpha, beta_end, TN))
    inject = unstack(
        dot3(
            jnp.concatenate([removed, value], axis=0),
            jnp.concatenate([beta_end, key_end], axis=0),
            TN,
        )
    )
    yield
    row = lax.broadcasted_iota(jnp.int32, (HS, PAIR), 0)
    column = lax.broadcasted_iota(jnp.int32, (HS, PAIR), 1) % HS
    mine = first_head(HS)
    change = change + jnp.where(row == column, start[HS - 1 : HS] * last - 1.0, 0.0)
    turned = pltpu.roll(inject, HS, 1)
    pay_ref[at, 0] = jnp.where(mine, change, turned).astype(BF16)
    pay_ref[at, 1] = jnp.where(mine, turned, change).astype(BF16)


def reach_unit(
    at,
    read_ref, keyed_ref, decay_ref, rate_ref, value_ref, start_alpha_ref, removed_ref, vec_ref,
    inclusive_ref, start_ref,
    reach_b_ref, reach_k_ref, reads_ref, out_ref,
):
    vec = vec_ref[...]
    inclusive, start = inclusive_ref[at], start_ref[at]
    _, log_decay, rate, _, unit, key = key_terms(keyed_ref[at], decay_ref[at], rate_ref[at], vec)
    yield
    grown, _, _, _, beta, key_hat = decayed(key, unit, rate, log_decay)
    read_hat = read_ref[at] * grown
    yield
    scores = dot3(read_hat, jnp.concatenate([stack(beta), stack(key_hat)], axis=0), NT)
    yield
    reach_b = scores[:, :PAIR] * inclusive
    reach_k = scores[:, PAIR:] * inclusive
    reach_b_ref[at] = reach_b
    reach_k_ref[at] = reach_k
    pair = dot3(
        reach_b,
        jnp.concatenate([stack(start_alpha_ref[at]), stack(removed_ref[at])], axis=1),
        NN,
    )
    local_out = dot3(reach_k, stack(value_ref[at]), NN)
    yield
    reads_ref[at] = read_hat * start + pair[:, :PAIR]
    out_ref[at] = pair[:, PAIR:] + local_out


def chain_kernel(odd_ref, pay_ref, out_ref):
    shift = odd_ref[0] * HS
    state = jnp.zeros((HS, HS), F32)
    for at in range(pay_ref.shape[0]):
        high, low = halves(state)
        packed = jnp.concatenate([high.astype(F32), low.astype(F32)], axis=1)
        out_ref[at] = pltpu.roll(packed, shift, 1).astype(BF16)
        item = pltpu.roll(pay_ref[at].astype(F32), shift, 1)
        change = item[:, :HS].astype(BF16)
        moved = dot(jnp.concatenate([high, low], axis=0), change, NN)
        state = state + moved[:HS] + moved[HS:] + item[:, HS:]


def chain_back_kernel(odd_ref, pay_ref, grad_ref, out_ref):
    shift = odd_ref[0] * HS
    state = jnp.zeros((HS, HS), F32)
    for at in reversed(range(pay_ref.shape[0])):
        high, low = halves(state)
        packed = jnp.concatenate([high.astype(F32), low.astype(F32)], axis=1)
        out_ref[at] = pltpu.roll(packed, shift, 1).astype(BF16)
        change = pltpu.roll(pay_ref[at].astype(F32), shift, 1)[:, :HS].astype(BF16)
        item = pltpu.roll(grad_ref[at].astype(F32), shift, 1)
        moved = dot(jnp.concatenate([high, low], axis=0), change, NT)
        state = state + moved[:HS] + moved[HS:] + item[:, :HS] + item[:, HS:]


def joined(pay):
    low_first = pay[0].astype(F32)
    low_second = pay[1].astype(F32)
    return jnp.where(
        first_head(HS),
        low_first + pltpu.roll(low_first, HS, 1),
        low_second + pltpu.roll(low_second, HS, 1),
    )


def parted(values):
    high, low = halves(values)
    high, low = high.astype(F32), pltpu.roll(low.astype(F32), HS, 1)
    mine = first_head(HS)
    return jnp.where(mine, high, low).astype(BF16), jnp.where(mine, low, high).astype(BF16)


def output_unit(
    at,
    state_ref, reads_ref, local_ref, read_ref, key_ref, value_ref, gate_ref, vec_ref,
    out_ref, gated_ref,
):
    vec = vec_ref[...]
    state = joined(state_ref[at])
    state_out = local_ref[at] + dot3(reads_ref[at], stack(state), NT)
    yield
    out_ref[at] = state_out
    bonus = head_sum(read_ref[at] * key_ref[at] * vec[13:14])
    center = state_out - head_sum(state_out) * (1.0 / HS)
    yield
    inverse = lax.rsqrt(head_sum(center * center) * (1.0 / HS) + GROUP_EPS)
    yield
    mixed = center * inverse * vec[14:15] + vec[15:16] + bonus * value_ref[at]
    gated_ref[at] = (mixed * gate_ref[at]).astype(BF16)


def add_sums(at, ref, parts):
    place = lax.broadcasted_iota(jnp.int32, (8, PAIR), 0)
    sums = jnp.zeros((8, PAIR), F32)
    for row, part in enumerate(parts):
        sums = sums + jnp.where(place == row, token_sum(part), 0.0)
    if at == 0:
        ref[...] = sums
    else:
        ref[...] += sums


def head_back_unit(
    at,
    grad_ref, out_ref, reads_ref, read_ref, key_ref, value_ref, gate_ref, vec_ref,
    out_grad_ref, gate_grad_ref, read_grad_ref, key_grad_ref, value_grad_ref, pay_ref, vec_grad_ref,
):
    vec = vec_ref[...]
    read, key, value = read_ref[at], key_ref[at], value_ref[at]
    grad = grad_ref[at]
    grad_mixed = grad * gate_ref[at]
    grad_normed = grad_mixed * vec[14:15]
    state_out = out_ref[at]
    bonus = head_sum(read * key * vec[13:14])
    along = head_sum(grad_mixed * value)
    center = state_out - head_sum(state_out) * (1.0 / HS)
    grad_center = grad_normed - head_sum(grad_normed) * (1.0 / HS)
    yield
    inverse = lax.rsqrt(head_sum(center * center) * (1.0 / HS) + GROUP_EPS)
    yield
    normed = center * inverse
    shared = head_sum(grad_normed * normed) * (1.0 / HS)
    yield
    mixed = normed * vec[14:15] + vec[15:16] + bonus * value
    gate_grad_ref[at] = (grad * mixed).astype(BF16)
    value_grad_ref[at] = bonus * grad_mixed
    read_grad_ref[at] = along * key * vec[13:14]
    key_grad_ref[at] = along * read * vec[13:14]
    out_grad = inverse * (grad_center - normed * shared)
    out_grad_ref[at] = out_grad
    pay = dot3(out_grad, reads_ref[at], TN)
    add_sums(at, vec_grad_ref, (along * read * key, grad_mixed * normed, grad_mixed))
    yield
    pay_ref[at, 0], pay_ref[at, 1] = parted(unstack(pay))


def last_unit(
    at,
    read_ref, keyed_ref, valued_ref, decay_ref, rate_ref, residual_ref, first_ref, vec_ref,
    strict_ref, inclusive_ref, start_ref, end_ref,
    solved_ref, lower_ref, reach_b_ref, reach_k_ref, start_alpha_ref, removed_ref,
    state_ref, after_ref, out_grad_ref, read_grad_ref, key_grad_ref, value_grad_ref,
    d_read_ref, d_keyed_ref, d_valued_ref, d_decay_ref, d_rate_ref, d_residual_ref, d_first_ref,
    vec_grad_ref,
):
    vec = vec_ref[...]
    final_row = lax.broadcasted_iota(jnp.int32, (HS, PAIR), 0) == HS - 1
    strict, inclusive = strict_ref[at], inclusive_ref[at]
    start, end = start_ref[at], end_ref[at]
    read, keyed, valued = read_ref[at], keyed_ref[at], valued_ref[at]
    first = first_ref[at].astype(F32)
    out_grad = out_grad_ref[at]
    state = joined(state_ref[at])
    after = joined(after_ref[at])
    spot, log_decay, rate, inverse_norm, unit, key = key_terms(
        keyed, decay_ref[at], rate_ref[at], vec
    )
    residual, value = value_terms(valued, residual_ref[at], first, vec)
    solution_rows = dot3(start_alpha_ref[at], stack(state), NT) + removed_ref[at]
    reached = dot3(jnp.concatenate([reach_b_ref[at], reach_k_ref[at]], axis=1), out_grad, TN)
    yield
    grown, shrunk, before, alpha, beta, key_hat = decayed(key, unit, rate, log_decay)
    read_hat = read * grown
    last = grown[HS - 1 : HS]
    yield
    beta_end = beta * (last * end)
    key_end = key_hat * (last * end)
    carried = dot3(jnp.concatenate([beta_end, key_end], axis=0), stack(after), NT)
    ends = dot3(jnp.concatenate([solution_rows, value], axis=0), stack(after), NN)
    yield
    d_rows = unstack(reached[:PAIR]) + carried[:HS]
    d_value = unstack(reached[PAIR:]) + carried[HS:]
    back = unstack(dot3(solved_ref[at], d_rows, TN))
    yield
    d_value = d_value + unstack(dot3(lower_ref[at], back, TN)) + value_grad_ref[at]
    outer = jnp.concatenate([out_grad, back], axis=0)
    scores = dot3(outer, jnp.concatenate([stack(solution_rows), stack(value)], axis=0), NT)
    entries = dot3(outer, stack(state), NN)
    yield
    mask = jnp.concatenate([inclusive, strict], axis=0)
    scores = scores * jnp.concatenate([mask, mask], axis=1)
    d_beta_end, d_key_end = ends[:HS] * end, ends[HS:] * end
    lefts = dot3(scores, jnp.concatenate([stack(beta), stack(key_hat)], axis=0), NN)
    rights = dot3(scores, jnp.concatenate([read_hat, alpha], axis=0), TN)
    yield
    d_read_hat = entries[:HS] * start + lefts[:HS]
    d_alpha = entries[HS:] * start + lefts[HS:]
    d_beta = unstack(rights[:PAIR]) + d_beta_end * last
    d_key_hat = unstack(rights[PAIR:]) + d_key_end * last
    d_last = token_sum(beta * d_beta_end + key_hat * d_key_end) + start[
        HS - 1 : HS
    ] * token_sum(state * after)
    d_moved = d_beta * shrunk
    d_key = key_grad_ref[at] + d_key_hat * shrunk
    d_read_ref[at] = (read_grad_ref[at] + d_read_hat * grown).astype(BF16)
    along = d_alpha * alpha
    d_total = d_read_hat * read_hat - d_beta * beta - d_key_hat * key_hat + along
    d_total = d_total + jnp.where(final_row, d_last * last, 0.0)
    d_unit = rate * d_moved - before * d_alpha
    d_decay = running_sum(d_total, True) - along
    shared = head_sum(unit * d_unit)
    yield
    d_rate = unit * d_moved + d_key * keyed * vec[12:13]
    d_scaled = (d_unit - unit * shared) * inverse_norm
    d_keyed = d_key * (1.0 + (rate - 1.0) * vec[12:13]) + d_scaled * vec[11:12]
    d_first = d_value * residual
    d_residual = d_first * (first - valued) * (1.0 - residual)
    d_rate_up = d_rate * rate * (1.0 - rate)
    d_decay_up = d_decay * log_decay * jax.nn.sigmoid(-spot)
    d_keyed_ref[at] = d_keyed.astype(BF16)
    d_valued_ref[at] = (d_value * (1.0 - residual)).astype(BF16)
    d_decay_ref[at] = d_decay_up.astype(BF16)
    d_rate_ref[at] = d_rate_up.astype(BF16)
    d_residual_ref[at] = d_residual.astype(BF16)
    d_first_ref[at] = d_first
    add_sums(
        at,
        vec_grad_ref,
        (d_decay_up, d_rate_up, d_residual, d_scaled * keyed, d_key * keyed * (rate - 1.0)),
    )


def head_call(unit, inputs, outputs, flops, pairs):
    count = inputs[0][0].shape[0]
    wide = pairs * PAIR
    kinds = [kind for _, kind in inputs] + [kind for kind, _ in outputs]

    def spec(kind):
        if kind == "tokens":
            return pl.BlockSpec((count, HS, wide), lambda i: (0, 0, i))
        if kind == "rows":
            return pl.BlockSpec((24, wide), lambda i: (0, i))
        if kind == "sums":
            return pl.BlockSpec((8, wide), lambda i: (0, i))
        if kind == "pay":
            return pl.BlockSpec((count, 2 * pairs, HS, PAIR), lambda i: (0, i, 0, 0))
        return pl.BlockSpec((count, HS, PAIR), lambda i: (0, 0, 0))

    shapes = {
        "tokens": (count, HS, EMBED_SIZE),
        "sums": (8, EMBED_SIZE),
        "pay": (count, H, HS, PAIR),
    }

    def view(kind, ref, at):
        if kind == "tokens":
            return ref.at[:, :, pl.ds(at * PAIR, PAIR)]
        if kind in ("rows", "sums"):
            return ref.at[:, pl.ds(at * PAIR, PAIR)]
        if kind == "pay":
            return ref.at[:, pl.ds(2 * at, 2)]
        return ref

    def kernel(*refs):
        running = []
        for pair in range(pairs):
            views = [view(kind, ref, pair) for kind, ref in zip(kinds, refs)]
            running += [unit(at, *views) for at in range(count)]
        done = object()
        while running:
            running = [run for run in running if next(run, done) is not done]

    bytes_moved = sum(4 * a.size for a, _ in inputs) + 4 * sum(
        count * HS * EMBED_SIZE for _ in outputs
    )
    return pl.pallas_call(
        kernel,
        grid=(HEAD_PAIRS // pairs,),
        in_specs=[spec(kind) for _, kind in inputs],
        out_specs=[spec(kind) for kind, _ in outputs],
        out_shape=[jax.ShapeDtypeStruct(shapes[kind], dtype) for kind, dtype in outputs],
        compiler_params=pltpu.CompilerParams(vmem_limit_bytes=HEAD_VMEM),
        cost_estimate=pl.CostEstimate(
            flops=flops, bytes_accessed=bytes_moved, transcendentals=count * HS * EMBED_SIZE * 6
        ),
    )(*[array for array, _ in inputs])


def chain_call(body, odd, *arrays):
    return pl.pallas_call(
        body,
        in_specs=[pl.BlockSpec(memory_space=pltpu.SMEM)]
        + [pl.BlockSpec(memory_space=pltpu.VMEM)] * len(arrays),
        out_specs=pl.BlockSpec(memory_space=pltpu.VMEM),
        out_shape=jax.ShapeDtypeStruct(arrays[0].shape, BF16),
        compiler_params=pltpu.CompilerParams(vmem_limit_bytes=CHAIN_VMEM),
        cost_estimate=pl.CostEstimate(
            flops=32 * 4 * HS**3, bytes_accessed=3 * 1024 * 1024, transcendentals=0
        ),
    )(odd, *arrays)


def project_kernel(*refs):
    weight_ref, norm_ref, before_ref, keep_ref = refs[:4]
    mixes, (read_ref, keyed_ref, valued_ref), ups = refs[4:10], refs[10:13], refs[13:17]
    mids_ref, slopes_ref, vec_ref = refs[17:]
    turned = [
        weight_ref[128 * i : 128 * i + 128, UP_AT + LOW_WIDE - 128 :].astype(F32).T
        for i in range(8)
    ]
    vec = jnp.concatenate(turned, axis=1)[LOW - 256 : LOW - 256 + 24]
    vec_ref[...] = vec
    length = norm_ref.shape[1]
    top = lax.broadcasted_iota(jnp.int32, (length, EMBED_SIZE), 0) == 0
    for at in range(norm_ref.shape[0]):
        normed = norm_ref[at] * vec[0:1] + vec[1:2]
        before = before_ref[at] * vec[0:1] + vec[1:2]
        prior = jnp.where(top, before, pltpu.roll(normed, 1, 0)) * keep_ref[at][:, :1]
        delta = prior - normed
        for index, mix in enumerate(mixes):
            mix[pl.ds(at * length, length)] = (normed + delta * vec[2 + index : 3 + index]).astype(
                BF16
            )
    mix_r, mix_w, mix_k, mix_v, mix_a, mix_g = mixes
    for index, (mix, target) in enumerate(
        ((mix_r, read_ref), (mix_k, keyed_ref), (mix_v, valued_ref))
    ):
        target[...] = dot(
            mix[...], weight_ref[:, index * EMBED_SIZE : (index + 1) * EMBED_SIZE], NN
        )
    down = weight_ref[:, DOWN_AT:UP_AT]
    up = weight_ref[:, UP_AT:]
    lane = lax.broadcasted_iota(jnp.int32, slopes_ref.shape, 1)
    insides = [jnp.logical_and(lane >= EDGES[i], lane < EDGES[i + 1]) for i in range(4)]
    low = jnp.zeros(slopes_ref.shape, F32)
    for inside, mix in zip(insides, (mix_w, mix_a, mix_v, mix_g)):
        low = jnp.where(inside, dot(mix[...], down, NN), low)
    decay, gate = jnp.tanh(low), jax.nn.sigmoid(low)
    mid = jnp.where(insides[0], decay, jnp.where(insides[3], gate, low)).astype(BF16)
    mids_ref[...] = mid
    slopes_ref[...] = jnp.where(
        insides[0], 1.0 - decay * decay, jnp.where(insides[3], gate * (1.0 - gate), 1.0)
    )
    for inside, target in zip(insides, ups):
        target[...] = dot(jnp.where(inside, mid, jnp.zeros_like(mid)), up, NT)


def project(weights, normed, before, keep):
    tokens = normed.shape[0] * normed.shape[1]
    whole = lambda shape: pl.BlockSpec(shape, lambda i: (0,) * len(shape))
    act = (tokens, EMBED_SIZE)
    low = (tokens, LOW_WIDE)
    outs = [(act, BF16)] * 6 + [(act, F32)] * 7 + [(low, BF16), (low, F32)]
    outs += [((24, EMBED_SIZE), F32)]
    inputs = (normed, before, keep)
    return pl.pallas_call(
        project_kernel,
        grid=(1,),
        in_specs=[whole((EMBED_SIZE, OUT_AT))] + [whole(part.shape) for part in inputs],
        out_specs=[whole(shape) for shape, _ in outs],
        out_shape=[jax.ShapeDtypeStruct(shape, kind) for shape, kind in outs],
        compiler_params=pltpu.CompilerParams(vmem_limit_bytes=GRAD_VMEM),
        cost_estimate=pl.CostEstimate(
            flops=2 * tokens * EMBED_SIZE * 5000, bytes_accessed=12_000_000, transcendentals=0
        ),
    )(weights, *inputs)


def turned_into(target, values):
    for at in range(values.shape[1] // 128):
        target(at, values[:, at * 128 : (at + 1) * 128].astype(F32).T.astype(BF16))


def channel_kernel(
    channel_ref, seed_ref, key_ref, val_ref, out_ref, grad_ref, squared_ref, act_ref
):
    seed = seed_ref[...]
    key = key_ref[...].reshape(EMBED_SIZE, -1)
    val = val_ref[...].reshape(-1, EMBED_SIZE)
    hidden = jnp.maximum(dot(channel_ref[...], key, NN), 0.0)
    squared = jnp.square(hidden).astype(BF16)
    d_squared = dot(seed, val, NT)
    act = (2.0 * hidden * d_squared).astype(BF16)
    act_ref[...] = act

    def into(at, part):
        squared_ref[at] = part.reshape(4, ROWS, part.shape[-1])

    turned_into(into, squared)
    out = dot(squared, val, NN)
    grad = dot(act, key, NT)

    @pl.when(pl.program_id(0) == 0)
    def _():
        out_ref[...] = out
        grad_ref[...] = grad

    @pl.when(pl.program_id(0) > 0)
    def _():
        out_ref[...] += out
        grad_ref[...] += grad


def channel_mix(channel, seed, full):
    tokens = channel.shape[0]
    block = 512
    whole = pl.BlockSpec((tokens, EMBED_SIZE), lambda j: (0, 0))
    return pl.pallas_call(
        channel_kernel,
        grid=(FF // block,),
        in_specs=[
            whole,
            whole,
            pl.BlockSpec((32, ROWS, block), lambda j: (0, 4 + j // 2, j % 2)),
            pl.BlockSpec((4, 4 * ROWS, EMBED_SIZE), lambda j: (j, 0, 0)),
        ],
        out_specs=[
            whole,
            whole,
            pl.BlockSpec((4, 4, ROWS, tokens), lambda j: (j, 0, 0, 0)),
            pl.BlockSpec((tokens, block), lambda j: (0, j)),
        ],
        out_shape=[
            jax.ShapeDtypeStruct((tokens, EMBED_SIZE), F32),
            jax.ShapeDtypeStruct((tokens, EMBED_SIZE), F32),
            jax.ShapeDtypeStruct((32, 4, ROWS, tokens), BF16),
            jax.ShapeDtypeStruct((tokens, FF), BF16),
        ],
        compiler_params=pltpu.CompilerParams(vmem_limit_bytes=GRAD_VMEM),
        cost_estimate=pl.CostEstimate(
            flops=8 * tokens * FF * EMBED_SIZE, bytes_accessed=20_000_000, transcendentals=0
        ),
    )(channel, seed, full, full)


def channel_grad_kernel(squared_ref, seed_ref, channel_ref, act_ref, out_ref, features):
    step = pl.program_id(0)

    def into_features(at, part):
        features[at] = part

    @pl.when(step == 4)
    def _():
        turned_into(into_features, channel_ref)

    def write(left_of, right):
        for group in range(8):
            out_ref[pl.ds(group * 4, 4)] = (
                dot(left_of(group), right, NN).astype(BF16).reshape(4, ROWS, EMBED_SIZE)
            )

    @pl.when(step < 4)
    def _():
        left_of = lambda group: squared_ref[pl.ds(group * 4, 4), 0].reshape(128, -1)
        write(left_of, seed_ref[...])

    @pl.when(step >= 4)
    def _():
        write(lambda group: features[group], act_ref[...])


def channel_grads(squared, seed, channel, act):
    tokens = seed.shape[0]
    whole = pl.BlockSpec((tokens, EMBED_SIZE), lambda j: (0, 0))
    return pl.pallas_call(
        channel_grad_kernel,
        grid=(8,),
        in_specs=[
            pl.BlockSpec((32, 1, ROWS, tokens), lambda j: (0, jnp.minimum(j, 3), 0, 0)),
            whole,
            whole,
            pl.BlockSpec((tokens, EMBED_SIZE), lambda j: (0, jnp.maximum(j - 4, 0))),
        ],
        out_specs=pl.BlockSpec((32, ROWS, EMBED_SIZE), lambda j: (0, j, 0)),
        out_shape=jax.ShapeDtypeStruct((32, 8 * ROWS, EMBED_SIZE), BF16),
        scratch_shapes=[pltpu.VMEM((8, 128, tokens), BF16)],
        compiler_params=pltpu.CompilerParams(vmem_limit_bytes=GRAD_VMEM),
        cost_estimate=pl.CostEstimate(
            flops=2 * tokens * 8 * EMBED_SIZE**2, bytes_accessed=20_000_000, transcendentals=0
        ),
    )(squared, seed, channel, act)


def turn_kernel(*refs):
    for slot, ref in enumerate(refs[:-1]):

        def into(at, part):
            refs[-1][slot, at * 2 : at * 2 + 2] = part.reshape(2, 2, ROWS, part.shape[-1])

        turned_into(into, ref)


def turned_by_owner(parts):
    tokens = parts[0].shape[0]
    shape = (len(parts), 16, 2, ROWS, tokens)
    return pl.pallas_call(
        turn_kernel,
        grid=(1,),
        in_specs=[pl.BlockSpec(part.shape, lambda i: (0, 0)) for part in parts],
        out_specs=pl.BlockSpec(shape, lambda i: (0, 0, 0, 0, 0)),
        out_shape=jax.ShapeDtypeStruct(shape, BF16),
        compiler_params=pltpu.CompilerParams(vmem_limit_bytes=GRAD_VMEM),
        cost_estimate=pl.CostEstimate(flops=0, bytes_accessed=4_000_000, transcendentals=0),
    )(*parts)


def time_grad_kernel(
    core_ref, inputs_ref, d_read, d_keyed, d_valued, d_att, d_decay, d_rate, d_residual, d_gate,
    up_ref, slopes_ref, mids_ref, low_ref, mine_ref, theirs_ref, turned,
):
    d_ups = (d_decay, d_rate, d_residual, d_gate)
    lane = lax.broadcasted_iota(jnp.int32, slopes_ref.shape, 1)
    insides = [jnp.logical_and(lane >= EDGES[i], lane < EDGES[i + 1]) for i in range(4)]
    up = up_ref[...]
    d_low = jnp.zeros(slopes_ref.shape, F32)
    for inside, d_up in zip(insides, d_ups):
        d_low = jnp.where(inside, dot(d_up[...], up, NN), d_low)
    d_low = (d_low * slopes_ref[...]).astype(BF16)
    low_ref[...] = d_low
    for slot, d_up in enumerate(d_ups):

        def into(at, part):
            turned[slot, at * 2 : at * 2 + 2] = part.reshape(2, 2, ROWS, part.shape[-1])

        turned_into(into, d_up)
    none = jnp.zeros(d_low.shape, BF16)

    def in_two(values):
        parts = [jnp.where(inside, values, none) for inside in insides]
        return (
            jnp.concatenate([part[:, :128] for part in parts[:2]], axis=0),
            jnp.concatenate([part[:, 128:] for part in parts[2:]], axis=0),
        )

    low_parts, mid_parts = in_two(d_low), in_two(mids_ref[...])
    block = 2 * ROWS

    def write(first, second):
        for z in range(4):
            chips = pl.ds(4 * z, 4)
            rows = pl.ds(4 * block * z, 4 * block)

            def left(slot):
                return inputs_ref[slot, chips].reshape(4 * block, -1)

            def left_up(slot):
                return turned[slot, chips].reshape(4 * block, -1)

            def low_grads(parts, slots, get):
                pairs = [jnp.concatenate([get(i) for i in pair], axis=1) for pair in slots]
                return jnp.concatenate(
                    [dot(pair, part, NN).astype(BF16) for pair, part in zip(pairs, parts)], axis=1
                )

            by_read = dot(left(0), d_read[...], NN).astype(BF16)
            by_key = dot(left(2), d_keyed[...], NN).astype(BF16)
            down = low_grads(low_parts, ((1, 4), (3, 5)), left)
            for x in range(4):
                at = pl.ds((x * 4 + z) * block, block)
                part = slice(x * block, (x + 1) * block)
                first[at, :EMBED_SIZE] = by_read[part]
                first[at, EMBED_SIZE : 2 * EMBED_SIZE] = by_key[part]
                first[at, 2 * EMBED_SIZE :] = down[part]
            second[rows, :EMBED_SIZE] = dot(left(3), d_valued[...], NN).astype(BF16)
            second[rows, EMBED_SIZE : 2 * EMBED_SIZE] = dot(left(6), d_att[...], NN).astype(BF16)
            second[rows, 2 * EMBED_SIZE :] = low_grads(mid_parts, ((0, 1), (2, 3)), left_up)

    @pl.when(core_ref[0] == 0)
    def _():
        write(mine_ref, theirs_ref)

    @pl.when(core_ref[0] == 1)
    def _():
        write(theirs_ref, mine_ref)


def time_grads(core, inputs, d_time, d_ups, weights, slopes, mids):
    tokens, wide = slopes.shape
    whole = lambda part: pl.BlockSpec(part.shape, lambda i: (0,) * part.ndim)
    shapes = [(tokens, wide), (EMBED_SIZE, HALF), (EMBED_SIZE, HALF)]
    return pl.pallas_call(
        time_grad_kernel,
        grid=(1,),
        in_specs=[pl.BlockSpec(memory_space=pltpu.SMEM)]
        + [whole(part) for part in (inputs, *d_time, *d_ups)]
        + [pl.BlockSpec((EMBED_SIZE, wide), lambda i: (0, UP_AT // wide))]
        + [whole(slopes), whole(mids)],
        out_specs=[pl.BlockSpec(shape, lambda i: (0, 0)) for shape in shapes],
        out_shape=[jax.ShapeDtypeStruct(shape, BF16) for shape in shapes],
        scratch_shapes=[pltpu.VMEM((4, 16, 2, ROWS, tokens), BF16)],
        compiler_params=pltpu.CompilerParams(vmem_limit_bytes=GRAD_VMEM),
        cost_estimate=pl.CostEstimate(
            flops=2 * tokens * EMBED_SIZE * 4 * HALF, bytes_accessed=12_000_000, transcendentals=0
        ),
    )(core, inputs, *d_time, *d_ups, weights, slopes, mids)


def moved(values, first=0, second=0, core=0):
    pairs = []
    for at in range(32):
        z, x, mine = at // 8, at // 2 % 4, at % 2
        if mine == 0:
            z, x = (z + second) % 4, (x + first) % 4
        else:
            z, x = (z + first) % 4, (x + second) % 4
        pairs.append((at, z * 8 + x * 2 + (mine + core) % 2))
    return lax.ppermute(values, "shard", pairs)


def ring_place():
    place = lax.axis_index("shard")
    z, x, core = place // 8, place // 2 % 4, place % 2
    return jnp.where(core == 0, x, z), jnp.where(core == 0, z, x), core


def picked(values, at):
    return lax.dynamic_index_in_dim(values, at % values.shape[0], 0, keepdims=False)


def around_ring(chunk, send):
    total = chunk(0).astype(F32)
    for step in (1, 3, 2):
        total = total + send(chunk(step), step).astype(F32)
    return total


def to_group(part, by):
    return lax.ppermute(part, "rep", [(i, (i + by) % 4) for i in range(4)])


def quarter_over_groups(values):
    place = lax.axis_index("rep")
    quarters = values.astype(BF16).reshape(4, -1, values.shape[1])
    return around_ring(lambda k: picked(quarters, place + k), to_group).astype(BF16)


def from_quarters(mine):
    place = lax.axis_index("rep")
    parts = jnp.stack([mine] + [to_group(mine, step) for step in (1, 2, 3)])
    ordered = [
        lax.dynamic_index_in_dim(parts, (place - k) % 4, 0, keepdims=False) for k in range(4)
    ]
    return jnp.concatenate(ordered, axis=0).astype(F32)


def passed_along(rows, by):
    size = lax.axis_size("shard")
    pairs = [(i, i + by) for i in range(size) if 0 <= i + by < size]
    return lax.ppermute(rows, "shard", pairs)


def product(left, right):
    return jnp.dot(left, right, preferred_element_type=F32)


def product_tn(left, right):
    return lax.dot_general(left, right, (((0,), (0,)), ((), ())), preferred_element_type=F32)


def product_nt(left, right):
    return lax.dot_general(left, right, (((1,), (1,)), ((), ())), preferred_element_type=F32)


def layer_norm(values, gain, bias):
    center = values - jnp.mean(values, axis=-1, keepdims=True)
    spread = jnp.mean(center * center, axis=-1, keepdims=True)
    return center * lax.rsqrt(spread + NORM_EPS) * gain + bias


def norm_piece(values, vec, row):
    return layer_norm(values, vec[row], vec[row + 1])


def mix_piece(values, before, vec, keep, first_row, count):
    prior = jnp.concatenate([before[:, None], values[:, :-1]], axis=1) * keep[:, :, None]
    delta = prior - values
    return tuple(values + delta * vec[first_row + index] for index in range(count))


def flat(values):
    return values.reshape(-1, values.shape[-1])


def gathered(shard):
    return lax.all_gather(shard, "shard", axis=0, tiled=True)


def scattered(full):
    return lax.psum_scatter(full, "shard", scatter_dimension=0, tiled=True)


def exchanged(pay):
    return lax.all_to_all(pay.reshape((-1,) + pay.shape[-2:]), "shard", 0, 0, tiled=False)


def local(
    layer_input,
    first_layer_values,
    segments,
    receptance_key_value_weight,
    time_output_weight,
    low_rank_down,
    low_rank_up,
    channel_key_weight,
    channel_value_weight,
    vectors,
    output_gradient,
):
    count, length, width = layer_input.shape
    rows = vectors.shape[1]
    spot_first, spot_second, spot_core = ring_place()
    filler = lambda used: jnp.zeros((rows, LOW_WIDE - used), BF16)
    weights = gathered(
        jnp.concatenate(
            [
                receptance_key_value_weight,
                low_rank_down,
                filler(LOW),
                low_rank_up.T,
                vectors.T,
                filler(LOW + vectors.shape[0]),
                time_output_weight,
            ],
            axis=1,
        )
    )
    rest = lax.all_gather(
        jnp.concatenate(
            [channel_value_weight] + jnp.split(channel_key_weight, 4, axis=1), axis=0
        ),
        "shard",
    )
    full_out = weights[:, OUT_AT:]

    edge = passed_along(segments[:, -1] + 1, 1) - 1
    keep = jnp.concatenate(
        [segments[:, :1] == edge[:, None], segments[:, 1:] == segments[:, :-1]], axis=1
    ).astype(F32)
    same = (segments[:, :, None] == segments[:, None, :]).astype(F32)
    later = lax.broadcasted_iota(jnp.int32, (length, length), 0)
    earlier = lax.broadcasted_iota(jnp.int32, (length, length), 1)
    strict = jnp.tile(same * (later > earlier).astype(F32), (1, 1, 2))
    inclusive = jnp.tile(same * (later >= earlier).astype(F32), (1, 1, 2))
    start = jnp.broadcast_to(
        (segments == edge[:, None]).astype(F32)[:, :, None], (count, length, PAIR)
    )
    end = jnp.broadcast_to(same[:, -1, :, None], (count, length, PAIR))
    masks = [(strict, "masks"), (inclusive, "masks"), (start, "masks"), (end, "masks")]
    odd = (lax.axis_index("shard") % 2).astype(jnp.int32).reshape(1)

    hidden = layer_input.astype(F32)
    raw_before = passed_along(layer_input[:, -1], 1).astype(F32)
    plain = lambda values: layer_norm(values, 1.0, 0.0)
    plain_before = plain(raw_before)[:, None]
    x_r, x_w, x_k, x_v, x_a, x_g, read, keyed, valued, *more = project(
        weights, plain(hidden), plain_before,
        jnp.broadcast_to(keep[:, :, None], (count, length, PAIR)),
    )
    decay_up, rate_up, residual_up, gate, mids, slopes, vec = more
    normed1, pull_norm1 = jax.vjp(partial(norm_piece, row=0), hidden, vec)
    before1 = plain_before[:, 0] * vec[0] + vec[1]
    _, pull_mix1 = jax.vjp(
        partial(mix_piece, keep=keep, first_row=2, count=6), normed1, before1, vec
    )
    downs = [weights[:, DOWN_AT + EDGES[i] : DOWN_AT + EDGES[i + 1]] for i in range(4)]
    shape = (count, length, width)
    read, keyed, valued, decay_up, rate_up, residual_up, gate = [
        part.reshape(shape) for part in (read, keyed, valued, decay_up, rate_up, residual_up, gate)
    ]
    vec_row, start_mask = (vec, "rows"), (start, "masks")
    pay, solved, lower, start_alpha, removed, key, value = head_call(
        first_unit,
        [
            (part, "tokens")
            for part in (keyed, valued, decay_up, rate_up, residual_up, first_layer_values)
        ]
        + [vec_row, (strict, "masks"), start_mask, (end, "masks")],
        [("pay", BF16)] + [("tokens", F32)] * 6,
        2_000_000_000,
        4,
    )
    chain_items = exchanged(pay)
    reach_b, reach_k, reads, local_out = head_call(
        reach_unit,
        [
            (part, "tokens")
            for part in (read, keyed, decay_up, rate_up, value, start_alpha, removed)
        ]
        + [vec_row, (inclusive, "masks"), start_mask],
        [("tokens", F32)] * 4,
        1_000_000_000,
        4,
    )
    states = exchanged(chain_call(chain_kernel, odd, chain_items)).reshape(pay.shape)
    tokens = [
        (part, "tokens")
        for part in (read, keyed, valued, decay_up, rate_up, residual_up, first_layer_values)
    ]
    gate_terms = [
        (read, "tokens"), (key, "tokens"), (value, "tokens"), (gate, "tokens"), (vec, "rows")
    ]
    state_out, gated = head_call(
        output_unit,
        [(states, "pay"), (reads, "tokens"), (local_out, "tokens")] + gate_terms,
        [("tokens", F32), ("tokens", BF16)],
        300_000_000,
        4,
    )
    gated = flat(gated)
    mixed_h = hidden + product(gated, full_out).reshape(shape)

    normed2, pull_norm2 = jax.vjp(partial(norm_piece, row=16), mixed_h, vec)
    before2 = passed_along(normed2[:, -1], 1)
    channel, pull_mix2 = jax.vjp(
        partial(mix_piece, keep=keep, first_row=18, count=1), normed2, before2, vec
    )
    channel_low = flat(channel[0].astype(BF16))
    seed = flat(output_gradient)
    channel_out, grad_channel, squared, grad_act = channel_mix(
        channel_low, seed, rest
    )
    channel_part = channel_grads(squared, seed, channel_low, grad_act)
    grad_channel, channel_part = lax.optimization_barrier((grad_channel, channel_part))
    own_channel = scattered(channel_part)[0]
    turned = turned_by_owner((x_r, x_w, x_k, x_v, x_a, x_g, gated))
    hidden_out = (mixed_h + channel_out.reshape(shape)).astype(BF16)
    grad_channel = grad_channel.reshape(shape)
    grad_norm2, grad_before2, vec_grad_a = pull_mix2((grad_channel,))
    grad_norm2 = grad_norm2.at[:, -1].add(passed_along(grad_before2, -1))
    grad_mixed, vec_grad_b = pull_norm2(grad_norm2)
    grad_mixed = grad_mixed + output_gradient.astype(F32)
    grad_att = flat(grad_mixed.astype(BF16))
    grad_gated = product_nt(grad_att, full_out).reshape(shape)

    out_grad, gate_grad, read_grad, key_grad, value_grad, grad_pay, vec_sums_a = head_call(
        head_back_unit,
        [(grad_gated, "tokens"), (state_out, "tokens"), (reads, "tokens")] + gate_terms,
        [("tokens", F32), ("tokens", BF16)]
        + [("tokens", F32)] * 3
        + [("pay", BF16), ("sums", F32)],
        300_000_000,
        4,
    )
    after = exchanged(
        chain_call(chain_back_kernel, odd, chain_items, exchanged(grad_pay))
    ).reshape(pay.shape)
    d_read, d_keyed, d_valued, d_decay, d_rate, d_residual, first_grad, vec_sums_b = head_call(
        last_unit,
        tokens
        + [(vec, "rows")]
        + masks
        + [
            (part, "tokens")
            for part in (solved, lower, reach_b, reach_k, start_alpha, removed)
        ]
        + [(states, "pay"), (after, "pay")]
        + [(part, "tokens") for part in (out_grad, read_grad, key_grad, value_grad)],
        [("tokens", BF16)] * 6 + [("tokens", F32), ("sums", F32)],
        3_000_000_000,
        2,
    )
    d_time = [flat(d_read), flat(d_keyed), flat(d_valued)]
    d_ups = [flat(part) for part in (d_decay, d_rate, d_residual, gate_grad)]
    d_low, mine, theirs = time_grads(odd, turned, [*d_time, grad_att], d_ups, weights, slopes, mids)
    barrier = lax.optimization_barrier

    arrived = moved(theirs, core=1)
    d_read, d_keyed, d_valued = d_time
    d_lows = [d_low[:, EDGES[i] : EDGES[i + 1]] for i in range(4)]
    back = [product_nt(low, weight) for low, weight in zip(d_lows, downs)]
    d_x_r, d_x_k, d_x_v = [
        product_nt(part, weights[:, i * EMBED_SIZE : (i + 1) * EMBED_SIZE])
        for i, part in enumerate((d_read, d_keyed, d_valued))
    ]
    d_x_v = d_x_v + back[2]
    d_mixes = (d_x_r, back[0], d_x_k, d_x_v, back[1], back[3])
    arrived, d_mixes = barrier((arrived, d_mixes))

    whole = (mine.astype(F32) + arrived.astype(F32)).astype(BF16).reshape(4, 4, 2, ROWS, HALF)
    chunk = lambda k: picked(whole, spot_first + k)
    far = chunk(2)
    from_behind = moved(far[:2], first=1)
    from_ahead = moved(far[2:], first=-1)
    grad_norm1, grad_before1, vec_grad_c = pull_mix1(
        tuple(part.reshape(shape) for part in d_mixes)
    )
    from_next = passed_along(grad_before1, -1)
    from_behind, from_ahead, grad_norm1, from_next, vec_grad_c = barrier(
        (from_behind, from_ahead, grad_norm1, from_next, vec_grad_c)
    )

    ahead, behind = chunk(1).astype(F32), chunk(3).astype(F32)
    ahead = jnp.concatenate([ahead[:2] + from_behind.astype(F32), ahead[2:]], axis=0)
    behind = jnp.concatenate([behind[:2], behind[2:] + from_ahead.astype(F32)], axis=0)
    from_behind = moved(ahead.astype(BF16), first=1)
    from_ahead = moved(behind.astype(BF16), first=-1)
    grad_norm1 = grad_norm1.at[:, -1].add(from_next)
    grad_hidden, vec_grad_d = pull_norm1(grad_norm1)
    hidden_grad = grad_mixed + grad_hidden
    vec_grad = vec_grad_a + vec_grad_b + vec_grad_c + vec_grad_d
    vec_grad = vec_grad + jnp.concatenate(
        [
            jnp.zeros((8, width), F32),
            vec_sums_b[:5],
            vec_sums_a[:3],
            jnp.zeros((vec.shape[0] - 16, width), F32),
        ],
        axis=0,
    )
    vec_parts = vec_grad.reshape(-1, 32, 32).transpose(1, 0, 2).reshape(32, 6, 128)
    own_vec = jnp.sum(exchanged(vec_parts), axis=0).reshape(-1, rows).T
    from_behind, from_ahead, own_vec, own_channel = barrier(
        (from_behind, from_ahead, own_vec, own_channel)
    )

    summed = (chunk(0).astype(F32) + from_behind.astype(F32) + from_ahead.astype(F32)).astype(BF16)
    summed = around_ring(
        lambda k: picked(summed, spot_second + k), lambda part, by: moved(part, second=by)
    ).astype(BF16)
    own_half = picked(summed, spot_core)
    other_half = moved(picked(summed, 1 - spot_core), core=1)
    own_channel = quarter_over_groups(own_channel)
    own_half, other_half, own_channel = barrier((own_half, other_half, own_channel))
    is_first = spot_core == 0
    own = jnp.concatenate(
        [
            jnp.where(is_first, own_half, other_half).astype(F32),
            jnp.where(is_first, other_half, own_half).astype(F32),
            own_vec,
            jnp.zeros((rows, 128 - vec.shape[0]), F32),
        ],
        axis=1,
    )
    own = quarter_over_groups(own)
    own_channel = from_quarters(own_channel)
    own, own_channel = barrier((own, own_channel))
    own = from_quarters(own)
    own_key = jnp.concatenate([own_channel[128 + 32 * k : 160 + 32 * k] for k in range(4)], axis=1)
    down_at = 2 * EMBED_SIZE
    value_at, out_at, up_at, vec_at = HALF, HALF + EMBED_SIZE, HALF + 2 * EMBED_SIZE, 2 * HALF
    return (
        hidden_out,
        hidden_grad,
        first_grad,
        jnp.concatenate([own[:, :down_at], own[:, value_at:out_at]], axis=1),
        own[:, out_at:up_at],
        own[:, down_at : down_at + LOW],
        own[:, up_at : up_at + LOW].T,
        own_key,
        own_channel[:128],
        own[:, vec_at : vec_at + vectors.shape[0]].T,
    )


def solution(mesh):
    tokens = P("rep", "shard", None)
    rows = P("shard", None)
    columns = P(None, "shard")
    return jax.shard_map(
        local,
        mesh=mesh,
        in_specs=(
            tokens, tokens, P("rep", "shard"), rows, rows, rows, columns, rows, rows, columns, tokens
        ),
        out_specs=(tokens, tokens, tokens, rows, rows, rows, columns, rows, rows, columns),
        check_vma=False,
    )
```

```python
from functools import partial

import jax
import jax.numpy as jnp
from jax import lax
from jax.experimental import pallas as pl
from jax.experimental.pallas import tpu as pltpu
from jax.sharding import PartitionSpec as P

EMBED_SIZE = 1024
H = 16
HS = 64
FF = 4096
DECAY_RANK = 64
LA = 64
LV = 32
LOW = 320
PAIR = 2 * HS
HEAD_PAIRS = H // 2
SMALL = 16

NORM_EPS = 1e-05
GROUP_EPS = 0.00064
UNIT_EPS = 1e-06
F32 = jnp.float32
BF16 = jnp.bfloat16
HEAD_VMEM = 60 * 1024 * 1024
CHAIN_VMEM = 60 * 1024 * 1024
GRAD_VMEM = 60 * 1024 * 1024
ROWS = 32
LOW_WIDE = 384
DOWN_AT = 3 * EMBED_SIZE
UP_AT = DOWN_AT + LOW_WIDE
OUT_AT = UP_AT + LOW_WIDE
HALF = 2 * EMBED_SIZE + LOW_WIDE
EDGES = (0, DECAY_RANK, DECAY_RANK + LA, DECAY_RANK + LA + LV, LOW)


def dot(left, right, dims):
    return lax.dot_general(left, right, (dims, ((), ())), preferred_element_type=F32)


def halves(values):
    high = values.astype(BF16)
    return high, (values - high.astype(F32)).astype(BF16)


def dot3(left, right, dims):
    left_high, left_low = halves(left)
    right_high, right_low = halves(right)
    return (
        dot(left_high, right_high, dims)
        + dot(left_high, right_low, dims)
        + dot(left_low, right_high, dims)
    )


def dot1(left, right, dims):
    return dot(left.astype(BF16), right.astype(BF16), dims)


NN = ((1,), (0,))
NT = ((1,), (1,))
TN = ((0,), (0,))


def first_head(rows):
    return lax.broadcasted_iota(jnp.int32, (rows, PAIR), 1) < HS


def stack(folded):
    mine = first_head(folded.shape[0])
    zero = jnp.zeros_like(folded)
    return jnp.concatenate([jnp.where(mine, folded, zero), jnp.where(mine, zero, folded)], axis=0)


def unstack(full):
    return jnp.where(first_head(HS), full[:HS], full[HS:])


def head_sum(values):
    row = lax.broadcasted_iota(jnp.int32, (PAIR, PAIR), 0) // HS
    column = lax.broadcasted_iota(jnp.int32, (PAIR, PAIR), 1) // HS
    same = (row == column).astype(BF16)
    high, low = halves(values)
    return dot(high, same, NN) + dot(low, same, NN)


def running_sum(values, reverse):
    rows = values.shape[0]
    row = lax.broadcasted_iota(jnp.int32, (rows, rows), 0)
    column = lax.broadcasted_iota(jnp.int32, (rows, rows), 1)
    ones = ((column >= row) if reverse else (column <= row)).astype(BF16)
    high, low = halves(values)
    return dot(ones, high, NN) + dot(ones, low, NN)


def token_sum(values):
    return jnp.sum(values, axis=0, keepdims=True)


def key_terms(keyed, decay_up, rate_up, vec):
    place = vec[8:9] + decay_up
    log_decay = -jnp.exp(-0.5) * jax.nn.sigmoid(place)
    rate = jax.nn.sigmoid(vec[9:10] + rate_up)
    scaled = keyed * vec[11:12]
    inverse_norm = lax.rsqrt(head_sum(scaled * scaled) + UNIT_EPS)
    unit = scaled * inverse_norm
    key = keyed * (1.0 + (rate - 1.0) * vec[12:13])
    return place, log_decay, rate, inverse_norm, unit, key


def value_terms(valued, residual_up, first, vec):
    residual = jax.nn.sigmoid(vec[10:11] + residual_up)
    return residual, valued + (first - valued) * residual


def decayed(key, unit, rate, log_decay):
    total = running_sum(log_decay, False)
    grown = jnp.exp(total)
    shrunk = jnp.exp(-total)
    before = jnp.exp(total - log_decay)
    alpha = -before * unit
    beta = unit * rate * shrunk
    key_hat = key * shrunk
    return grown, shrunk, before, alpha, beta, key_hat


def solve_lower(lower):
    row = lax.broadcasted_iota(jnp.int32, (HS, PAIR), 0)
    column = lax.broadcasted_iota(jnp.int32, (HS, PAIR), 1) % HS
    eye = (row == column).astype(F32)
    small = (row // SMALL) == (column // SMALL)
    middle = (row // (2 * SMALL)) == (column // (2 * SMALL))
    zero = jnp.zeros_like(lower)
    power = jnp.where(small, lower, zero)
    result = eye + power
    power = dot3(power, stack(power), NN)
    yield
    for last in (False, False, True):
        held = stack(power)
        if last:
            result = result + dot3(result, held, NN)
        else:
            both = dot3(jnp.concatenate([result, power], axis=0), held, NN)
            result = result + both[:HS]
            power = both[HS:]
        yield
    for part in (
        jnp.where(jnp.logical_and(middle, jnp.logical_not(small)), lower, zero),
        jnp.where(middle, zero, lower),
    ):
        inner = dot3(result, stack(part), NN)
        yield
        result = result + dot3(inner, stack(result), NN)
        yield
    return result


def first_unit(
    at,
    keyed_ref, valued_ref, decay_ref, rate_ref, residual_ref, first_ref, vec_ref,
    strict_ref, start_ref, end_ref,
    pay_ref, solved_ref, lower_ref, start_alpha_ref, removed_ref, key_out_ref, value_out_ref,
):
    vec = vec_ref[...]
    strict, start, end = strict_ref[at], start_ref[at], end_ref[at]
    _, log_decay, rate, _, unit, key = key_terms(keyed_ref[at], decay_ref[at], rate_ref[at], vec)
    _, value = value_terms(valued_ref[at], residual_ref[at], first_ref[at].astype(F32), vec)
    key_out_ref[at] = key
    value_out_ref[at] = value
    yield
    grown, _, _, alpha, beta, key_hat = decayed(key, unit, rate, log_decay)
    last = grown[HS - 1 : HS]
    yield
    scores = dot3(alpha, jnp.concatenate([stack(beta), stack(key_hat)], axis=0), NT)
    yield
    lower_ak = scores[:, PAIR:] * strict
    lower_ref[at] = lower_ak
    applied = dot3(lower_ak, stack(value), NN)
    solved = yield from solve_lower(scores[:, :PAIR] * strict)
    solved_ref[at] = solved
    pair = dot3(solved, jnp.concatenate([stack(alpha * start), stack(applied)], axis=1), NN)
    yield
    start_alpha, removed = pair[:, :PAIR], pair[:, PAIR:]
    start_alpha_ref[at] = start_alpha
    removed_ref[at] = removed
    beta_end = beta * (last * end)
    key_end = key_hat * (last * end)
    change = unstack(dot3(start_alpha, beta_end, TN))
    inject = unstack(
        dot3(
            jnp.concatenate([removed, value], axis=0),
            jnp.concatenate([beta_end, key_end], axis=0),
            TN,
        )
    )
    yield
    row = lax.broadcasted_iota(jnp.int32, (HS, PAIR), 0)
    column = lax.broadcasted_iota(jnp.int32, (HS, PAIR), 1) % HS
    mine = first_head(HS)
    change = change + jnp.where(row == column, start[HS - 1 : HS] * last - 1.0, 0.0)
    turned = pltpu.roll(inject, HS, 1)
    pay_ref[at, 0] = jnp.where(mine, change, turned).astype(BF16)
    pay_ref[at, 1] = jnp.where(mine, turned, change).astype(BF16)


def reach_unit(
    at,
    read_ref, keyed_ref, decay_ref, rate_ref, value_ref, start_alpha_ref, removed_ref, vec_ref,
    inclusive_ref, start_ref,
    reach_b_ref, reach_k_ref, reads_ref, out_ref,
):
    vec = vec_ref[...]
    inclusive, start = inclusive_ref[at], start_ref[at]
    _, log_decay, rate, _, unit, key = key_terms(keyed_ref[at], decay_ref[at], rate_ref[at], vec)
    yield
    grown, _, _, _, beta, key_hat = decayed(key, unit, rate, log_decay)
    read_hat = read_ref[at] * grown
    yield
    scores = dot3(read_hat, jnp.concatenate([stack(beta), stack(key_hat)], axis=0), NT)
    yield
    reach_b = scores[:, :PAIR] * inclusive
    reach_k = scores[:, PAIR:] * inclusive
    reach_b_ref[at] = reach_b
    reach_k_ref[at] = reach_k
    pair = dot3(
        reach_b,
        jnp.concatenate([stack(start_alpha_ref[at]), stack(removed_ref[at])], axis=1),
        NN,
    )
    local_out = dot3(reach_k, stack(value_ref[at]), NN)
    yield
    reads_ref[at] = read_hat * start + pair[:, :PAIR]
    out_ref[at] = pair[:, PAIR:] + local_out


def chain(steps, form, change_of, item_of, write):
    stretches = [steps[i : i + len(steps) // 4] for i in range(0, len(steps), len(steps) // 4)]
    row = lax.broadcasted_iota(jnp.int32, (HS, HS), 0)
    eye = (row == lax.broadcasted_iota(jnp.int32, (HS, HS), 1)).astype(F32)
    none = jnp.zeros((HS, HS), F32)
    product_of = [eye for _ in stretches]
    total_of = [none for _ in stretches]
    before = {}
    for turn in range(len(stretches[0])):
        for at, stretch in enumerate(stretches):
            step = stretch[turn]
            before[step] = product_of[at], total_of[at]
            parts = jnp.concatenate([side_by_side(product_of[at]), side_by_side(total_of[at])], 0)
            change = change_of(step)
            gone = dot(parts, jnp.concatenate([change, change], axis=form[1][0]), form)
            product_of[at] = product_of[at] + gone[:HS]
            total_of[at] = total_of[at] + gone[HS:] + item_of(step)

    def through(state, product):
        high, low = halves(product)
        wide = side_by_side(state)
        twice = jnp.concatenate([high, high], axis=0)
        once = jnp.concatenate([low, jnp.zeros_like(low)], axis=0)
        return dot(wide, twice, NN) + dot(wide, once, NN)

    state = none
    for at, stretch in enumerate(stretches):
        for step in stretch:
            if at == 0:
                write(step, before[step][1])
            else:
                write(step, through(state, before[step][0]) + before[step][1])
        if at == 0:
            state = total_of[at]
        else:
            state = through(state, product_of[at]) + total_of[at]


def side_by_side(values):
    return jnp.concatenate(halves(values), axis=1)


def wide_rows(values):
    return jnp.concatenate([values[: HS // 2], values[HS // 2 :]], axis=1).astype(BF16)


def chain_kernel(odd_ref, pay_ref, out_ref):
    shift = odd_ref[0] * HS
    items = [pltpu.roll(pay_ref[at].astype(F32), shift, 1) for at in range(pay_ref.shape[0])]

    def write(step, state):
        out_ref[step] = wide_rows(state)

    chain(
        list(range(len(items))),
        NN,
        lambda step: items[step][:, :HS].astype(BF16),
        lambda step: items[step][:, HS:],
        write,
    )


def chain_back_kernel(odd_ref, pay_ref, grad_ref, out_ref):
    shift = odd_ref[0] * HS

    def change_of(step):
        return pltpu.roll(pay_ref[step].astype(F32), shift, 1)[:, :HS].astype(BF16)

    def item_of(step):
        item = grad_ref[step].astype(F32)
        return jnp.concatenate([item[:, :HS], item[:, HS:]], axis=0)

    def write(step, state):
        out_ref[step] = wide_rows(state)

    chain(list(reversed(range(pay_ref.shape[0]))), NT, change_of, item_of, write)


def joined(pay):
    first, second = pay[0].astype(F32), pay[1].astype(F32)
    return jnp.where(
        first_head(HS),
        jnp.concatenate([first, pltpu.roll(first, HS, 1)], axis=0),
        jnp.concatenate([pltpu.roll(second, HS, 1), second], axis=0),
    )


def parted(values):
    top, bottom = values[: HS // 2], values[HS // 2 :]
    mine = first_head(HS // 2)
    first = jnp.where(mine, top, pltpu.roll(bottom, HS, 1))
    second = jnp.where(mine, pltpu.roll(top, HS, 1), bottom)
    return first.astype(BF16), second.astype(BF16)


def output_unit(
    at,
    state_ref, reads_ref, local_ref, read_ref, key_ref, value_ref, gate_ref, vec_ref,
    out_ref, gated_ref,
):
    vec = vec_ref[...]
    state = joined(state_ref[at])
    state_out = local_ref[at] + dot1(reads_ref[at], stack(state), NT)
    yield
    out_ref[at] = state_out
    bonus = head_sum(read_ref[at] * key_ref[at] * vec[13:14])
    center = state_out - head_sum(state_out) * (1.0 / HS)
    yield
    inverse = lax.rsqrt(head_sum(center * center) * (1.0 / HS) + GROUP_EPS)
    yield
    mixed = center * inverse * vec[14:15] + vec[15:16] + bonus * value_ref[at]
    gated_ref[at] = (mixed * gate_ref[at]).astype(BF16)


def add_sums(at, ref, parts):
    place = lax.broadcasted_iota(jnp.int32, (8, PAIR), 0)
    sums = jnp.zeros((8, PAIR), F32)
    for row, part in enumerate(parts):
        sums = sums + jnp.where(place == row, token_sum(part), 0.0)
    if at == 0:
        ref[...] = sums
    else:
        ref[...] += sums


def head_back_unit(
    at,
    grad_ref, out_ref, reads_ref, read_ref, key_ref, value_ref, gate_ref, vec_ref,
    out_grad_ref, gate_grad_ref, read_grad_ref, key_grad_ref, value_grad_ref, pay_ref, vec_grad_ref,
):
    vec = vec_ref[...]
    read, key, value = read_ref[at], key_ref[at], value_ref[at]
    grad = grad_ref[at]
    grad_mixed = grad * gate_ref[at]
    grad_normed = grad_mixed * vec[14:15]
    state_out = out_ref[at]
    bonus = head_sum(read * key * vec[13:14])
    along = head_sum(grad_mixed * value)
    center = state_out - head_sum(state_out) * (1.0 / HS)
    grad_center = grad_normed - head_sum(grad_normed) * (1.0 / HS)
    yield
    inverse = lax.rsqrt(head_sum(center * center) * (1.0 / HS) + GROUP_EPS)
    yield
    normed = center * inverse
    shared = head_sum(grad_normed * normed) * (1.0 / HS)
    yield
    mixed = normed * vec[14:15] + vec[15:16] + bonus * value
    gate_grad_ref[at] = (grad * mixed).astype(BF16)
    value_grad_ref[at] = bonus * grad_mixed
    read_grad_ref[at] = along * key * vec[13:14]
    key_grad_ref[at] = along * read * vec[13:14]
    out_grad = inverse * (grad_center - normed * shared)
    out_grad_ref[at] = out_grad
    pay = dot1(out_grad, reads_ref[at], TN)
    add_sums(at, vec_grad_ref, (along * read * key, grad_mixed * normed, grad_mixed))
    yield
    pay_ref[at, 0], pay_ref[at, 1] = parted(unstack(pay))


def last_unit(
    at,
    read_ref, keyed_ref, valued_ref, decay_ref, rate_ref, residual_ref, first_ref, vec_ref,
    strict_ref, inclusive_ref, start_ref, end_ref,
    solved_ref, lower_ref, reach_b_ref, reach_k_ref, start_alpha_ref, removed_ref,
    state_ref, after_ref, out_grad_ref, read_grad_ref, key_grad_ref, value_grad_ref,
    d_read_ref, d_keyed_ref, d_valued_ref, d_decay_ref, d_rate_ref, d_residual_ref, d_first_ref,
    vec_grad_ref,
):
    vec = vec_ref[...]
    final_row = lax.broadcasted_iota(jnp.int32, (HS, PAIR), 0) == HS - 1
    strict, inclusive = strict_ref[at], inclusive_ref[at]
    start, end = start_ref[at], end_ref[at]
    read, keyed, valued = read_ref[at], keyed_ref[at], valued_ref[at]
    first = first_ref[at].astype(F32)
    out_grad = out_grad_ref[at]
    state = joined(state_ref[at])
    after = joined(after_ref[at])
    spot, log_decay, rate, inverse_norm, unit, key = key_terms(
        keyed, decay_ref[at], rate_ref[at], vec
    )
    residual, value = value_terms(valued, residual_ref[at], first, vec)
    solution_rows = dot1(start_alpha_ref[at], stack(state), NT) + removed_ref[at]
    reached = dot1(jnp.concatenate([reach_b_ref[at], reach_k_ref[at]], axis=1), out_grad, TN)
    yield
    grown, shrunk, before, alpha, beta, key_hat = decayed(key, unit, rate, log_decay)
    read_hat = read * grown
    last = grown[HS - 1 : HS]
    yield
    beta_end = beta * (last * end)
    key_end = key_hat * (last * end)
    carried = dot1(jnp.concatenate([beta_end, key_end], axis=0), stack(after), NT)
    ends = dot1(jnp.concatenate([solution_rows, value], axis=0), stack(after), NN)
    yield
    d_rows = unstack(reached[:PAIR]) + carried[:HS]
    d_value = unstack(reached[PAIR:]) + carried[HS:]
    back = unstack(dot1(solved_ref[at], d_rows, TN))
    yield
    d_value = d_value + unstack(dot1(lower_ref[at], back, TN)) + value_grad_ref[at]
    outer = jnp.concatenate([out_grad, back], axis=0)
    scores = dot1(outer, jnp.concatenate([stack(solution_rows), stack(value)], axis=0), NT)
    entries = dot1(outer, stack(state), NN)
    yield
    mask = jnp.concatenate([inclusive, strict], axis=0)
    scores = scores * jnp.concatenate([mask, mask], axis=1)
    d_beta_end, d_key_end = ends[:HS] * end, ends[HS:] * end
    lefts = dot3(scores, jnp.concatenate([stack(beta), stack(key_hat)], axis=0), NN)
    rights = dot3(scores, jnp.concatenate([read_hat, alpha], axis=0), TN)
    yield
    d_read_hat = entries[:HS] * start + lefts[:HS]
    d_alpha = entries[HS:] * start + lefts[HS:]
    d_beta = unstack(rights[:PAIR]) + d_beta_end * last
    d_key_hat = unstack(rights[PAIR:]) + d_key_end * last
    d_last = token_sum(beta * d_beta_end + key_hat * d_key_end) + start[
        HS - 1 : HS
    ] * token_sum(state * after)
    d_moved = d_beta * shrunk
    d_key = key_grad_ref[at] + d_key_hat * shrunk
    d_read_ref[at] = (read_grad_ref[at] + d_read_hat * grown).astype(BF16)
    along = d_alpha * alpha
    d_total = d_read_hat * read_hat - d_beta * beta - d_key_hat * key_hat + along
    d_total = d_total + jnp.where(final_row, d_last * last, 0.0)
    d_unit = rate * d_moved - before * d_alpha
    d_decay = running_sum(d_total, True) - along
    shared = head_sum(unit * d_unit)
    yield
    d_rate = unit * d_moved + d_key * keyed * vec[12:13]
    d_scaled = (d_unit - unit * shared) * inverse_norm
    d_keyed = d_key * (1.0 + (rate - 1.0) * vec[12:13]) + d_scaled * vec[11:12]
    d_first = d_value * residual
    d_residual = d_first * (first - valued) * (1.0 - residual)
    d_rate_up = d_rate * rate * (1.0 - rate)
    d_decay_up = d_decay * log_decay * jax.nn.sigmoid(-spot)
    d_keyed_ref[at] = d_keyed.astype(BF16)
    d_valued_ref[at] = (d_value * (1.0 - residual)).astype(BF16)
    d_decay_ref[at] = d_decay_up.astype(BF16)
    d_rate_ref[at] = d_rate_up.astype(BF16)
    d_residual_ref[at] = d_residual.astype(BF16)
    d_first_ref[at] = d_first
    add_sums(
        at,
        vec_grad_ref,
        (d_decay_up, d_rate_up, d_residual, d_scaled * keyed, d_key * keyed * (rate - 1.0)),
    )


def head_call(unit, inputs, outputs, flops, pairs):
    count = inputs[0][0].shape[0]
    wide = pairs * PAIR
    kinds = [kind for _, kind in inputs] + [kind for kind, _ in outputs]

    def spec(kind):
        if kind == "tokens":
            return pl.BlockSpec((count, HS, wide), lambda i: (0, 0, i))
        if kind == "rows":
            return pl.BlockSpec((24, wide), lambda i: (0, i))
        if kind == "sums":
            return pl.BlockSpec((8, wide), lambda i: (0, i))
        if kind == "pay":
            return pl.BlockSpec((count, 2 * pairs, HS, PAIR), lambda i: (0, i, 0, 0))
        if kind == "states":
            return pl.BlockSpec((count, 2 * pairs, HS // 2, PAIR), lambda i: (0, i, 0, 0))
        return pl.BlockSpec((count, HS, PAIR), lambda i: (0, 0, 0))

    shapes = {
        "tokens": (count, HS, EMBED_SIZE),
        "sums": (8, EMBED_SIZE),
        "pay": (count, H, HS, PAIR),
        "states": (count, H, HS // 2, PAIR),
    }

    def view(kind, ref, at):
        if kind == "tokens":
            return ref.at[:, :, pl.ds(at * PAIR, PAIR)]
        if kind in ("rows", "sums"):
            return ref.at[:, pl.ds(at * PAIR, PAIR)]
        if kind in ("pay", "states"):
            return ref.at[:, pl.ds(2 * at, 2)]
        return ref

    def kernel(*refs):
        running = []
        for pair in range(pairs):
            views = [view(kind, ref, pair) for kind, ref in zip(kinds, refs)]
            running += [unit(at, *views) for at in range(count)]
        done = object()
        while running:
            running = [run for run in running if next(run, done) is not done]

    bytes_moved = sum(4 * a.size for a, _ in inputs) + 4 * sum(
        count * HS * EMBED_SIZE for _ in outputs
    )
    return pl.pallas_call(
        kernel,
        grid=(HEAD_PAIRS // pairs,),
        in_specs=[spec(kind) for _, kind in inputs],
        out_specs=[spec(kind) for kind, _ in outputs],
        out_shape=[jax.ShapeDtypeStruct(shapes[kind], dtype) for kind, dtype in outputs],
        compiler_params=pltpu.CompilerParams(vmem_limit_bytes=HEAD_VMEM),
        cost_estimate=pl.CostEstimate(
            flops=flops, bytes_accessed=bytes_moved, transcendentals=count * HS * EMBED_SIZE * 6
        ),
    )(*[array for array, _ in inputs])


def chain_call(body, odd, *arrays):
    return pl.pallas_call(
        body,
        in_specs=[pl.BlockSpec(memory_space=pltpu.SMEM)]
        + [pl.BlockSpec(memory_space=pltpu.VMEM)] * len(arrays),
        out_specs=pl.BlockSpec(memory_space=pltpu.VMEM),
        out_shape=jax.ShapeDtypeStruct((arrays[0].shape[0], HS // 2, PAIR), BF16),
        compiler_params=pltpu.CompilerParams(vmem_limit_bytes=CHAIN_VMEM),
        cost_estimate=pl.CostEstimate(
            flops=32 * 4 * HS**3, bytes_accessed=3 * 1024 * 1024, transcendentals=0
        ),
    )(odd, *arrays)


def project_kernel(*refs):
    weight_ref, norm_ref, before_ref, keep_ref = refs[:4]
    mixes, (read_ref, keyed_ref, valued_ref), ups = refs[4:10], refs[10:13], refs[13:17]
    mids_ref, slopes_ref, vec_ref = refs[17:]
    turned = [
        weight_ref[128 * i : 128 * i + 128, UP_AT + LOW_WIDE - 128 :].astype(F32).T
        for i in range(8)
    ]
    vec = jnp.concatenate(turned, axis=1)[LOW - 256 : LOW - 256 + 24]
    vec_ref[...] = vec
    length = norm_ref.shape[1]
    for at in range(norm_ref.shape[0]):
        normed, delta = shifted(norm_ref, before_ref, keep_ref, vec, at)
        for index, mix in enumerate(mixes):
            mix[pl.ds(at * length, length)] = (normed + delta * vec[2 + index : 3 + index]).astype(
                BF16
            )
    mix_r, mix_w, mix_k, mix_v, mix_a, mix_g = mixes
    for index, (mix, target) in enumerate(
        ((mix_r, read_ref), (mix_k, keyed_ref), (mix_v, valued_ref))
    ):
        target[...] = dot(
            mix[...], weight_ref[:, index * EMBED_SIZE : (index + 1) * EMBED_SIZE], NN
        )
    down = weight_ref[:, DOWN_AT:UP_AT]
    up = weight_ref[:, UP_AT:]
    lane = lax.broadcasted_iota(jnp.int32, slopes_ref.shape, 1)
    insides = [jnp.logical_and(lane >= EDGES[i], lane < EDGES[i + 1]) for i in range(4)]
    low = jnp.zeros(slopes_ref.shape, F32)
    for inside, mix in zip(insides, (mix_w, mix_a, mix_v, mix_g)):
        low = jnp.where(inside, dot(mix[...], down, NN), low)
    decay, gate = jnp.tanh(low), jax.nn.sigmoid(low)
    mid = jnp.where(insides[0], decay, jnp.where(insides[3], gate, low)).astype(BF16)
    mids_ref[...] = mid
    slopes_ref[...] = jnp.where(
        insides[0], 1.0 - decay * decay, jnp.where(insides[3], gate * (1.0 - gate), 1.0)
    )
    for inside, target in zip(insides, ups):
        target[...] = dot(jnp.where(inside, mid, jnp.zeros_like(mid)), up, NT)


def project(weights, normed, before, keep):
    tokens = normed.shape[0] * normed.shape[1]
    whole = lambda shape: pl.BlockSpec(shape, lambda i: (0,) * len(shape))
    act = (tokens, EMBED_SIZE)
    low = (tokens, LOW_WIDE)
    outs = [(act, BF16)] * 6 + [(act, F32)] * 7 + [(low, BF16), (low, F32)]
    outs += [((24, EMBED_SIZE), F32)]
    inputs = (normed, before, keep)
    return pl.pallas_call(
        project_kernel,
        grid=(1,),
        in_specs=[whole((EMBED_SIZE, OUT_AT))] + [whole(part.shape) for part in inputs],
        out_specs=[whole(shape) for shape, _ in outs],
        out_shape=[jax.ShapeDtypeStruct(shape, kind) for shape, kind in outs],
        compiler_params=pltpu.CompilerParams(vmem_limit_bytes=GRAD_VMEM),
        cost_estimate=pl.CostEstimate(
            flops=2 * tokens * EMBED_SIZE * 5000, bytes_accessed=12_000_000, transcendentals=0
        ),
    )(weights, *inputs)


def turned_into(target, values):
    for at in range(values.shape[1] // 128):
        target(at, values[:, at * 128 : (at + 1) * 128].astype(F32).T.astype(BF16))


def channel_kernel(
    channel_ref, seed_ref, key_ref, val_ref, out_ref, grad_ref, squared_ref, act_ref
):
    seed = seed_ref[...]
    key = key_ref[...].reshape(EMBED_SIZE, -1)
    val = val_ref[...].reshape(-1, EMBED_SIZE)
    hidden = jnp.maximum(dot(channel_ref[...], key, NN), 0.0)
    squared = jnp.square(hidden).astype(BF16)
    d_squared = dot(seed, val, NT)
    act = (2.0 * hidden * d_squared).astype(BF16)
    act_ref[...] = act

    def into(at, part):
        squared_ref[at] = part.reshape(4, ROWS, part.shape[-1])

    turned_into(into, squared)
    out = dot(squared, val, NN)
    grad = dot(act, key, NT)

    @pl.when(pl.program_id(0) == 0)
    def _():
        out_ref[...] = out
        grad_ref[...] = grad

    @pl.when(pl.program_id(0) > 0)
    def _():
        out_ref[...] += out
        grad_ref[...] += grad


def channel_mix(channel, seed, full):
    tokens = channel.shape[0]
    block = 512
    whole = pl.BlockSpec((tokens, EMBED_SIZE), lambda j: (0, 0))
    return pl.pallas_call(
        channel_kernel,
        grid=(FF // block,),
        in_specs=[
            whole,
            whole,
            pl.BlockSpec((32, ROWS, block), lambda j: (0, 4 + j // 2, j % 2)),
            pl.BlockSpec((4, 4 * ROWS, EMBED_SIZE), lambda j: (j, 0, 0)),
        ],
        out_specs=[
            whole,
            whole,
            pl.BlockSpec((4, 4, ROWS, tokens), lambda j: (j, 0, 0, 0)),
            pl.BlockSpec((tokens, block), lambda j: (0, j)),
        ],
        out_shape=[
            jax.ShapeDtypeStruct((tokens, EMBED_SIZE), F32),
            jax.ShapeDtypeStruct((tokens, EMBED_SIZE), F32),
            jax.ShapeDtypeStruct((32, 4, ROWS, tokens), BF16),
            jax.ShapeDtypeStruct((tokens, FF), BF16),
        ],
        compiler_params=pltpu.CompilerParams(vmem_limit_bytes=GRAD_VMEM),
        cost_estimate=pl.CostEstimate(
            flops=8 * tokens * FF * EMBED_SIZE, bytes_accessed=20_000_000, transcendentals=0
        ),
    )(channel, seed, full, full)


def channel_grad_kernel(squared_ref, seed_ref, channel_ref, act_ref, out_ref, features):
    step = pl.program_id(0)

    def into_features(at, part):
        features[at] = part

    @pl.when(step == 4)
    def _():
        turned_into(into_features, channel_ref)

    def write(left_of, right):
        for group in range(8):
            out_ref[pl.ds(group * 4, 4)] = (
                dot(left_of(group), right, NN).astype(BF16).reshape(4, ROWS, EMBED_SIZE)
            )

    @pl.when(step < 4)
    def _():
        left_of = lambda group: squared_ref[pl.ds(group * 4, 4), 0].reshape(128, -1)
        write(left_of, seed_ref[...])

    @pl.when(step >= 4)
    def _():
        write(lambda group: features[group], act_ref[...])


def channel_grads(squared, seed, channel, act):
    tokens = seed.shape[0]
    whole = pl.BlockSpec((tokens, EMBED_SIZE), lambda j: (0, 0))
    return pl.pallas_call(
        channel_grad_kernel,
        grid=(8,),
        in_specs=[
            pl.BlockSpec((32, 1, ROWS, tokens), lambda j: (0, jnp.minimum(j, 3), 0, 0)),
            whole,
            whole,
            pl.BlockSpec((tokens, EMBED_SIZE), lambda j: (0, jnp.maximum(j - 4, 0))),
        ],
        out_specs=pl.BlockSpec((32, ROWS, EMBED_SIZE), lambda j: (0, j, 0)),
        out_shape=jax.ShapeDtypeStruct((32, 8 * ROWS, EMBED_SIZE), BF16),
        scratch_shapes=[pltpu.VMEM((8, 128, tokens), BF16)],
        compiler_params=pltpu.CompilerParams(vmem_limit_bytes=GRAD_VMEM),
        cost_estimate=pl.CostEstimate(
            flops=2 * tokens * 8 * EMBED_SIZE**2, bytes_accessed=20_000_000, transcendentals=0
        ),
    )(squared, seed, channel, act)


def shifted(norm_ref, before_ref, keep_ref, vec, at):
    length = norm_ref.shape[1]
    top = lax.broadcasted_iota(jnp.int32, (length, EMBED_SIZE), 0) == 0
    normed = norm_ref[at] * vec[0:1] + vec[1:2]
    before = before_ref[at] * vec[0:1] + vec[1:2]
    prior = jnp.where(top, before, pltpu.roll(normed, 1, 0)) * keep_ref[at][:, :1]
    return normed, prior - normed


def input_back_kernel(
    low_ref, d_read, d_keyed, d_valued, weight_ref, norm_ref, before_ref, keep_ref, vec_ref,
    grad_ref, edge_ref, sums_ref,
):
    vec = vec_ref[...]
    low, down = low_ref[...], weight_ref[:, DOWN_AT:]
    lane = lax.broadcasted_iota(jnp.int32, low.shape, 1)
    by_low = []
    for at in range(4):
        inside = jnp.logical_and(lane >= EDGES[at], lane < EDGES[at + 1])
        by_low.append(dot(jnp.where(inside, low, jnp.zeros_like(low)), down, NT))
    by_main = [
        dot(part[...], weight_ref[:, i * EMBED_SIZE : (i + 1) * EMBED_SIZE], NT)
        for i, part in enumerate((d_read, d_keyed, d_valued))
    ]
    grads = (by_main[0], by_low[0], by_main[1], by_main[2] + by_low[2], by_low[1], by_low[3])
    length = norm_ref.shape[1]
    bottom = lax.broadcasted_iota(jnp.int32, (length, EMBED_SIZE), 0) == length - 1
    place = lax.broadcasted_iota(jnp.int32, (8, EMBED_SIZE), 0)
    sums = jnp.zeros((8, EMBED_SIZE), F32)
    for at in range(norm_ref.shape[0]):
        rows = slice(at * length, (at + 1) * length)
        _, delta = shifted(norm_ref, before_ref, keep_ref, vec, at)
        total = sum(part[rows] for part in grads)
        mixed = sum(part[rows] * vec[2 + i : 3 + i] for i, part in enumerate(grads))
        kept = mixed * keep_ref[at][:, :1]
        later = jnp.where(bottom, 0.0, pltpu.roll(kept, length - 1, 0))
        grad_ref[at] = total - mixed + later
        edge_ref[at] = kept[:8]
        for i, part in enumerate(grads):
            sums = sums + jnp.where(place == i, token_sum(delta * part[rows]), 0.0)
    sums_ref[...] = sums


def input_back(low, d_time, weights, normed, before, keep, vec):
    count, length, width = normed.shape
    whole = lambda shape: pl.BlockSpec(shape, lambda i: (0,) * len(shape))
    inputs = (low, *d_time, weights, normed, before, keep, vec)
    outs = [(count, length, width), (count, 8, width), (8, width)]
    specs = [whole(part.shape) for part in inputs]
    specs[4] = whole((EMBED_SIZE, UP_AT))
    return pl.pallas_call(
        input_back_kernel,
        grid=(1,),
        in_specs=specs,
        out_specs=[whole(shape) for shape in outs],
        out_shape=[jax.ShapeDtypeStruct(shape, F32) for shape in outs],
        compiler_params=pltpu.CompilerParams(vmem_limit_bytes=GRAD_VMEM),
        cost_estimate=pl.CostEstimate(flops=0, bytes_accessed=1_000_000, transcendentals=0),
    )(*inputs)


def turn_kernel(*refs):
    for slot, ref in enumerate(refs[:-1]):

        def into(at, part):
            refs[-1][slot, at * 2 : at * 2 + 2] = part.reshape(2, 2, ROWS, part.shape[-1])

        turned_into(into, ref)


def turned_by_owner(parts):
    tokens = parts[0].shape[0]
    shape = (len(parts), 16, 2, ROWS, tokens)
    return pl.pallas_call(
        turn_kernel,
        grid=(1,),
        in_specs=[pl.BlockSpec(part.shape, lambda i: (0, 0)) for part in parts],
        out_specs=pl.BlockSpec(shape, lambda i: (0, 0, 0, 0, 0)),
        out_shape=jax.ShapeDtypeStruct(shape, BF16),
        compiler_params=pltpu.CompilerParams(vmem_limit_bytes=GRAD_VMEM),
        cost_estimate=pl.CostEstimate(flops=0, bytes_accessed=4_000_000, transcendentals=0),
    )(*parts)


def time_grad_kernel(
    core_ref, inputs_ref, d_read, d_keyed, d_valued, d_att, d_decay, d_rate, d_residual, d_gate,
    up_ref, slopes_ref, mids_ref, low_ref, mine_ref, theirs_ref, turned,
):
    d_ups = (d_decay, d_rate, d_residual, d_gate)
    lane = lax.broadcasted_iota(jnp.int32, slopes_ref.shape, 1)
    insides = [jnp.logical_and(lane >= EDGES[i], lane < EDGES[i + 1]) for i in range(4)]
    up = up_ref[...]
    d_low = jnp.zeros(slopes_ref.shape, F32)
    for inside, d_up in zip(insides, d_ups):
        d_low = jnp.where(inside, dot(d_up[...], up, NN), d_low)
    d_low = (d_low * slopes_ref[...]).astype(BF16)
    low_ref[...] = d_low
    for slot, d_up in enumerate(d_ups):

        def into(at, part):
            turned[slot, at * 2 : at * 2 + 2] = part.reshape(2, 2, ROWS, part.shape[-1])

        turned_into(into, d_up)
    none = jnp.zeros(d_low.shape, BF16)

    def in_two(values):
        parts = [jnp.where(inside, values, none) for inside in insides]
        return (
            jnp.concatenate([part[:, :128] for part in parts[:2]], axis=0),
            jnp.concatenate([part[:, 128:] for part in parts[2:]], axis=0),
        )

    low_parts, mid_parts = in_two(d_low), in_two(mids_ref[...])
    block = 2 * ROWS

    def write(first, second):
        for z in range(4):
            chips = pl.ds(4 * z, 4)
            rows = pl.ds(4 * block * z, 4 * block)

            def left(slot):
                return inputs_ref[slot, chips].reshape(4 * block, -1)

            def left_up(slot):
                return turned[slot, chips].reshape(4 * block, -1)

            def low_grads(parts, slots, get):
                pairs = [jnp.concatenate([get(i) for i in pair], axis=1) for pair in slots]
                return jnp.concatenate(
                    [dot(pair, part, NN).astype(BF16) for pair, part in zip(pairs, parts)], axis=1
                )

            by_read = dot(left(0), d_read[...], NN).astype(BF16)
            by_key = dot(left(2), d_keyed[...], NN).astype(BF16)
            down = low_grads(low_parts, ((1, 4), (3, 5)), left)
            for x, quarter in [(x, quarter) for x in range(4) for quarter in range(4)]:
                at = pl.ds(((quarter * 4 + x) * 4 + z) * block // 4, block // 4)
                part = slice(x * block + quarter * block // 4, x * block + (quarter + 1) * block // 4)
                first[at, :EMBED_SIZE] = by_read[part]
                first[at, EMBED_SIZE : 2 * EMBED_SIZE] = by_key[part]
                first[at, 2 * EMBED_SIZE :] = down[part]
            second[rows, :EMBED_SIZE] = dot(left(3), d_valued[...], NN).astype(BF16)
            second[rows, EMBED_SIZE : 2 * EMBED_SIZE] = dot(left(6), d_att[...], NN).astype(BF16)
            second[rows, 2 * EMBED_SIZE :] = low_grads(mid_parts, ((0, 1), (2, 3)), left_up)

    @pl.when(core_ref[0] == 0)
    def _():
        write(mine_ref, theirs_ref)

    @pl.when(core_ref[0] == 1)
    def _():
        write(theirs_ref, mine_ref)


def time_grads(core, inputs, d_time, d_ups, weights, slopes, mids):
    tokens, wide = slopes.shape
    whole = lambda part: pl.BlockSpec(part.shape, lambda i: (0,) * part.ndim)
    shapes = [(tokens, wide), (EMBED_SIZE, HALF), (EMBED_SIZE, HALF)]
    return pl.pallas_call(
        time_grad_kernel,
        grid=(1,),
        in_specs=[pl.BlockSpec(memory_space=pltpu.SMEM)]
        + [whole(part) for part in (inputs, *d_time, *d_ups)]
        + [pl.BlockSpec((EMBED_SIZE, wide), lambda i: (0, UP_AT // wide))]
        + [whole(slopes), whole(mids)],
        out_specs=[pl.BlockSpec(shape, lambda i: (0, 0)) for shape in shapes],
        out_shape=[jax.ShapeDtypeStruct(shape, BF16) for shape in shapes],
        scratch_shapes=[pltpu.VMEM((4, 16, 2, ROWS, tokens), BF16)],
        compiler_params=pltpu.CompilerParams(vmem_limit_bytes=GRAD_VMEM),
        cost_estimate=pl.CostEstimate(
            flops=2 * tokens * EMBED_SIZE * 4 * HALF, bytes_accessed=12_000_000, transcendentals=0
        ),
    )(core, inputs, *d_time, *d_ups, weights, slopes, mids)


def moved(values, first=0, second=0, third=0, core=0):
    pairs = []
    for at in range(128):
        y, z, x, mine = at // 32, at // 8 % 4, at // 2 % 4, at % 2
        x = (x + second) % 4
        if mine == 0:
            y, z = (y + first) % 4, (z + third) % 4
        else:
            z, y = (z + first) % 4, (y + third) % 4
        pairs.append((at, y * 32 + z * 8 + x * 2 + (mine + core) % 2))
    return lax.ppermute(values, ("rep", "shard"), pairs)


def over_two_axes(parts):
    groups = [
        [y * 32 + z * 8 + x * 2 for x in range(4) for z in range(4)] for y in range(4)
    ] + [
        [y * 32 + z * 8 + x * 2 + 1 for x in range(4) for y in range(4)] for z in range(4)
    ]
    parts = parts.reshape((16,) + parts.shape[2:])
    arrived = lax.all_to_all(parts, ("rep", "shard"), 0, 0, axis_index_groups=groups)
    return jnp.sum(arrived.astype(F32), axis=0)


def to_owners(quarter):
    arrived = []
    for step in range(4):
        pairs = []
        for at in range(128):
            y, chip, mine = at // 32, at // 2 % 16, at % 2
            to = (y % 2 * 2 + mine + step) % 4
            pairs.append((at, to * 32 + chip * 2 + y // 2))
        arrived.append(lax.ppermute(quarter, ("rep", "shard"), pairs))
    turn = jnp.stack([arrived[-step % 4] for step in range(4)] * 2)
    ordered = lax.dynamic_slice_in_dim(turn, -lax.axis_index("rep") % 4, 4)
    rows, columns = quarter.shape
    ordered = ordered.reshape(2, 2, rows, columns).swapaxes(1, 2)
    return ordered.reshape(2 * rows, 2 * columns).astype(F32)


def ring_place():
    place, y = lax.axis_index("shard"), lax.axis_index("rep")
    z, x, core = place // 8, place // 2 % 4, place % 2
    return jnp.where(core == 0, y, z), x, jnp.where(core == 0, z, y), core


def picked(values, at):
    return lax.dynamic_index_in_dim(values, at % values.shape[0], 0, keepdims=False)


def around_ring(chunk, send):
    total = chunk(0).astype(F32)
    for step in (1, 3, 2):
        total = total + send(chunk(step), step).astype(F32)
    return total


def to_group(part, by):
    return lax.ppermute(part, "rep", [(i, (i + by) % 4) for i in range(4)])


def quarter_over_groups(values):
    place = lax.axis_index("rep")
    quarters = values.astype(BF16).reshape(4, -1, values.shape[1])
    return around_ring(lambda k: picked(quarters, place + k), to_group).astype(BF16)


def from_quarters(mine):
    place = lax.axis_index("rep")
    parts = [mine] + [to_group(mine, step) for step in (3, 2, 1)]
    twice = jnp.concatenate(parts * 2, axis=0)
    return lax.dynamic_slice_in_dim(twice, (-place) % 4 * mine.shape[0], 4 * mine.shape[0]).astype(
        F32
    )


def passed_along(rows, by):
    size = lax.axis_size("shard")
    pairs = [(i, i + by) for i in range(size) if 0 <= i + by < size]
    return lax.ppermute(rows, "shard", pairs)


def product(left, right):
    return jnp.dot(left, right, preferred_element_type=F32)


def product_tn(left, right):
    return lax.dot_general(left, right, (((0,), (0,)), ((), ())), preferred_element_type=F32)


def product_nt(left, right):
    return lax.dot_general(left, right, (((1,), (1,)), ((), ())), preferred_element_type=F32)


def layer_norm(values, gain, bias):
    center = values - jnp.mean(values, axis=-1, keepdims=True)
    spread = jnp.mean(center * center, axis=-1, keepdims=True)
    return center * lax.rsqrt(spread + NORM_EPS) * gain + bias


def norm_piece(values, vec, row):
    return layer_norm(values, vec[row], vec[row + 1])


def mix_piece(values, before, vec, keep, first_row, count):
    prior = jnp.concatenate([before[:, None], values[:, :-1]], axis=1) * keep[:, :, None]
    delta = prior - values
    return tuple(values + delta * vec[first_row + index] for index in range(count))


def flat(values):
    return values.reshape(-1, values.shape[-1])


def gathered(shard):
    return lax.all_gather(shard, "shard", axis=0, tiled=True)


def scattered(full):
    return lax.psum_scatter(full, "shard", scatter_dimension=0, tiled=True)


def exchanged(pay):
    return lax.all_to_all(pay.reshape((-1,) + pay.shape[-2:]), "shard", 0, 0, tiled=False)


def local(
    layer_input,
    first_layer_values,
    segments,
    receptance_key_value_weight,
    time_output_weight,
    low_rank_down,
    low_rank_up,
    channel_key_weight,
    channel_value_weight,
    vectors,
    output_gradient,
):
    count, length, width = layer_input.shape
    rows = vectors.shape[1]
    spot_first, _, spot_third, spot_core = ring_place()
    filler = lambda used: jnp.zeros((rows, LOW_WIDE - used), BF16)
    weights = gathered(
        jnp.concatenate(
            [
                receptance_key_value_weight,
                low_rank_down,
                filler(LOW),
                low_rank_up.T,
                vectors.T,
                filler(LOW + vectors.shape[0]),
                time_output_weight,
            ],
            axis=1,
        )
    )
    rest = lax.all_gather(
        jnp.concatenate(
            [channel_value_weight] + jnp.split(channel_key_weight, 4, axis=1), axis=0
        ),
        "shard",
    )
    full_out = weights[:, OUT_AT:]

    edge = passed_along(segments[:, -1] + 1, 1) - 1
    keep = jnp.concatenate(
        [segments[:, :1] == edge[:, None], segments[:, 1:] == segments[:, :-1]], axis=1
    ).astype(F32)
    same = (segments[:, :, None] == segments[:, None, :]).astype(F32)
    later = lax.broadcasted_iota(jnp.int32, (length, length), 0)
    earlier = lax.broadcasted_iota(jnp.int32, (length, length), 1)
    strict = jnp.tile(same * (later > earlier).astype(F32), (1, 1, 2))
    inclusive = jnp.tile(same * (later >= earlier).astype(F32), (1, 1, 2))
    start = jnp.broadcast_to(
        (segments == edge[:, None]).astype(F32)[:, :, None], (count, length, PAIR)
    )
    end = jnp.broadcast_to(same[:, -1, :, None], (count, length, PAIR))
    masks = [(strict, "masks"), (inclusive, "masks"), (start, "masks"), (end, "masks")]
    odd = (lax.axis_index("shard") % 2).astype(jnp.int32).reshape(1)

    hidden = layer_input.astype(F32)
    raw_before = passed_along(layer_input[:, -1], 1).astype(F32)
    plain = lambda values: layer_norm(values, 1.0, 0.0)
    plain_hidden, plain_before = plain(hidden), plain(raw_before)[:, None]
    keep_wide = jnp.broadcast_to(keep[:, :, None], (count, length, PAIR))
    x_r, x_w, x_k, x_v, x_a, x_g, read, keyed, valued, *more = project(
        weights, plain_hidden, plain_before, keep_wide
    )
    decay_up, rate_up, residual_up, gate, mids, slopes, vec = more
    _, pull_norm1 = jax.vjp(partial(norm_piece, row=0), hidden, vec)
    shape = (count, length, width)
    read, keyed, valued, decay_up, rate_up, residual_up, gate = [
        part.reshape(shape) for part in (read, keyed, valued, decay_up, rate_up, residual_up, gate)
    ]
    vec_row, start_mask = (vec, "rows"), (start, "masks")
    pay, solved, lower, start_alpha, removed, key, value = head_call(
        first_unit,
        [
            (part, "tokens")
            for part in (keyed, valued, decay_up, rate_up, residual_up, first_layer_values)
        ]
        + [vec_row, (strict, "masks"), start_mask, (end, "masks")],
        [("pay", BF16)] + [("tokens", F32)] * 6,
        2_000_000_000,
        4,
    )
    chain_items = exchanged(pay)
    reach_b, reach_k, reads, local_out = head_call(
        reach_unit,
        [
            (part, "tokens")
            for part in (read, keyed, decay_up, rate_up, value, start_alpha, removed)
        ]
        + [vec_row, (inclusive, "masks"), start_mask],
        [("tokens", F32)] * 4,
        1_000_000_000,
        4,
    )
    states_shape = (count, H, HS // 2, PAIR)
    states = exchanged(chain_call(chain_kernel, odd, chain_items)).reshape(states_shape)
    tokens = [
        (part, "tokens")
        for part in (read, keyed, valued, decay_up, rate_up, residual_up, first_layer_values)
    ]
    gate_terms = [
        (read, "tokens"), (key, "tokens"), (value, "tokens"), (gate, "tokens"), (vec, "rows")
    ]
    state_out, gated = head_call(
        output_unit,
        [(states, "states"), (reads, "tokens"), (local_out, "tokens")] + gate_terms,
        [("tokens", F32), ("tokens", BF16)],
        300_000_000,
        4,
    )
    gated = flat(gated)
    mixed_h = hidden + product(gated, full_out).reshape(shape)

    normed2, pull_norm2 = jax.vjp(partial(norm_piece, row=16), mixed_h, vec)
    before2 = passed_along(normed2[:, -1], 1)
    channel, pull_mix2 = jax.vjp(
        partial(mix_piece, keep=keep, first_row=18, count=1), normed2, before2, vec
    )
    channel_low = flat(channel[0].astype(BF16))
    seed = flat(output_gradient)
    channel_out, grad_channel, squared, grad_act = channel_mix(
        channel_low, seed, rest
    )
    channel_part = channel_grads(squared, seed, channel_low, grad_act)
    grad_channel, channel_part = lax.optimization_barrier((grad_channel, channel_part))
    own_channel = scattered(channel_part)[0]
    turned = turned_by_owner((x_r, x_w, x_k, x_v, x_a, x_g, gated))
    hidden_out = (mixed_h + channel_out.reshape(shape)).astype(BF16)
    grad_channel = grad_channel.reshape(shape)
    grad_norm2, grad_before2, vec_grad_a = pull_mix2((grad_channel,))
    grad_norm2 = grad_norm2.at[:, -1].add(passed_along(grad_before2, -1))
    grad_mixed, vec_grad_b = pull_norm2(grad_norm2)
    grad_mixed = grad_mixed + output_gradient.astype(F32)
    grad_att = flat(grad_mixed.astype(BF16))
    grad_gated = product_nt(grad_att, full_out).reshape(shape)

    out_grad, gate_grad, read_grad, key_grad, value_grad, grad_pay, vec_sums_a = head_call(
        head_back_unit,
        [(grad_gated, "tokens"), (state_out, "tokens"), (reads, "tokens")] + gate_terms,
        [("tokens", F32), ("tokens", BF16)]
        + [("tokens", F32)] * 3
        + [("states", BF16), ("sums", F32)],
        300_000_000,
        4,
    )
    after = exchanged(
        chain_call(chain_back_kernel, odd, chain_items, exchanged(grad_pay))
    ).reshape(states_shape)
    d_read, d_keyed, d_valued, d_decay, d_rate, d_residual, first_grad, vec_sums_b = head_call(
        last_unit,
        tokens
        + [(vec, "rows")]
        + masks
        + [
            (part, "tokens")
            for part in (solved, lower, reach_b, reach_k, start_alpha, removed)
        ]
        + [(states, "states"), (after, "states")]
        + [(part, "tokens") for part in (out_grad, read_grad, key_grad, value_grad)],
        [("tokens", BF16)] * 6 + [("tokens", F32), ("sums", F32)],
        3_000_000_000,
        2,
    )
    d_time = [flat(d_read), flat(d_keyed), flat(d_valued)]
    d_ups = [flat(part) for part in (d_decay, d_rate, d_residual, gate_grad)]
    d_low, mine, theirs = time_grads(odd, turned, [*d_time, grad_att], d_ups, weights, slopes, mids)
    barrier = lax.optimization_barrier

    by_place = (4, 4, 4, ROWS // 2, HALF)
    mine, theirs = mine.reshape(by_place), theirs.reshape(by_place)
    far_theirs = picked(theirs, spot_third + 2)
    far_arrived = moved(far_theirs, core=1)
    far_mine = picked(mine, spot_first + 2)
    far_arrived, far_mine, theirs = barrier((far_arrived, far_mine, theirs))
    far = (far_mine.astype(F32) + far_arrived.astype(F32)).astype(BF16)
    arrived = moved(theirs, core=1)
    from_behind = moved(far[:2], first=1)
    from_ahead = moved(far[2:], first=-1)
    far, d_low = barrier((far, d_low))
    grad_norm1, grad_edge, mix_sums = input_back(
        d_low, d_time, weights, plain_hidden, plain_before, keep_wide, vec
    )
    from_behind, from_ahead, arrived, grad_norm1, grad_edge = barrier(
        (from_behind, from_ahead, arrived, grad_norm1, grad_edge)
    )

    def chunk(k):
        own_part, other_part = [picked(part, spot_first + k) for part in (mine, arrived)]
        return own_part.astype(F32) + other_part.astype(F32)

    ahead, behind = chunk(1), chunk(3)
    ahead = jnp.concatenate([ahead[:2] + from_behind.astype(F32), ahead[2:]], axis=0)
    behind = jnp.concatenate([behind[:2], behind[2:] + from_ahead.astype(F32)], axis=0)
    from_behind = moved(ahead.astype(BF16), first=1)
    from_ahead = moved(behind.astype(BF16), first=-1)
    grad_norm1 = grad_norm1.at[:, -1].add(passed_along(grad_edge[:, 0], -1))
    grad_hidden, vec_grad_d = pull_norm1(grad_norm1)
    hidden_grad = grad_mixed + grad_hidden
    vec_grad = vec_grad_a + vec_grad_b + vec_grad_d
    vec_grad = vec_grad + jnp.concatenate(
        [
            jnp.zeros((2, width), F32),
            mix_sums[:6],
            vec_sums_b[:5],
            vec_sums_a[:3],
            jnp.zeros((vec.shape[0] - 16, width), F32),
        ],
        axis=0,
    )
    vec_turned = jnp.pad(vec_grad.T, ((0, 0), (0, LOW_WIDE - LOW - vec.shape[0]))).astype(BF16)
    vec_turned = vec_turned.reshape(4, 4, 4, ROWS // 2, LOW_WIDE - LOW)
    vec_turned = jnp.where(spot_core == 0, vec_turned.swapaxes(0, 2), vec_turned)
    along_first = lambda part, by: moved(part, first=by)
    vec_part = around_ring(lambda k: picked(vec_turned, spot_first + k), along_first)
    from_behind, from_ahead, vec_part = barrier((from_behind, from_ahead, vec_part))

    vec_at = HALF - LOW_WIDE + LOW
    summed = chunk(0) + from_behind.astype(F32) + from_ahead.astype(F32)
    summed = (summed + jnp.pad(vec_part, ((0, 0),) * 3 + ((vec_at, 0),))).astype(BF16)
    summed = over_two_axes(summed).astype(BF16)
    own_channel = quarter_over_groups(own_channel)
    summed, own_channel = barrier((summed, own_channel))
    own = to_owners(summed)
    own_channel = from_quarters(own_channel)
    own_key = jnp.concatenate([own_channel[128 + 32 * k : 160 + 32 * k] for k in range(4)], axis=1)
    down_at = 2 * EMBED_SIZE
    value_at, out_at, up_at = HALF, HALF + EMBED_SIZE, HALF + 2 * EMBED_SIZE
    own_vec = own[:, vec_at:HALF] + own[:, HALF + vec_at :]
    return (
        hidden_out,
        hidden_grad,
        first_grad,
        jnp.concatenate([own[:, :down_at], own[:, value_at:out_at]], axis=1),
        own[:, out_at:up_at],
        own[:, down_at : down_at + LOW],
        own[:, up_at : up_at + LOW].T,
        own_key,
        own_channel[:128],
        own_vec[:, : vectors.shape[0]].T,
    )


def solution(mesh):
    tokens = P("rep", "shard", None)
    rows = P("shard", None)
    columns = P(None, "shard")
    return jax.shard_map(
        local,
        mesh=mesh,
        in_specs=(
            tokens, tokens, P("rep", "shard"), rows, rows, rows, columns, rows, rows, columns, tokens
        ),
        out_specs=(tokens, tokens, tokens, rows, rows, rows, columns, rows, rows, columns),
        check_vma=False,
    )
```

```python
from functools import partial

import jax
import jax.numpy as jnp
from jax import lax
from jax.experimental import pallas as pl
from jax.experimental.pallas import tpu as pltpu
from jax.sharding import PartitionSpec as P

EMBED_SIZE = 1024
H = 16
HS = 64
FF = 4096
DECAY_RANK = 64
LA = 64
LV = 32
LOW = 320
PAIR = 2 * HS
HEAD_PAIRS = H // 2
SMALL = 16

NORM_EPS = 1e-05
GROUP_EPS = 0.00064
UNIT_EPS = 1e-06
F32 = jnp.float32
BF16 = jnp.bfloat16
HEAD_VMEM = 60 * 1024 * 1024
CHAIN_VMEM = 60 * 1024 * 1024
GRAD_VMEM = 60 * 1024 * 1024
ROWS = 32
LOW_WIDE = 384
DOWN_AT = 3 * EMBED_SIZE
UP_AT = DOWN_AT + LOW_WIDE
OUT_AT = UP_AT + LOW_WIDE
HALF = 2 * EMBED_SIZE + LOW_WIDE
EDGES = (0, DECAY_RANK, DECAY_RANK + LA, DECAY_RANK + LA + LV, LOW)


def dot(left, right, dims):
    return lax.dot_general(left, right, (dims, ((), ())), preferred_element_type=F32)


def halves(values):
    high = values.astype(BF16)
    return high, (values - high.astype(F32)).astype(BF16)


def dot3(left, right, dims):
    left_high, left_low = halves(left)
    right_high, right_low = halves(right)
    return (
        dot(left_high, right_high, dims)
        + dot(left_high, right_low, dims)
        + dot(left_low, right_high, dims)
    )


def dot1(left, right, dims):
    return dot(left.astype(BF16), right.astype(BF16), dims)


NN = ((1,), (0,))
NT = ((1,), (1,))
TN = ((0,), (0,))


def first_head(rows):
    return lax.broadcasted_iota(jnp.int32, (rows, PAIR), 1) < HS


def stack(folded):
    mine = first_head(folded.shape[0])
    zero = jnp.zeros_like(folded)
    return jnp.concatenate([jnp.where(mine, folded, zero), jnp.where(mine, zero, folded)], axis=0)


def unstack(full):
    return jnp.where(first_head(HS), full[:HS], full[HS:])


def head_sum(values):
    row = lax.broadcasted_iota(jnp.int32, (PAIR, PAIR), 0) // HS
    column = lax.broadcasted_iota(jnp.int32, (PAIR, PAIR), 1) // HS
    same = (row == column).astype(BF16)
    high, low = halves(values)
    return dot(high, same, NN) + dot(low, same, NN)


def running_sum(values, reverse):
    rows = values.shape[0]
    row = lax.broadcasted_iota(jnp.int32, (rows, rows), 0)
    column = lax.broadcasted_iota(jnp.int32, (rows, rows), 1)
    ones = ((column >= row) if reverse else (column <= row)).astype(BF16)
    high, low = halves(values)
    return dot(ones, high, NN) + dot(ones, low, NN)


def token_sum(values):
    return jnp.sum(values, axis=0, keepdims=True)


def key_terms(keyed, decay_up, rate_up, vec):
    place = vec[8:9] + decay_up
    log_decay = -jnp.exp(-0.5) * jax.nn.sigmoid(place)
    rate = jax.nn.sigmoid(vec[9:10] + rate_up)
    scaled = keyed * vec[11:12]
    inverse_norm = lax.rsqrt(head_sum(scaled * scaled) + UNIT_EPS)
    unit = scaled * inverse_norm
    key = keyed * (1.0 + (rate - 1.0) * vec[12:13])
    return place, log_decay, rate, inverse_norm, unit, key


def value_terms(valued, residual_up, first, vec):
    residual = jax.nn.sigmoid(vec[10:11] + residual_up)
    return residual, valued + (first - valued) * residual


def decayed(key, unit, rate, log_decay):
    total = running_sum(log_decay, False)
    grown = jnp.exp(total)
    shrunk = jnp.exp(-total)
    before = jnp.exp(total - log_decay)
    alpha = -before * unit
    beta = unit * rate * shrunk
    key_hat = key * shrunk
    return grown, shrunk, before, alpha, beta, key_hat


def solve_lower(lower):
    row = lax.broadcasted_iota(jnp.int32, (HS, PAIR), 0)
    column = lax.broadcasted_iota(jnp.int32, (HS, PAIR), 1) % HS
    eye = (row == column).astype(F32)
    small = (row // SMALL) == (column // SMALL)
    middle = (row // (2 * SMALL)) == (column // (2 * SMALL))
    zero = jnp.zeros_like(lower)
    power = jnp.where(small, lower, zero)
    result = eye + power
    power = dot3(power, stack(power), NN)
    yield
    for last in (False, False, True):
        held = stack(power)
        if last:
            result = result + dot3(result, held, NN)
        else:
            both = dot3(jnp.concatenate([result, power], axis=0), held, NN)
            result = result + both[:HS]
            power = both[HS:]
        yield
    for part in (
        jnp.where(jnp.logical_and(middle, jnp.logical_not(small)), lower, zero),
        jnp.where(middle, zero, lower),
    ):
        inner = dot3(result, stack(part), NN)
        yield
        result = result + dot3(inner, stack(result), NN)
        yield
    return result


def first_unit(
    at,
    keyed_ref, valued_ref, decay_ref, rate_ref, residual_ref, first_ref, vec_ref,
    strict_ref, start_ref, end_ref,
    pay_ref, solved_ref, lower_ref, start_alpha_ref, removed_ref, key_out_ref, value_out_ref,
):
    vec = vec_ref[...]
    strict, start, end = strict_ref[at], start_ref[at], end_ref[at]
    _, log_decay, rate, _, unit, key = key_terms(keyed_ref[at], decay_ref[at], rate_ref[at], vec)
    _, value = value_terms(valued_ref[at], residual_ref[at], first_ref[at].astype(F32), vec)
    key_out_ref[at] = key
    value_out_ref[at] = value
    yield
    grown, _, _, alpha, beta, key_hat = decayed(key, unit, rate, log_decay)
    last = grown[HS - 1 : HS]
    yield
    scores = dot3(alpha, jnp.concatenate([stack(beta), stack(key_hat)], axis=0), NT)
    yield
    lower_ak = scores[:, PAIR:] * strict
    lower_ref[at] = lower_ak
    applied = dot3(lower_ak, stack(value), NN)
    solved = yield from solve_lower(scores[:, :PAIR] * strict)
    solved_ref[at] = solved
    pair = dot3(solved, jnp.concatenate([stack(alpha * start), stack(applied)], axis=1), NN)
    yield
    start_alpha, removed = pair[:, :PAIR], pair[:, PAIR:]
    start_alpha_ref[at] = start_alpha
    removed_ref[at] = removed
    beta_end = beta * (last * end)
    key_end = key_hat * (last * end)
    change = unstack(dot3(start_alpha, beta_end, TN))
    inject = unstack(
        dot3(
            jnp.concatenate([removed, value], axis=0),
            jnp.concatenate([beta_end, key_end], axis=0),
            TN,
        )
    )
    yield
    row = lax.broadcasted_iota(jnp.int32, (HS, PAIR), 0)
    column = lax.broadcasted_iota(jnp.int32, (HS, PAIR), 1) % HS
    mine = first_head(HS)
    change = change + jnp.where(row == column, start[HS - 1 : HS] * last - 1.0, 0.0)
    turned = pltpu.roll(inject, HS, 1)
    pay_ref[at, 0] = jnp.where(mine, change, turned).astype(BF16)
    pay_ref[at, 1] = jnp.where(mine, turned, change).astype(BF16)


def reach_unit(
    at,
    read_ref, keyed_ref, decay_ref, rate_ref, value_ref, start_alpha_ref, removed_ref, vec_ref,
    inclusive_ref, start_ref,
    reach_b_ref, reach_k_ref, reads_ref, out_ref,
):
    vec = vec_ref[...]
    inclusive, start = inclusive_ref[at], start_ref[at]
    _, log_decay, rate, _, unit, key = key_terms(keyed_ref[at], decay_ref[at], rate_ref[at], vec)
    yield
    grown, _, _, _, beta, key_hat = decayed(key, unit, rate, log_decay)
    read_hat = read_ref[at] * grown
    yield
    scores = dot3(read_hat, jnp.concatenate([stack(beta), stack(key_hat)], axis=0), NT)
    yield
    reach_b = scores[:, :PAIR] * inclusive
    reach_k = scores[:, PAIR:] * inclusive
    reach_b_ref[at] = reach_b
    reach_k_ref[at] = reach_k
    pair = dot3(
        reach_b,
        jnp.concatenate([stack(start_alpha_ref[at]), stack(removed_ref[at])], axis=1),
        NN,
    )
    local_out = dot3(reach_k, stack(value_ref[at]), NN)
    yield
    reads_ref[at] = read_hat * start + pair[:, :PAIR]
    out_ref[at] = pair[:, PAIR:] + local_out


def chain(steps, form, change_of, item_of, write):
    stretches = [steps[i : i + len(steps) // 4] for i in range(0, len(steps), len(steps) // 4)]
    row = lax.broadcasted_iota(jnp.int32, (HS, HS), 0)
    eye = (row == lax.broadcasted_iota(jnp.int32, (HS, HS), 1)).astype(F32)
    none = jnp.zeros((HS, HS), F32)
    product_of = [eye for _ in stretches]
    total_of = [none for _ in stretches]
    before = {}
    for turn in range(len(stretches[0])):
        for at, stretch in enumerate(stretches):
            step = stretch[turn]
            before[step] = product_of[at], total_of[at]
            parts = jnp.concatenate([side_by_side(product_of[at]), side_by_side(total_of[at])], 0)
            change = change_of(step)
            gone = dot(parts, jnp.concatenate([change, change], axis=form[1][0]), form)
            product_of[at] = product_of[at] + gone[:HS]
            total_of[at] = total_of[at] + gone[HS:] + item_of(step)

    def through(state, product):
        high, low = halves(product)
        wide = side_by_side(state)
        twice = jnp.concatenate([high, high], axis=0)
        once = jnp.concatenate([low, jnp.zeros_like(low)], axis=0)
        return dot(wide, twice, NN) + dot(wide, once, NN)

    state = none
    for at, stretch in enumerate(stretches):
        for step in stretch:
            if at == 0:
                write(step, before[step][1])
            else:
                write(step, through(state, before[step][0]) + before[step][1])
        if at == 0:
            state = total_of[at]
        else:
            state = through(state, product_of[at]) + total_of[at]


def side_by_side(values):
    return jnp.concatenate(halves(values), axis=1)


def wide_rows(values):
    return jnp.concatenate([values[: HS // 2], values[HS // 2 :]], axis=1).astype(BF16)


def chain_kernel(odd_ref, pay_ref, out_ref):
    shift = odd_ref[0] * HS
    items = [pltpu.roll(pay_ref[at].astype(F32), shift, 1) for at in range(pay_ref.shape[0])]

    def write(step, state):
        out_ref[step] = wide_rows(state)

    chain(
        list(range(len(items))),
        NN,
        lambda step: items[step][:, :HS].astype(BF16),
        lambda step: items[step][:, HS:],
        write,
    )


def chain_back_kernel(odd_ref, pay_ref, grad_ref, out_ref):
    shift = odd_ref[0] * HS

    def change_of(step):
        return pltpu.roll(pay_ref[step].astype(F32), shift, 1)[:, :HS].astype(BF16)

    def item_of(step):
        item = grad_ref[step].astype(F32)
        return jnp.concatenate([item[:, :HS], item[:, HS:]], axis=0)

    def write(step, state):
        out_ref[step] = wide_rows(state)

    chain(list(reversed(range(pay_ref.shape[0]))), NT, change_of, item_of, write)


def joined(pay):
    first, second = pay[0].astype(F32), pay[1].astype(F32)
    return jnp.where(
        first_head(HS),
        jnp.concatenate([first, pltpu.roll(first, HS, 1)], axis=0),
        jnp.concatenate([pltpu.roll(second, HS, 1), second], axis=0),
    )


def parted(values):
    top, bottom = values[: HS // 2], values[HS // 2 :]
    mine = first_head(HS // 2)
    first = jnp.where(mine, top, pltpu.roll(bottom, HS, 1))
    second = jnp.where(mine, pltpu.roll(top, HS, 1), bottom)
    return first.astype(BF16), second.astype(BF16)


def output_unit(
    at,
    state_ref, reads_ref, local_ref, read_ref, key_ref, value_ref, gate_ref, vec_ref,
    out_ref, gated_ref,
):
    vec = vec_ref[...]
    state = joined(state_ref[at])
    state_out = local_ref[at] + dot1(reads_ref[at], stack(state), NT)
    yield
    out_ref[at] = state_out
    bonus = head_sum(read_ref[at] * key_ref[at] * vec[13:14])
    center = state_out - head_sum(state_out) * (1.0 / HS)
    yield
    inverse = lax.rsqrt(head_sum(center * center) * (1.0 / HS) + GROUP_EPS)
    yield
    mixed = center * inverse * vec[14:15] + vec[15:16] + bonus * value_ref[at]
    gated_ref[at] = (mixed * gate_ref[at]).astype(BF16)


def add_sums(at, ref, parts):
    place = lax.broadcasted_iota(jnp.int32, (8, PAIR), 0)
    sums = jnp.zeros((8, PAIR), F32)
    for row, part in enumerate(parts):
        sums = sums + jnp.where(place == row, token_sum(part), 0.0)
    if at == 0:
        ref[...] = sums
    else:
        ref[...] += sums


def head_back_unit(
    at,
    grad_ref, out_ref, reads_ref, read_ref, key_ref, value_ref, gate_ref, vec_ref,
    out_grad_ref, gate_grad_ref, read_grad_ref, key_grad_ref, value_grad_ref, pay_ref, vec_grad_ref,
):
    vec = vec_ref[...]
    read, key, value = read_ref[at], key_ref[at], value_ref[at]
    grad = grad_ref[at]
    grad_mixed = grad * gate_ref[at]
    grad_normed = grad_mixed * vec[14:15]
    state_out = out_ref[at]
    bonus = head_sum(read * key * vec[13:14])
    along = head_sum(grad_mixed * value)
    center = state_out - head_sum(state_out) * (1.0 / HS)
    grad_center = grad_normed - head_sum(grad_normed) * (1.0 / HS)
    yield
    inverse = lax.rsqrt(head_sum(center * center) * (1.0 / HS) + GROUP_EPS)
    yield
    normed = center * inverse
    shared = head_sum(grad_normed * normed) * (1.0 / HS)
    yield
    mixed = normed * vec[14:15] + vec[15:16] + bonus * value
    gate_grad_ref[at] = (grad * mixed).astype(BF16)
    value_grad_ref[at] = bonus * grad_mixed
    read_grad_ref[at] = along * key * vec[13:14]
    key_grad_ref[at] = along * read * vec[13:14]
    out_grad = inverse * (grad_center - normed * shared)
    out_grad_ref[at] = out_grad
    pay = dot1(out_grad, reads_ref[at], TN)
    add_sums(at, vec_grad_ref, (along * read * key, grad_mixed * normed, grad_mixed))
    yield
    pay_ref[at, 0], pay_ref[at, 1] = parted(unstack(pay))


def last_unit(
    at,
    read_ref, keyed_ref, valued_ref, decay_ref, rate_ref, residual_ref, first_ref, vec_ref,
    strict_ref, inclusive_ref, start_ref, end_ref,
    solved_ref, lower_ref, reach_b_ref, reach_k_ref, start_alpha_ref, removed_ref,
    state_ref, after_ref, out_grad_ref, read_grad_ref, key_grad_ref, value_grad_ref,
    d_read_ref, d_keyed_ref, d_valued_ref, d_decay_ref, d_rate_ref, d_residual_ref, d_first_ref,
    vec_grad_ref,
):
    vec = vec_ref[...]
    final_row = lax.broadcasted_iota(jnp.int32, (HS, PAIR), 0) == HS - 1
    strict, inclusive = strict_ref[at], inclusive_ref[at]
    start, end = start_ref[at], end_ref[at]
    read, keyed, valued = read_ref[at], keyed_ref[at], valued_ref[at]
    first = first_ref[at].astype(F32)
    out_grad = out_grad_ref[at]
    state = joined(state_ref[at])
    after = joined(after_ref[at])
    spot, log_decay, rate, inverse_norm, unit, key = key_terms(
        keyed, decay_ref[at], rate_ref[at], vec
    )
    residual, value = value_terms(valued, residual_ref[at], first, vec)
    solution_rows = dot1(start_alpha_ref[at], stack(state), NT) + removed_ref[at]
    reached = dot1(jnp.concatenate([reach_b_ref[at], reach_k_ref[at]], axis=1), out_grad, TN)
    yield
    grown, shrunk, before, alpha, beta, key_hat = decayed(key, unit, rate, log_decay)
    read_hat = read * grown
    last = grown[HS - 1 : HS]
    yield
    beta_end = beta * (last * end)
    key_end = key_hat * (last * end)
    carried = dot1(jnp.concatenate([beta_end, key_end], axis=0), stack(after), NT)
    ends = dot1(jnp.concatenate([solution_rows, value], axis=0), stack(after), NN)
    yield
    d_rows = unstack(reached[:PAIR]) + carried[:HS]
    d_value = unstack(reached[PAIR:]) + carried[HS:]
    back = unstack(dot1(solved_ref[at], d_rows, TN))
    yield
    d_value = d_value + unstack(dot1(lower_ref[at], back, TN)) + value_grad_ref[at]
    outer = jnp.concatenate([out_grad, back], axis=0)
    scores = dot1(outer, jnp.concatenate([stack(solution_rows), stack(value)], axis=0), NT)
    entries = dot1(outer, stack(state), NN)
    yield
    mask = jnp.concatenate([inclusive, strict], axis=0)
    scores = scores * jnp.concatenate([mask, mask], axis=1)
    d_beta_end, d_key_end = ends[:HS] * end, ends[HS:] * end
    lefts = dot3(scores, jnp.concatenate([stack(beta), stack(key_hat)], axis=0), NN)
    rights = dot3(scores, jnp.concatenate([read_hat, alpha], axis=0), TN)
    yield
    d_read_hat = entries[:HS] * start + lefts[:HS]
    d_alpha = entries[HS:] * start + lefts[HS:]
    d_beta = unstack(rights[:PAIR]) + d_beta_end * last
    d_key_hat = unstack(rights[PAIR:]) + d_key_end * last
    d_last = token_sum(beta * d_beta_end + key_hat * d_key_end) + start[
        HS - 1 : HS
    ] * token_sum(state * after)
    d_moved = d_beta * shrunk
    d_key = key_grad_ref[at] + d_key_hat * shrunk
    d_read_ref[at] = (read_grad_ref[at] + d_read_hat * grown).astype(BF16)
    along = d_alpha * alpha
    d_total = d_read_hat * read_hat - d_beta * beta - d_key_hat * key_hat + along
    d_total = d_total + jnp.where(final_row, d_last * last, 0.0)
    d_unit = rate * d_moved - before * d_alpha
    d_decay = running_sum(d_total, True) - along
    shared = head_sum(unit * d_unit)
    yield
    d_rate = unit * d_moved + d_key * keyed * vec[12:13]
    d_scaled = (d_unit - unit * shared) * inverse_norm
    d_keyed = d_key * (1.0 + (rate - 1.0) * vec[12:13]) + d_scaled * vec[11:12]
    d_first = d_value * residual
    d_residual = d_first * (first - valued) * (1.0 - residual)
    d_rate_up = d_rate * rate * (1.0 - rate)
    d_decay_up = d_decay * log_decay * jax.nn.sigmoid(-spot)
    d_keyed_ref[at] = d_keyed.astype(BF16)
    d_valued_ref[at] = (d_value * (1.0 - residual)).astype(BF16)
    d_decay_ref[at] = d_decay_up.astype(BF16)
    d_rate_ref[at] = d_rate_up.astype(BF16)
    d_residual_ref[at] = d_residual.astype(BF16)
    d_first_ref[at] = d_first
    add_sums(
        at,
        vec_grad_ref,
        (d_decay_up, d_rate_up, d_residual, d_scaled * keyed, d_key * keyed * (rate - 1.0)),
    )


def head_call(unit, inputs, outputs, flops, pairs):
    count = inputs[0][0].shape[0]
    wide = pairs * PAIR
    kinds = [kind for _, kind in inputs] + [kind for kind, _ in outputs]

    def spec(kind):
        if kind == "tokens":
            return pl.BlockSpec((count, HS, wide), lambda i: (0, 0, i))
        if kind == "rows":
            return pl.BlockSpec((24, wide), lambda i: (0, i))
        if kind == "sums":
            return pl.BlockSpec((8, wide), lambda i: (0, i))
        if kind == "pay":
            return pl.BlockSpec((count, 2 * pairs, HS, PAIR), lambda i: (0, i, 0, 0))
        if kind == "states":
            return pl.BlockSpec((count, 2 * pairs, HS // 2, PAIR), lambda i: (0, i, 0, 0))
        return pl.BlockSpec((count, HS, PAIR), lambda i: (0, 0, 0))

    shapes = {
        "tokens": (count, HS, EMBED_SIZE),
        "sums": (8, EMBED_SIZE),
        "pay": (count, H, HS, PAIR),
        "states": (count, H, HS // 2, PAIR),
    }

    def view(kind, ref, at):
        if kind == "tokens":
            return ref.at[:, :, pl.ds(at * PAIR, PAIR)]
        if kind in ("rows", "sums"):
            return ref.at[:, pl.ds(at * PAIR, PAIR)]
        if kind in ("pay", "states"):
            return ref.at[:, pl.ds(2 * at, 2)]
        return ref

    def kernel(*refs):
        running = []
        for pair in range(pairs):
            views = [view(kind, ref, pair) for kind, ref in zip(kinds, refs)]
            running += [unit(at, *views) for at in range(count)]
        done = object()
        while running:
            running = [run for run in running if next(run, done) is not done]

    bytes_moved = sum(4 * a.size for a, _ in inputs) + 4 * sum(
        count * HS * EMBED_SIZE for _ in outputs
    )
    return pl.pallas_call(
        kernel,
        grid=(HEAD_PAIRS // pairs,),
        in_specs=[spec(kind) for _, kind in inputs],
        out_specs=[spec(kind) for kind, _ in outputs],
        out_shape=[jax.ShapeDtypeStruct(shapes[kind], dtype) for kind, dtype in outputs],
        compiler_params=pltpu.CompilerParams(vmem_limit_bytes=HEAD_VMEM),
        cost_estimate=pl.CostEstimate(
            flops=flops, bytes_accessed=bytes_moved, transcendentals=count * HS * EMBED_SIZE * 6
        ),
    )(*[array for array, _ in inputs])


def chain_call(body, odd, *arrays):
    return pl.pallas_call(
        body,
        in_specs=[pl.BlockSpec(memory_space=pltpu.SMEM)]
        + [pl.BlockSpec(memory_space=pltpu.VMEM)] * len(arrays),
        out_specs=pl.BlockSpec(memory_space=pltpu.VMEM),
        out_shape=jax.ShapeDtypeStruct((arrays[0].shape[0], HS // 2, PAIR), BF16),
        compiler_params=pltpu.CompilerParams(vmem_limit_bytes=CHAIN_VMEM),
        cost_estimate=pl.CostEstimate(
            flops=32 * 4 * HS**3, bytes_accessed=3 * 1024 * 1024, transcendentals=0
        ),
    )(odd, *arrays)


def project_kernel(*refs):
    weight_ref, norm_ref, before_ref, keep_ref = refs[:4]
    mixes, (read_ref, keyed_ref, valued_ref), ups = refs[4:10], refs[10:13], refs[13:17]
    mids_ref, slopes_ref, vec_ref = refs[17:]
    turned = [
        weight_ref[128 * i : 128 * i + 128, UP_AT + LOW_WIDE - 128 :].astype(F32).T
        for i in range(8)
    ]
    vec = jnp.concatenate(turned, axis=1)[LOW - 256 : LOW - 256 + 24]
    vec_ref[...] = vec
    length = norm_ref.shape[1]
    for at in range(norm_ref.shape[0]):
        normed, delta = shifted(norm_ref, before_ref, keep_ref, vec, at)
        for index, mix in enumerate(mixes):
            mix[pl.ds(at * length, length)] = (normed + delta * vec[2 + index : 3 + index]).astype(
                BF16
            )
    mix_r, mix_w, mix_k, mix_v, mix_a, mix_g = mixes
    for index, (mix, target) in enumerate(
        ((mix_r, read_ref), (mix_k, keyed_ref), (mix_v, valued_ref))
    ):
        target[...] = dot(
            mix[...], weight_ref[:, index * EMBED_SIZE : (index + 1) * EMBED_SIZE], NN
        )
    down = weight_ref[:, DOWN_AT:UP_AT]
    up = weight_ref[:, UP_AT:]
    lane = lax.broadcasted_iota(jnp.int32, slopes_ref.shape, 1)
    insides = [jnp.logical_and(lane >= EDGES[i], lane < EDGES[i + 1]) for i in range(4)]
    low = jnp.zeros(slopes_ref.shape, F32)
    for inside, mix in zip(insides, (mix_w, mix_a, mix_v, mix_g)):
        low = jnp.where(inside, dot(mix[...], down, NN), low)
    decay, gate = jnp.tanh(low), jax.nn.sigmoid(low)
    mid = jnp.where(insides[0], decay, jnp.where(insides[3], gate, low)).astype(BF16)
    mids_ref[...] = mid
    slopes_ref[...] = jnp.where(
        insides[0], 1.0 - decay * decay, jnp.where(insides[3], gate * (1.0 - gate), 1.0)
    )
    for inside, target in zip(insides, ups):
        target[...] = dot(jnp.where(inside, mid, jnp.zeros_like(mid)), up, NT)


def project(weights, normed, before, keep):
    tokens = normed.shape[0] * normed.shape[1]
    whole = lambda shape: pl.BlockSpec(shape, lambda i: (0,) * len(shape))
    act = (tokens, EMBED_SIZE)
    low = (tokens, LOW_WIDE)
    outs = [(act, BF16)] * 6 + [(act, F32)] * 7 + [(low, BF16), (low, F32)]
    outs += [((24, EMBED_SIZE), F32)]
    inputs = (normed, before, keep)
    return pl.pallas_call(
        project_kernel,
        grid=(1,),
        in_specs=[whole((EMBED_SIZE, OUT_AT))] + [whole(part.shape) for part in inputs],
        out_specs=[whole(shape) for shape, _ in outs],
        out_shape=[jax.ShapeDtypeStruct(shape, kind) for shape, kind in outs],
        compiler_params=pltpu.CompilerParams(vmem_limit_bytes=GRAD_VMEM),
        cost_estimate=pl.CostEstimate(
            flops=2 * tokens * EMBED_SIZE * 5000, bytes_accessed=12_000_000, transcendentals=0
        ),
    )(weights, *inputs)


def turned_into(target, values):
    for at in range(values.shape[1] // 128):
        target(at, values[:, at * 128 : (at + 1) * 128].astype(F32).T.astype(BF16))


def channel_kernel(
    channel_ref, seed_ref, key_ref, val_ref, out_ref, grad_ref, squared_ref, act_ref
):
    seed = seed_ref[...]
    key = key_ref[...].reshape(EMBED_SIZE, -1)
    val = val_ref[...].reshape(-1, EMBED_SIZE)
    hidden = jnp.maximum(dot(channel_ref[...], key, NN), 0.0)
    squared = jnp.square(hidden).astype(BF16)
    d_squared = dot(seed, val, NT)
    act = (2.0 * hidden * d_squared).astype(BF16)
    act_ref[...] = act

    def into(at, part):
        squared_ref[at] = part.reshape(4, ROWS, part.shape[-1])

    turned_into(into, squared)
    out = dot(squared, val, NN)
    grad = dot(act, key, NT)

    @pl.when(pl.program_id(0) == 0)
    def _():
        out_ref[...] = out
        grad_ref[...] = grad

    @pl.when(pl.program_id(0) > 0)
    def _():
        out_ref[...] += out
        grad_ref[...] += grad


def channel_mix(channel, seed, full):
    tokens = channel.shape[0]
    block = 512
    whole = pl.BlockSpec((tokens, EMBED_SIZE), lambda j: (0, 0))
    return pl.pallas_call(
        channel_kernel,
        grid=(FF // block,),
        in_specs=[
            whole,
            whole,
            pl.BlockSpec((32, ROWS, block), lambda j: (0, 4 + j // 2, j % 2)),
            pl.BlockSpec((4, 4 * ROWS, EMBED_SIZE), lambda j: (j, 0, 0)),
        ],
        out_specs=[
            whole,
            whole,
            pl.BlockSpec((4, 4, ROWS, tokens), lambda j: (j, 0, 0, 0)),
            pl.BlockSpec((tokens, block), lambda j: (0, j)),
        ],
        out_shape=[
            jax.ShapeDtypeStruct((tokens, EMBED_SIZE), F32),
            jax.ShapeDtypeStruct((tokens, EMBED_SIZE), F32),
            jax.ShapeDtypeStruct((32, 4, ROWS, tokens), BF16),
            jax.ShapeDtypeStruct((tokens, FF), BF16),
        ],
        compiler_params=pltpu.CompilerParams(vmem_limit_bytes=GRAD_VMEM),
        cost_estimate=pl.CostEstimate(
            flops=8 * tokens * FF * EMBED_SIZE, bytes_accessed=20_000_000, transcendentals=0
        ),
    )(channel, seed, full, full)


def channel_grad_kernel(squared_ref, seed_ref, channel_ref, act_ref, out_ref, features):
    step = pl.program_id(0)

    def into_features(at, part):
        features[at] = part

    @pl.when(step == 4)
    def _():
        turned_into(into_features, channel_ref)

    def write(left_of, right):
        for group in range(8):
            out_ref[pl.ds(group * 4, 4)] = (
                dot(left_of(group), right, NN).astype(BF16).reshape(4, ROWS, EMBED_SIZE)
            )

    @pl.when(step < 4)
    def _():
        left_of = lambda group: squared_ref[pl.ds(group * 4, 4), 0].reshape(128, -1)
        write(left_of, seed_ref[...])

    @pl.when(step >= 4)
    def _():
        write(lambda group: features[group], act_ref[...])


def channel_grads(squared, seed, channel, act):
    tokens = seed.shape[0]
    whole = pl.BlockSpec((tokens, EMBED_SIZE), lambda j: (0, 0))
    return pl.pallas_call(
        channel_grad_kernel,
        grid=(8,),
        in_specs=[
            pl.BlockSpec((32, 1, ROWS, tokens), lambda j: (0, jnp.minimum(j, 3), 0, 0)),
            whole,
            whole,
            pl.BlockSpec((tokens, EMBED_SIZE), lambda j: (0, jnp.maximum(j - 4, 0))),
        ],
        out_specs=pl.BlockSpec((32, ROWS, EMBED_SIZE), lambda j: (0, j, 0)),
        out_shape=jax.ShapeDtypeStruct((32, 8 * ROWS, EMBED_SIZE), BF16),
        scratch_shapes=[pltpu.VMEM((8, 128, tokens), BF16)],
        compiler_params=pltpu.CompilerParams(vmem_limit_bytes=GRAD_VMEM),
        cost_estimate=pl.CostEstimate(
            flops=2 * tokens * 8 * EMBED_SIZE**2, bytes_accessed=20_000_000, transcendentals=0
        ),
    )(squared, seed, channel, act)


def shifted(norm_ref, before_ref, keep_ref, vec, at):
    length = norm_ref.shape[1]
    top = lax.broadcasted_iota(jnp.int32, (length, EMBED_SIZE), 0) == 0
    normed = norm_ref[at] * vec[0:1] + vec[1:2]
    before = before_ref[at] * vec[0:1] + vec[1:2]
    prior = jnp.where(top, before, pltpu.roll(normed, 1, 0)) * keep_ref[at][:, :1]
    return normed, prior - normed


def input_back_kernel(
    low_ref, d_read, d_keyed, d_valued, weight_ref, norm_ref, before_ref, keep_ref, vec_ref,
    grad_ref, edge_ref, sums_ref,
):
    vec = vec_ref[...]
    low, down = low_ref[...], weight_ref[:, DOWN_AT:]
    lane = lax.broadcasted_iota(jnp.int32, low.shape, 1)
    by_low = []
    for at in range(4):
        inside = jnp.logical_and(lane >= EDGES[at], lane < EDGES[at + 1])
        by_low.append(dot(jnp.where(inside, low, jnp.zeros_like(low)), down, NT))
    by_main = [
        dot(part[...], weight_ref[:, i * EMBED_SIZE : (i + 1) * EMBED_SIZE], NT)
        for i, part in enumerate((d_read, d_keyed, d_valued))
    ]
    grads = (by_main[0], by_low[0], by_main[1], by_main[2] + by_low[2], by_low[1], by_low[3])
    length = norm_ref.shape[1]
    bottom = lax.broadcasted_iota(jnp.int32, (length, EMBED_SIZE), 0) == length - 1
    place = lax.broadcasted_iota(jnp.int32, (8, EMBED_SIZE), 0)
    sums = jnp.zeros((8, EMBED_SIZE), F32)
    for at in range(norm_ref.shape[0]):
        rows = slice(at * length, (at + 1) * length)
        _, delta = shifted(norm_ref, before_ref, keep_ref, vec, at)
        total = sum(part[rows] for part in grads)
        mixed = sum(part[rows] * vec[2 + i : 3 + i] for i, part in enumerate(grads))
        kept = mixed * keep_ref[at][:, :1]
        later = jnp.where(bottom, 0.0, pltpu.roll(kept, length - 1, 0))
        grad_ref[at] = total - mixed + later
        edge_ref[at] = kept[:8]
        for i, part in enumerate(grads):
            sums = sums + jnp.where(place == i, token_sum(delta * part[rows]), 0.0)
    sums_ref[...] = sums


def input_back(low, d_time, weights, normed, before, keep, vec):
    count, length, width = normed.shape
    whole = lambda shape: pl.BlockSpec(shape, lambda i: (0,) * len(shape))
    inputs = (low, *d_time, weights, normed, before, keep, vec)
    outs = [(count, length, width), (count, 8, width), (8, width)]
    specs = [whole(part.shape) for part in inputs]
    specs[4] = whole((EMBED_SIZE, UP_AT))
    return pl.pallas_call(
        input_back_kernel,
        grid=(1,),
        in_specs=specs,
        out_specs=[whole(shape) for shape in outs],
        out_shape=[jax.ShapeDtypeStruct(shape, F32) for shape in outs],
        compiler_params=pltpu.CompilerParams(vmem_limit_bytes=GRAD_VMEM),
        cost_estimate=pl.CostEstimate(flops=0, bytes_accessed=1_000_000, transcendentals=0),
    )(*inputs)


def turn_kernel(*refs):
    for slot, ref in enumerate(refs[:-1]):

        def into(at, part):
            refs[-1][slot, at * 2 : at * 2 + 2] = part.reshape(2, 2, ROWS, part.shape[-1])

        turned_into(into, ref)


def turned_by_owner(parts):
    tokens = parts[0].shape[0]
    shape = (len(parts), 16, 2, ROWS, tokens)
    return pl.pallas_call(
        turn_kernel,
        grid=(1,),
        in_specs=[pl.BlockSpec(part.shape, lambda i: (0, 0)) for part in parts],
        out_specs=pl.BlockSpec(shape, lambda i: (0, 0, 0, 0, 0)),
        out_shape=jax.ShapeDtypeStruct(shape, BF16),
        compiler_params=pltpu.CompilerParams(vmem_limit_bytes=GRAD_VMEM),
        cost_estimate=pl.CostEstimate(flops=0, bytes_accessed=4_000_000, transcendentals=0),
    )(*parts)


def time_grad_kernel(
    core_ref, inputs_ref, d_read, d_keyed, d_valued, d_att, d_decay, d_rate, d_residual, d_gate,
    up_ref, slopes_ref, mids_ref, low_ref, mine_ref, theirs_ref, turned, first, second, sems,
):
    d_ups = (d_decay, d_rate, d_residual, d_gate)
    lane = lax.broadcasted_iota(jnp.int32, slopes_ref.shape, 1)
    insides = [jnp.logical_and(lane >= EDGES[i], lane < EDGES[i + 1]) for i in range(4)]
    up = up_ref[...]
    d_low = jnp.zeros(slopes_ref.shape, F32)
    for inside, d_up in zip(insides, d_ups):
        d_low = jnp.where(inside, dot(d_up[...], up, NN), d_low)
    d_low = (d_low * slopes_ref[...]).astype(BF16)
    low_ref[...] = d_low
    for slot, d_up in enumerate(d_ups):

        def into(at, part):
            turned[slot, at * 2 : at * 2 + 2] = part.reshape(2, 2, ROWS, part.shape[-1])

        turned_into(into, d_up)
    none = jnp.zeros(d_low.shape, BF16)

    def in_two(values):
        parts = [jnp.where(inside, values, none) for inside in insides]
        return (
            jnp.concatenate([part[:, :128] for part in parts[:2]], axis=0),
            jnp.concatenate([part[:, 128:] for part in parts[2:]], axis=0),
        )

    low_parts, mid_parts = in_two(d_low), in_two(mids_ref[...])
    block = 2 * ROWS

    def low_grads(parts, slots, get):
        pairs = [jnp.concatenate([get(i) for i in pair], axis=1) for pair in slots]
        return jnp.concatenate(
            [dot(pair, part, NN).astype(BF16) for pair, part in zip(pairs, parts)], axis=1
        )

    def copies(z, first_out, second_out):
        return (
            pltpu.make_async_copy(first.at[:, :, z], first_out.at[:, :, z], sems.at[0, z]),
            pltpu.make_async_copy(second.at[z], second_out.at[z], sems.at[1, z]),
        )

    def for_core(act):
        @pl.when(core_ref[0] == 0)
        def _():
            act(mine_ref, theirs_ref)

        @pl.when(core_ref[0] == 1)
        def _():
            act(theirs_ref, mine_ref)

    for z in range(4):
        chips = pl.ds(4 * z, 4)

        def left(slot):
            return inputs_ref[slot, chips].reshape(4 * block, -1)

        def left_up(slot):
            return turned[slot, chips].reshape(4 * block, -1)

        def owners(values):
            return values.reshape(4, 4, block // 4, values.shape[1])

        by_read = dot(left(0), d_read[...], NN).astype(BF16)
        by_key = dot(left(2), d_keyed[...], NN).astype(BF16)
        down = low_grads(low_parts, ((1, 4), (3, 5)), left)
        for x, quarter in [(x, quarter) for x in range(4) for quarter in range(4)]:
            part = slice(x * block + quarter * block // 4, x * block + (quarter + 1) * block // 4)
            first[quarter, x, z, :, :EMBED_SIZE] = by_read[part]
            first[quarter, x, z, :, EMBED_SIZE : 2 * EMBED_SIZE] = by_key[part]
            first[quarter, x, z, :, 2 * EMBED_SIZE :] = down[part]
        by_value = dot(left(3), d_valued[...], NN).astype(BF16)
        by_att = dot(left(6), d_att[...], NN).astype(BF16)
        second[z, :, :, :, :EMBED_SIZE] = owners(by_value)
        second[z, :, :, :, EMBED_SIZE : 2 * EMBED_SIZE] = owners(by_att)
        second[z, :, :, :, 2 * EMBED_SIZE :] = owners(
            low_grads(mid_parts, ((0, 1), (2, 3)), left_up)
        )

        def start(first_out, second_out):
            for copy in copies(z, first_out, second_out):
                copy.start()

        for_core(start)

    def finish(first_out, second_out):
        for z in range(4):
            for copy in copies(z, first_out, second_out):
                copy.wait()

    for_core(finish)


def time_grads(core, inputs, d_time, d_ups, weights, slopes, mids):
    tokens, wide = slopes.shape
    whole = lambda part: pl.BlockSpec(part.shape, lambda i: (0,) * part.ndim)
    low, half = (tokens, wide), (4, 4, 4, ROWS // 2, HALF)
    return pl.pallas_call(
        time_grad_kernel,
        grid=(1,),
        in_specs=[pl.BlockSpec(memory_space=pltpu.SMEM)]
        + [whole(part) for part in (inputs, *d_time, *d_ups)]
        + [pl.BlockSpec((EMBED_SIZE, wide), lambda i: (0, UP_AT // wide))]
        + [whole(slopes), whole(mids)],
        out_specs=[pl.BlockSpec(low, lambda i: (0, 0))] + [pl.BlockSpec(memory_space=pl.ANY)] * 2,
        out_shape=[jax.ShapeDtypeStruct(shape, BF16) for shape in (low, half, half)],
        scratch_shapes=[
            pltpu.VMEM((4, 16, 2, ROWS, tokens), BF16),
            pltpu.VMEM(half, BF16),
            pltpu.VMEM(half, BF16),
            pltpu.SemaphoreType.DMA((2, 4)),
        ],
        compiler_params=pltpu.CompilerParams(vmem_limit_bytes=GRAD_VMEM),
        cost_estimate=pl.CostEstimate(
            flops=2 * tokens * EMBED_SIZE * 4 * HALF, bytes_accessed=12_000_000, transcendentals=0
        ),
    )(core, inputs, *d_time, *d_ups, weights, slopes, mids)


def moved(values, first=0, second=0, third=0, core=0):
    pairs = []
    for at in range(128):
        y, z, x, mine = at // 32, at // 8 % 4, at // 2 % 4, at % 2
        x = (x + second) % 4
        if mine == 0:
            y, z = (y + first) % 4, (z + third) % 4
        else:
            z, y = (z + first) % 4, (y + third) % 4
        pairs.append((at, y * 32 + z * 8 + x * 2 + (mine + core) % 2))
    return lax.ppermute(values, ("rep", "shard"), pairs)


def over_two_axes(parts):
    groups = [
        [y * 32 + z * 8 + x * 2 for x in range(4) for z in range(4)] for y in range(4)
    ] + [
        [y * 32 + z * 8 + x * 2 + 1 for x in range(4) for y in range(4)] for z in range(4)
    ]
    parts = parts.reshape((16,) + parts.shape[2:])
    arrived = lax.all_to_all(parts, ("rep", "shard"), 0, 0, axis_index_groups=groups)
    return jnp.sum(arrived.astype(F32), axis=0)


def to_owners(quarter):
    arrived = []
    for step in range(4):
        pairs = []
        for at in range(128):
            y, chip, mine = at // 32, at // 2 % 16, at % 2
            to = (y % 2 * 2 + mine + step) % 4
            pairs.append((at, to * 32 + chip * 2 + y // 2))
        arrived.append(lax.ppermute(quarter, ("rep", "shard"), pairs))
    turn = jnp.stack([arrived[-step % 4] for step in range(4)] * 2)
    ordered = lax.dynamic_slice_in_dim(turn, -lax.axis_index("rep") % 4, 4)
    rows, columns = quarter.shape
    ordered = ordered.reshape(2, 2, rows, columns).swapaxes(1, 2)
    return ordered.reshape(2 * rows, 2 * columns).astype(F32)


def ring_place():
    place, y = lax.axis_index("shard"), lax.axis_index("rep")
    z, x, core = place // 8, place // 2 % 4, place % 2
    return jnp.where(core == 0, y, z), x, jnp.where(core == 0, z, y), core


def picked(values, at):
    return lax.dynamic_index_in_dim(values, at % values.shape[0], 0, keepdims=False)


def around_ring(chunk, send):
    total = chunk(0).astype(F32)
    for step in (1, 3, 2):
        total = total + send(chunk(step), step).astype(F32)
    return total


def to_group(part, by):
    return lax.ppermute(part, "rep", [(i, (i + by) % 4) for i in range(4)])


def quarter_over_groups(values):
    place = lax.axis_index("rep")
    quarters = values.astype(BF16).reshape(4, -1, values.shape[1])
    return around_ring(lambda k: picked(quarters, place + k), to_group).astype(BF16)


def from_quarters(mine):
    place = lax.axis_index("rep")
    parts = [mine] + [to_group(mine, step) for step in (3, 2, 1)]
    twice = jnp.concatenate(parts * 2, axis=0)
    return lax.dynamic_slice_in_dim(twice, (-place) % 4 * mine.shape[0], 4 * mine.shape[0]).astype(
        F32
    )


def passed_along(rows, by):
    size = lax.axis_size("shard")
    pairs = [(i, i + by) for i in range(size) if 0 <= i + by < size]
    return lax.ppermute(rows, "shard", pairs)


def product(left, right):
    return jnp.dot(left, right, preferred_element_type=F32)


def product_tn(left, right):
    return lax.dot_general(left, right, (((0,), (0,)), ((), ())), preferred_element_type=F32)


def product_nt(left, right):
    return lax.dot_general(left, right, (((1,), (1,)), ((), ())), preferred_element_type=F32)


def layer_norm(values, gain, bias):
    center = values - jnp.mean(values, axis=-1, keepdims=True)
    spread = jnp.mean(center * center, axis=-1, keepdims=True)
    return center * lax.rsqrt(spread + NORM_EPS) * gain + bias


def norm_piece(values, vec, row):
    return layer_norm(values, vec[row], vec[row + 1])


def mix_piece(values, before, vec, keep, first_row, count):
    prior = jnp.concatenate([before[:, None], values[:, :-1]], axis=1) * keep[:, :, None]
    delta = prior - values
    return tuple(values + delta * vec[first_row + index] for index in range(count))


def flat(values):
    return values.reshape(-1, values.shape[-1])


def gathered(shard):
    return lax.all_gather(shard, "shard", axis=0, tiled=True)


def scattered(full):
    return lax.psum_scatter(full, "shard", scatter_dimension=0, tiled=True)


def exchanged(pay):
    return lax.all_to_all(pay.reshape((-1,) + pay.shape[-2:]), "shard", 0, 0, tiled=False)


def local(
    layer_input,
    first_layer_values,
    segments,
    receptance_key_value_weight,
    time_output_weight,
    low_rank_down,
    low_rank_up,
    channel_key_weight,
    channel_value_weight,
    vectors,
    output_gradient,
):
    count, length, width = layer_input.shape
    rows = vectors.shape[1]
    spot_first, _, spot_third, spot_core = ring_place()
    filler = lambda used: jnp.zeros((rows, LOW_WIDE - used), BF16)
    weights = gathered(
        jnp.concatenate(
            [
                receptance_key_value_weight,
                low_rank_down,
                filler(LOW),
                low_rank_up.T,
                vectors.T,
                filler(LOW + vectors.shape[0]),
                time_output_weight,
            ],
            axis=1,
        )
    )
    rest = lax.all_gather(
        jnp.concatenate(
            [channel_value_weight] + jnp.split(channel_key_weight, 4, axis=1), axis=0
        ),
        "shard",
    )
    full_out = weights[:, OUT_AT:]

    edge = passed_along(segments[:, -1] + 1, 1) - 1
    keep = jnp.concatenate(
        [segments[:, :1] == edge[:, None], segments[:, 1:] == segments[:, :-1]], axis=1
    ).astype(F32)
    same = (segments[:, :, None] == segments[:, None, :]).astype(F32)
    later = lax.broadcasted_iota(jnp.int32, (length, length), 0)
    earlier = lax.broadcasted_iota(jnp.int32, (length, length), 1)
    strict = jnp.tile(same * (later > earlier).astype(F32), (1, 1, 2))
    inclusive = jnp.tile(same * (later >= earlier).astype(F32), (1, 1, 2))
    start = jnp.broadcast_to(
        (segments == edge[:, None]).astype(F32)[:, :, None], (count, length, PAIR)
    )
    end = jnp.broadcast_to(same[:, -1, :, None], (count, length, PAIR))
    masks = [(strict, "masks"), (inclusive, "masks"), (start, "masks"), (end, "masks")]
    odd = (lax.axis_index("shard") % 2).astype(jnp.int32).reshape(1)

    hidden = layer_input.astype(F32)
    raw_before = passed_along(layer_input[:, -1], 1).astype(F32)
    plain = lambda values: layer_norm(values, 1.0, 0.0)
    plain_hidden, plain_before = plain(hidden), plain(raw_before)[:, None]
    keep_wide = jnp.broadcast_to(keep[:, :, None], (count, length, PAIR))
    x_r, x_w, x_k, x_v, x_a, x_g, read, keyed, valued, *more = project(
        weights, plain_hidden, plain_before, keep_wide
    )
    decay_up, rate_up, residual_up, gate, mids, slopes, vec = more
    _, pull_norm1 = jax.vjp(partial(norm_piece, row=0), hidden, vec)
    shape = (count, length, width)
    read, keyed, valued, decay_up, rate_up, residual_up, gate = [
        part.reshape(shape) for part in (read, keyed, valued, decay_up, rate_up, residual_up, gate)
    ]
    vec_row, start_mask = (vec, "rows"), (start, "masks")
    pay, solved, lower, start_alpha, removed, key, value = head_call(
        first_unit,
        [
            (part, "tokens")
            for part in (keyed, valued, decay_up, rate_up, residual_up, first_layer_values)
        ]
        + [vec_row, (strict, "masks"), start_mask, (end, "masks")],
        [("pay", BF16)] + [("tokens", F32)] * 6,
        2_000_000_000,
        4,
    )
    chain_items = exchanged(pay)
    reach_b, reach_k, reads, local_out = head_call(
        reach_unit,
        [
            (part, "tokens")
            for part in (read, keyed, decay_up, rate_up, value, start_alpha, removed)
        ]
        + [vec_row, (inclusive, "masks"), start_mask],
        [("tokens", F32)] * 4,
        1_000_000_000,
        4,
    )
    states_shape = (count, H, HS // 2, PAIR)
    states = exchanged(chain_call(chain_kernel, odd, chain_items)).reshape(states_shape)
    tokens = [
        (part, "tokens")
        for part in (read, keyed, valued, decay_up, rate_up, residual_up, first_layer_values)
    ]
    gate_terms = [
        (read, "tokens"), (key, "tokens"), (value, "tokens"), (gate, "tokens"), (vec, "rows")
    ]
    state_out, gated = head_call(
        output_unit,
        [(states, "states"), (reads, "tokens"), (local_out, "tokens")] + gate_terms,
        [("tokens", F32), ("tokens", BF16)],
        300_000_000,
        4,
    )
    gated = flat(gated)
    mixed_h = hidden + product(gated, full_out).reshape(shape)

    normed2, pull_norm2 = jax.vjp(partial(norm_piece, row=16), mixed_h, vec)
    before2 = passed_along(normed2[:, -1], 1)
    channel, pull_mix2 = jax.vjp(
        partial(mix_piece, keep=keep, first_row=18, count=1), normed2, before2, vec
    )
    channel_low = flat(channel[0].astype(BF16))
    seed = flat(output_gradient)
    channel_out, grad_channel, squared, grad_act = channel_mix(
        channel_low, seed, rest
    )
    channel_part = channel_grads(squared, seed, channel_low, grad_act)
    grad_channel, channel_part = lax.optimization_barrier((grad_channel, channel_part))
    own_channel = scattered(channel_part)[0]
    turned = turned_by_owner((x_r, x_w, x_k, x_v, x_a, x_g, gated))
    hidden_out = (mixed_h + channel_out.reshape(shape)).astype(BF16)
    grad_channel = grad_channel.reshape(shape)
    grad_norm2, grad_before2, vec_grad_a = pull_mix2((grad_channel,))
    grad_norm2 = grad_norm2.at[:, -1].add(passed_along(grad_before2, -1))
    grad_mixed, vec_grad_b = pull_norm2(grad_norm2)
    grad_mixed = grad_mixed + output_gradient.astype(F32)
    grad_att = flat(grad_mixed.astype(BF16))
    grad_gated = product_nt(grad_att, full_out).reshape(shape)

    out_grad, gate_grad, read_grad, key_grad, value_grad, grad_pay, vec_sums_a = head_call(
        head_back_unit,
        [(grad_gated, "tokens"), (state_out, "tokens"), (reads, "tokens")] + gate_terms,
        [("tokens", F32), ("tokens", BF16)]
        + [("tokens", F32)] * 3
        + [("states", BF16), ("sums", F32)],
        300_000_000,
        4,
    )
    after = exchanged(
        chain_call(chain_back_kernel, odd, chain_items, exchanged(grad_pay))
    ).reshape(states_shape)
    d_read, d_keyed, d_valued, d_decay, d_rate, d_residual, first_grad, vec_sums_b = head_call(
        last_unit,
        tokens
        + [(vec, "rows")]
        + masks
        + [
            (part, "tokens")
            for part in (solved, lower, reach_b, reach_k, start_alpha, removed)
        ]
        + [(states, "states"), (after, "states")]
        + [(part, "tokens") for part in (out_grad, read_grad, key_grad, value_grad)],
        [("tokens", BF16)] * 6 + [("tokens", F32), ("sums", F32)],
        3_000_000_000,
        2,
    )
    d_time = [flat(d_read), flat(d_keyed), flat(d_valued)]
    d_ups = [flat(part) for part in (d_decay, d_rate, d_residual, gate_grad)]
    d_low, mine, theirs = time_grads(odd, turned, [*d_time, grad_att], d_ups, weights, slopes, mids)
    barrier = lax.optimization_barrier

    far_theirs = picked(theirs, spot_third + 2)
    far_arrived = moved(far_theirs, core=1)
    far_mine = picked(mine, spot_first + 2)
    far_arrived, far_mine, theirs = barrier((far_arrived, far_mine, theirs))
    far = (far_mine.astype(F32) + far_arrived.astype(F32)).astype(BF16)
    arrived = moved(theirs, core=1)
    from_behind = moved(far[:2], first=1)
    from_ahead = moved(far[2:], first=-1)
    far, d_low = barrier((far, d_low))
    grad_norm1, grad_edge, mix_sums = input_back(
        d_low, d_time, weights, plain_hidden, plain_before, keep_wide, vec
    )
    from_behind, from_ahead, arrived, grad_norm1, grad_edge = barrier(
        (from_behind, from_ahead, arrived, grad_norm1, grad_edge)
    )

    def chunk(k):
        own_part, other_part = [picked(part, spot_first + k) for part in (mine, arrived)]
        return own_part.astype(F32) + other_part.astype(F32)

    ahead, behind = chunk(1), chunk(3)
    ahead = jnp.concatenate([ahead[:2] + from_behind.astype(F32), ahead[2:]], axis=0)
    behind = jnp.concatenate([behind[:2], behind[2:] + from_ahead.astype(F32)], axis=0)
    from_behind = moved(ahead.astype(BF16), first=1)
    from_ahead = moved(behind.astype(BF16), first=-1)
    grad_norm1 = grad_norm1.at[:, -1].add(passed_along(grad_edge[:, 0], -1))
    grad_hidden, vec_grad_d = pull_norm1(grad_norm1)
    hidden_grad = grad_mixed + grad_hidden
    vec_grad = vec_grad_a + vec_grad_b + vec_grad_d
    vec_grad = vec_grad + jnp.concatenate(
        [
            jnp.zeros((2, width), F32),
            mix_sums[:6],
            vec_sums_b[:5],
            vec_sums_a[:3],
            jnp.zeros((vec.shape[0] - 16, width), F32),
        ],
        axis=0,
    )
    vec_turned = jnp.pad(vec_grad.T, ((0, 0), (0, LOW_WIDE - LOW - vec.shape[0]))).astype(BF16)
    vec_turned = vec_turned.reshape(4, 4, 4, ROWS // 2, LOW_WIDE - LOW)
    vec_turned = jnp.where(spot_core == 0, vec_turned.swapaxes(0, 2), vec_turned)
    along_first = lambda part, by: moved(part, first=by)
    vec_part = around_ring(lambda k: picked(vec_turned, spot_first + k), along_first)
    from_behind, from_ahead, vec_part = barrier((from_behind, from_ahead, vec_part))

    vec_at = HALF - LOW_WIDE + LOW
    summed = chunk(0) + from_behind.astype(F32) + from_ahead.astype(F32)
    summed = (summed + jnp.pad(vec_part, ((0, 0),) * 3 + ((vec_at, 0),))).astype(BF16)
    summed = over_two_axes(summed).astype(BF16)
    own_channel = quarter_over_groups(own_channel)
    summed, own_channel = barrier((summed, own_channel))
    own = to_owners(summed)
    own_channel = from_quarters(own_channel)
    own_key = jnp.concatenate([own_channel[128 + 32 * k : 160 + 32 * k] for k in range(4)], axis=1)
    down_at = 2 * EMBED_SIZE
    value_at, out_at, up_at = HALF, HALF + EMBED_SIZE, HALF + 2 * EMBED_SIZE
    own_vec = own[:, vec_at:HALF] + own[:, HALF + vec_at :]
    return (
        hidden_out,
        hidden_grad,
        first_grad,
        jnp.concatenate([own[:, :down_at], own[:, value_at:out_at]], axis=1),
        own[:, out_at:up_at],
        own[:, down_at : down_at + LOW],
        own[:, up_at : up_at + LOW].T,
        own_key,
        own_channel[:128],
        own_vec[:, : vectors.shape[0]].T,
    )


def solution(mesh):
    tokens = P("rep", "shard", None)
    rows = P("shard", None)
    columns = P(None, "shard")
    return jax.shard_map(
        local,
        mesh=mesh,
        in_specs=(
            tokens, tokens, P("rep", "shard"), rows, rows, rows, columns, rows, rows, columns, tokens
        ),
        out_specs=(tokens, tokens, tokens, rows, rows, rows, columns, rows, rows, columns),
        check_vma=False,
    )
```
